128 devices in a mesh: src: 4 (over x_lo, core), slab: 32 (over x_hi, z, y).
Axes of the slice: x: 4 (x_hi: 2, x_lo: 2; x = x_hi * 2 + x_lo), y: 4, z: 4, core: 2. Of those that a mesh axis runs over, the one named last changes fastest.
Arguments:
- log_cond: float32 [256, 256, 256], P('slab'), may hold values from -1.5 to 1.5
- perturb: float32 [256, 256, 256], P('slab'), may hold values from -6 to 6
- potentials: float32 [4, 256, 256, 256], P('src', 'slab'), may hold values from -6 to 6
- rec_depth: int32 [2, 4096], replicated, may hold values from 0 to 255
- rec_plan: int32 [2, 4096], replicated, may hold values from 0 to 65535
Outputs:
- hess_vec: float32 [256, 256, 256], P('slab')
The draws below stay inside these ranges and needn't reach their ends.
All inputs are finite; a program needn't handle non-finite values.
Results may differ from the reference program's by a relative error of at most 0.0003.
Values sent between devices are 32-bit elements; how exact they have to be, the bound alone decides.
A program may use at most 256 MiB of HBM per device.

```python
import jax
import jax.numpy as jnp
from jax import lax

NXY = 256
NPAIR = 4096
ITERS = 4
SOURCES = 4
NZ = 256


def plant(values, stream_key, least, top_value):
    dims = values.shape
    spot = [jax.random.randint(jax.random.fold_in(stream_key, axis), (), 0, dims[axis]) for axis in range(len(dims))]
    values = values.at[tuple(spot)].set(least)
    longest = dims.index(max(dims))
    spot[longest] = (spot[longest] + 1) % dims[longest]
    return values.at[tuple(spot)].set(top_value)


def steps_of(rng, dims, split, least, largest):
    factor_of = 1.0
    for axis_at, blocks in split:
        draws = jax.random.uniform(jax.random.fold_in(jax.random.fold_in(rng, 6), axis_at), (blocks,), jnp.float32, least / len(split), largest / len(split))
        factor_of = factor_of * jnp.repeat(jnp.exp(draws), dims[axis_at] // blocks).reshape((-1,) + (1,) * (len(dims) - 1 - axis_at))
    return factor_of


def scatter_about(key, shape, spread, most, pieces=(), kind=jnp.bfloat16):
    entries = jax.random.normal(key, shape, jnp.float32) * spread
    if len(pieces) > 0:
        entries = steps_of(key, shape, pieces, -0.22, 0.18) * entries
    return jnp.clip(entries, min=-most, max=most).astype(kind)


def setup_inputs(seed: int = 0) -> dict:
    keys = jax.random.split(jax.random.key(seed), 6)
    log_cond = jnp.clip(jax.random.uniform(keys[0], (NZ, NXY, NXY), jnp.float32, -1.5, 1.5) * steps_of(keys[0], (NZ, NXY, NXY), ((0, 32),), -0.4, 0.0), -1.5, 1.5)
    perturb = scatter_about(keys[1], (NZ, NXY, NXY), 1.0, 6.0, ((0, 32),), jnp.float32)
    potentials = scatter_about(keys[2], (SOURCES, NZ, NXY, NXY), 1.0, 6.0, ((0, 4), (1, 32)), jnp.float32)
    rec_depth = plant(jax.random.randint(keys[3], (2, NPAIR), 0, NZ), jax.random.fold_in(keys[3], 1), 0, NZ - 1).astype(jnp.int32)
    rec_plan = plant(jax.random.randint(keys[4], (2, NPAIR), 0, NXY * NXY), jax.random.fold_in(keys[4], 1), 0, (NXY * NXY) - 1).astype(jnp.int32)
    return dict(log_cond=log_cond, perturb=perturb, potentials=potentials, rec_depth=rec_depth, rec_plan=rec_plan)


def shifted(field, axis, step):
    size = field.shape[axis]
    zero = jnp.zeros_like(lax.slice_in_dim(field, 0, 1, axis=axis))
    if step > 0:
        return jnp.concatenate([lax.slice_in_dim(field, 1, size, axis=axis), zero], axis=axis)
    return jnp.concatenate([zero, lax.slice_in_dim(field, 0, size - 1, axis=axis)], axis=axis)


def coefficients(padded):
    core = padded[..., 1:-1, :, :]
    faces = 0.5 * (padded[..., 1:, :, :] + padded[..., :-1, :, :])
    return (faces[..., :-1, :, :], faces[..., 1:, :, :],
            0.5 * (core + shifted(core, -2, -1)), 0.5 * (core + shifted(core, -2, 1)),
            0.5 * (core + shifted(core, -1, -1)), 0.5 * (core + shifted(core, -1, 1)))


def apply_faces(coef, padded):
    core = padded[..., 1:-1, :, :]
    total = coef[0] * (core - padded[..., :-2, :, :]) + coef[1] * (core - padded[..., 2:, :, :])
    total = total + coef[2] * (core - shifted(core, -2, -1)) + coef[3] * (core - shifted(core, -2, 1))
    total = total + coef[4] * (core - shifted(core, -1, -1)) + coef[5] * (core - shifted(core, -1, 1))
    return total


def pair_sum(upad, lpad):
    upot = upad[..., 1:-1, :, :]
    ladj = lpad[..., 1:-1, :, :]
    total = (upot - upad[..., :-2, :, :]) * (ladj - lpad[..., :-2, :, :])
    total = total + (upot - upad[..., 2:, :, :]) * (ladj - lpad[..., 2:, :, :])
    for axis in (-2, -1):
        for step in (-1, 1):
            total = total + (upot - shifted(upot, axis, step)) * (ladj - shifted(ladj, axis, step))
    return 0.5 * total


def zpad(field):
    return jnp.pad(field, ((1, 1), (0, 0), (0, 0)))


def reference(log_cond, perturb, potentials, rec_depth, rec_plan):
    sigma = jnp.exp(log_cond)
    weighted = sigma * perturb
    coef = coefficients(zpad(sigma))
    wcoef = coefficients(zpad(weighted))
    plane = NXY * NXY
    plus = (rec_depth[0] * plane + rec_plan[0]).astype(jnp.int32)
    minus = (rec_depth[1] * plane + rec_plan[1]).astype(jnp.int32)

    def solve(rhs):
        solution = jnp.zeros_like(rhs)
        resid = rhs
        direction = rhs
        norm_now = jnp.sum(resid * resid)
        for step in range(ITERS):
            image = apply_faces(coef, zpad(direction))
            alpha = norm_now / jnp.sum(direction * image)
            solution = solution + alpha * direction
            resid = resid - alpha * image
            norm_next = jnp.sum(resid * resid)
            direction = resid + (norm_next / norm_now) * direction
            norm_now = norm_next
        return solution

    def one_source(total, upot):
        upad = zpad(upot)
        tangent = solve(-apply_faces(wcoef, upad))
        flat = tangent.reshape(-1)
        data = flat[plus] - flat[minus]
        back = jnp.zeros_like(flat).at[plus].add(data).at[minus].add(-data).reshape(tangent.shape)
        adjoint = solve(back)
        return total + pair_sum(upad, zpad(adjoint)), None

    total, unused = lax.scan(one_source, jnp.zeros_like(sigma), potentials)
    return -sigma * total
```

```python
import functools

import jax
import jax.numpy as jnp
from jax import lax
from jax.experimental import pallas as pl
from jax.experimental.pallas import tpu as pltpu
from jax.sharding import PartitionSpec as P

MESH = pl.DeviceIdType.MESH
F32 = jnp.float32
VMEM = pltpu.VMEM
SMEM = pltpu.SMEM
DMA = pltpu.SemaphoreType.DMA
PAD = 8
WIDE = 4
ROWS = 64
THETA = (6.0, 2.0, 10.0)


def lane_iota(shape):
    return lax.broadcasted_iota(jnp.int32, shape, len(shape) - 1)


def fold(value):
    rows, cols = value.shape
    return jnp.sum(value.reshape(rows // 8, 8, cols), axis=0)


def next_lane(value):
    return pltpu.roll(value, value.shape[1] - 1, 1)


def prev_lane(value):
    return pltpu.roll(value, 1, 1)


def chunks(nx):
    rows = min(ROWS, nx)
    return [(r, rows) for r in range(0, nx, rows)]


def make_coefs(sig, dg, hx, hy, hz, count, first, last, nx):
    cols = sig.shape[-1]

    def body(q, carry):
        low_in = jnp.logical_and(q - 1 >= first, q <= last).astype(F32)
        for r, rows in chunks(nx):
            here = sig[q + 1, pl.ds(PAD + r, rows), :]
            up = sig[q + 1, pl.ds(PAD + r + 1, rows), :]
            down = sig[q + 1, pl.ds(PAD + r - 1, rows), :]
            low = sig[q, pl.ds(PAD + r, rows), :]
            high = sig[q + 2, pl.ds(PAD + r, rows), :]
            lane = lane_iota(here.shape)
            right = jnp.where(lane == cols - 1, 0.0, next_lane(here))
            left = jnp.where(lane == 0, 0.0, prev_lane(here))
            near = 0.5 * (here + right)
            hx[q, pl.ds(r, rows), :] = jnp.where(lane == cols - 1, 0.0, near)
            hy[q, pl.ds(PAD + r, rows), :] = 0.5 * (here + up)
            hz[q, pl.ds(r, rows), :] = (0.5 * low_in) * (here + low)
            total = ((up + down) + (left + right)) + (low + high)
            dg[q, pl.ds(r, rows), :] = 3.0 * here + 0.5 * total
        return carry

    lax.fori_loop(0, count, body, 0)


def make_top(sig, hz, count, first, last, nx):
    inside = jnp.logical_and(count - 1 >= first, count <= last).astype(F32)
    for r, rows in chunks(nx):
        here = sig[count + 1, pl.ds(PAD + r, rows), :]
        low = sig[count, pl.ds(PAD + r, rows), :]
        hz[count, pl.ds(r, rows), :] = (0.5 * inside) * (here + low)


def operator(v, p, dg, hx, hy, hz, q, r, rows):
    here = v[p, pl.ds(PAD + r, rows), :]
    wx = hx[q, pl.ds(r, rows), :]
    acc = dg[q, pl.ds(r, rows), :] * here
    acc = acc - wx * next_lane(here)
    acc = acc - prev_lane(wx * here)
    acc = acc - hy[q, pl.ds(PAD + r, rows), :] * v[p, pl.ds(PAD + r + 1, rows), :]
    acc = acc - hy[q, pl.ds(PAD + r - 1, rows), :] * v[p, pl.ds(PAD + r - 1, rows), :]
    acc = acc - hz[q, pl.ds(r, rows), :] * v[p - 1, pl.ds(PAD + r, rows), :]
    acc = acc - hz[q + 1, pl.ds(r, rows), :] * v[p + 1, pl.ds(PAD + r, rows), :]
    return here, acc


def zero_pads(ref, nx):
    zero = jnp.zeros((ref.shape[0], PAD, ref.shape[2]), F32)
    ref[:, pl.ds(0, PAD), :] = zero
    ref[:, pl.ds(PAD + nx, PAD), :] = zero


def splat(row, index):
    return jnp.sum(jnp.where(lane_iota(row.shape) == index, row, 0.0), axis=1, keepdims=True)


def solve_small(row, scale, thetas):
    gram = {}
    n = 0
    for i in range(4):
        for j in range(i + 1):
            gram[i, j] = gram[j, i] = splat(row, n)
            n += 1
    last = splat(row, n)
    mat = {}
    for i in range(4):
        for j in range(i + 1):
            if j == 3:
                mat[i, j] = last
            else:
                mat[i, j] = scale * gram[i, j + 1] + thetas[j] * gram[i, j]
    low, inv = {}, {}
    for j in range(4):
        pivot = mat[j, j]
        for k in range(j):
            pivot = pivot - low[j, k] * low[j, k] * mat["d", k]
        mat["d", j] = pivot
        good = pivot > 1e-7 * mat[j, j]
        inv[j] = jnp.where(good, 1.0 / jnp.where(good, pivot, 1.0), 0.0)
        for i in range(j + 1, 4):
            value = mat[i, j]
            for k in range(j):
                value = value - low[i, k] * low[j, k] * mat["d", k]
            low[i, j] = value * inv[j]
    y = []
    for i in range(4):
        value = gram[i, 0]
        for k in range(i):
            value = value - low[i, k] * y[k]
        y.append(value)
    c = [None] * 4
    for i in reversed(range(4)):
        value = y[i] * inv[i]
        for k in range(i + 1, 4):
            value = value - low[k, i] * c[k]
        c[i] = value
    return c


def pack_row(accs):
    lane = lane_iota((1, 128))
    row = jnp.zeros((1, 128), F32)
    for n, acc in enumerate(accs):
        total = jnp.sum(jnp.sum(acc, axis=0, keepdims=True), axis=1, keepdims=True)
        row = row + jnp.where(lane == n, total, 0.0)
    return row


def send_all(buf, send_sem, recv_sem, src, me, slabs):
    for d in range(1, slabs):
        pltpu.make_async_remote_copy(
            src_ref=buf.at[0],
            dst_ref=buf.at[d],
            send_sem=send_sem,
            recv_sem=recv_sem,
            device_id=(src, lax.rem(me + d, slabs)),
            device_id_type=MESH,
        ).start()


def wait_all(buf, sem, slabs):
    rest = buf.at[pl.ds(1, slabs - 1)]
    pltpu.make_async_copy(rest, rest, sem).wait()


def greet(src, me, slabs, others):
    barrier = pltpu.get_barrier_semaphore()
    for d in range(1, slabs):
        pl.semaphore_signal(
            barrier, inc=1, device_id=(src, lax.rem(me + d, slabs)), device_id_type=MESH
        )
    for other in others:
        pl.semaphore_signal(barrier, inc=1, device_id=(other, me), device_id_type=MESH)
    pl.semaphore_wait(barrier, slabs - 1 + len(others))


def flip(src, bit):
    return src + bit - 2 * bit * (lax.rem(src // bit, 2))


def remote(src_ref, dst_ref, send_sem, recv_sem, target):
    return pltpu.make_async_remote_copy(
        src_ref=src_ref,
        dst_ref=dst_ref,
        send_sem=send_sem,
        recv_sem=recv_sem,
        device_id=target,
        device_id_type=MESH,
    )


def first_kernel(
    slabs, lc, pt, u, tan, halo_out, uh_out, mean_out,
    sig, wgt, uw, dg, hx, hy, hz, v0, v1, v2, v3, lch, pth, far, stat, mom,
    s_first, r_first, s_core, r_core, s_far, r_far, s_x, r_x, s_c2, r_c2, s_v, r_v, s_all, r_all,
):
    src = lax.axis_index("src")
    me = lax.axis_index("slab")
    depth, nx, cols = lc.shape
    has_low = me > 0
    has_high = me < slabs - 1
    core = lax.rem(src, 2)
    mate, across = flip(src, 1), flip(src, 2)
    greet(src, me, slabs, (mate, across))

    def both(send):
        @pl.when(has_high)
        def _():
            send(0, me + 1)

        @pl.when(has_low)
        def _():
            send(1, me - 1)

    def arrives(side):
        return has_low if side == 0 else has_high

    def near(side):
        return depth - 1 if side == 0 else 0

    def copy_u(side, to):
        return remote(u.at[near(side)], uh_out.at[side], s_first.at[0, side], r_first.at[0, side], (src, to))

    def copy_c(ref, dst, side, to):
        return remote(ref.at[near(side)], dst.at[side], s_first.at[1, side], r_first.at[1, side], (src, to))

    def begin(side, to):
        copy_u(side, to).start()

        @pl.when(core == 0)
        def _():
            copy_c(lc, lch, side, to).start()

        @pl.when(core == 1)
        def _():
            copy_c(pt, pth, side, to).start()

    both(begin)

    zero_pads(sig, nx)
    zero_pads(wgt, nx)
    zero_pads(uw, nx)
    zero_pads(hy, nx)
    for ref in (v0, v1, v2, v3):
        zero_pads(ref, nx)

    def own(q, acc):
        for r, rows in chunks(nx):
            value = jnp.exp(lc[q, pl.ds(r, rows), :])
            sig[q + 1, pl.ds(PAD + r, rows), :] = value
            wgt[q + 1, pl.ds(PAD + r, rows), :] = value * pt[q, pl.ds(r, rows), :]
            uw[q + 1, pl.ds(PAD + r, rows), :] = u[q, pl.ds(r, rows), :]
            acc = acc + fold(value)
        return acc

    acc = lax.fori_loop(0, depth, own, jnp.zeros((8, cols), F32))
    stat[0] = jnp.broadcast_to(pack_row([acc]), (8, 128))
    send_all(stat, s_all.at[0], r_all.at[0], src, me, slabs)

    far_plane = {0: depth - 2 - src, 1: 1 + src}

    def copy_far(side, to):
        return remote(lc.at[far_plane[side]], far.at[side, 0], s_far.at[side], r_far.at[side], (src, to))

    both(lambda side, to: copy_far(side, to).start())

    for side in (0, 1):
        got = arrives(side)

        @pl.when(got)
        def _():
            copy_u(side, me).wait_recv()

            @pl.when(core == 0)
            def _():
                copy_c(lc, lch, side, me).wait_recv()
                remote(lch.at[side], lch.at[side], s_core.at[side], r_core.at[side], (mate, me)).start()

            @pl.when(core == 1)
            def _():
                copy_c(pt, pth, side, me).wait_recv()
                remote(pth.at[side], pth.at[side], s_core.at[side], r_core.at[side], (mate, me)).start()

    for side in (0, 1):
        plane = 0 if side == 0 else depth + 1

        @pl.when(arrives(side))
        def _():
            @pl.when(core == 0)
            def _():
                remote(lch.at[side], pth.at[side], s_core.at[side], r_core.at[side], (mate, me)).wait_recv()

            @pl.when(core == 1)
            def _():
                remote(pth.at[side], lch.at[side], s_core.at[side], r_core.at[side], (mate, me)).wait_recv()

            for r, rows in chunks(nx):
                value = jnp.exp(lch[side, pl.ds(r, rows), :])
                sig[plane, pl.ds(PAD + r, rows), :] = value
                wgt[plane, pl.ds(PAD + r, rows), :] = value * pth[side, pl.ds(r, rows), :]
                uw[plane, pl.ds(PAD + r, rows), :] = uh_out[side]  [r : r + rows, :]

        @pl.when(jnp.logical_not(arrives(side)))
        def _():
            for ref in (sig, wgt, uw):
                ref[plane, pl.ds(PAD, nx), :] = jnp.zeros((nx, cols), F32)
            uh_out[side] = jnp.zeros((nx, cols), F32)

    def rhs_plane(q, carry):
        for r, rows in chunks(nx):
            c = wgt[q + 1, pl.ds(PAD + r, rows), :]
            f = uw[q + 1, pl.ds(PAD + r, rows), :]
            lane = lane_iota(c.shape)
            cr = jnp.where(lane == cols - 1, 0.0, next_lane(c))
            fr = jnp.where(lane == cols - 1, 0.0, next_lane(f))
            flow = (c + cr) * (f - fr)
            total = flow + jnp.where(lane == 0, c * f, -prev_lane(flow))
            for dq, dr in ((0, 1), (0, -1), (1, 0), (-1, 0)):
                cj = wgt[q + 1 + dq, pl.ds(PAD + r + dr, rows), :]
                fj = uw[q + 1 + dq, pl.ds(PAD + r + dr, rows), :]
                total = total + (c + cj) * (f - fj)
            v0[q + 1, pl.ds(PAD + r, rows), :] = -0.5 * total
        return carry

    fields = (v0, v1, v2, v3)

    def copy_v(k, side, to):
        plane = depth if side == 0 else 1
        halo = 0 if side == 0 else depth + 1
        ref = fields[k]
        return remote(
            ref.at[plane, pl.ds(PAD, nx)], ref.at[halo, pl.ds(PAD, nx)],
            s_v.at[k, side], r_v.at[k, side], (src, to),
        )

    def halo_ready(k):
        for side in (0, 1):
            @pl.when(arrives(side))
            def _():
                copy_v(k, side, me).wait_recv()

    for ref in fields:
        @pl.when(jnp.logical_not(has_low))
        def _():
            ref[0, pl.ds(PAD, nx), :] = jnp.zeros((nx, cols), F32)

        @pl.when(jnp.logical_not(has_high))
        def _():
            ref[depth + 1, pl.ds(PAD, nx), :] = jnp.zeros((nx, cols), F32)

    def edges_first(plane, carry):
        carry = lax.fori_loop(0, 2, lambda i, c: plane(i * (depth - 1), c), carry)
        return carry

    def inner(plane, carry):
        return lax.fori_loop(1, depth - 1, plane, carry)

    edges_first(rhs_plane, 0)
    both(lambda side, to: copy_v(0, side, to).start())
    inner(rhs_plane, 0)
    first, last = -me * depth, (slabs - me) * depth - 1
    make_coefs(sig, dg, hx, hy, hz, depth, first, last, nx)
    make_top(sig, hz, depth, first, last, nx)

    wait_all(stat, r_all.at[0], slabs)
    mean = jnp.sum(stat[...], axis=0)
    mean = jnp.sum(jnp.where(lane_iota((8, 128)) == 0, mean, 0.0), axis=1, keepdims=True)[0:1]
    mean = mean * (1.0 / (slabs * depth * nx * cols))
    mean_out[...] = jnp.broadcast_to(mean, (8, 128))
    scale = 6.0 * mean
    inv = 1.0 / scale

    zero = jnp.zeros((8, cols), F32)
    dots = []
    for k in range(3):
        shift = THETA[k] * mean * inv

        def step(q, accs, k=k, shift=shift):
            accs = list(accs)
            for r, rows in chunks(nx):
                here, image = operator(fields[k], q + 1, dg, hx, hy, hz, q, r, rows)
                new = inv * image - shift * here
                fields[k + 1][q + 1, pl.ds(PAD + r, rows), :] = new
                if k == 0:
                    accs[0] = accs[0] + fold(here * here)
                for i in range(k + 1):
                    other = here if i == k else fields[i][q + 1, pl.ds(PAD + r, rows), :]
                    accs[i + (k == 0)] = accs[i + (k == 0)] + fold(new * other)
                accs[-1] = accs[-1] + fold(new * new)
            return tuple(accs)

        accs = (zero,) * (3 if k == 0 else k + 2)
        accs = inner(step, accs)
        halo_ready(k)
        accs = edges_first(step, accs)
        both(lambda side, to: copy_v(k + 1, side, to).start())
        dots.extend(accs)

    def energy(q, acc):
        for r, rows in chunks(nx):
            here, image = operator(v3, q + 1, dg, hx, hy, hz, q, r, rows)
            acc = acc + fold(here * image)
        return acc

    acc = inner(energy, zero)

    for side in (0, 1):
        @pl.when(arrives(side))
        def _():
            copy_far(side, me).wait_recv()
            remote(far.at[side, 0], far.at[side, 1], s_x.at[side], r_x.at[side], (across, me)).start()

    halo_ready(3)
    dots.append(edges_first(energy, acc))
    mom[0] = jnp.broadcast_to(pack_row(dots), (8, 128))
    send_all(mom, s_all.at[1], r_all.at[1], src, me, slabs)

    for side in (0, 1):
        @pl.when(arrives(side))
        def _():
            remote(far.at[side, 0], far.at[side, 1], s_x.at[side], r_x.at[side], (across, me)).wait_recv()
            remote(
                far.at[side, pl.ds(0, 2)], far.at[side, pl.ds(2, 2)],
                s_c2.at[side], r_c2.at[side], (mate, me),
            ).start()

    wait_all(mom, r_all.at[1], slabs)
    row = jnp.sum(mom[...], axis=0)[0:1]
    c = solve_small(row, scale, [t * mean for t in THETA])

    def combine(q, carry):
        for r, rows in chunks(nx):
            value = c[0] * v0[q + 1, pl.ds(PAD + r, rows), :]
            for i in (1, 2, 3):
                value = value + c[i] * fields[i][q + 1, pl.ds(PAD + r, rows), :]
            tan[q, pl.ds(r, rows), :] = value
        return carry

    lax.fori_loop(0, depth, combine, 0)

    for side in (0, 1):
        @pl.when(arrives(side))
        def _():
            remote(
                far.at[side, pl.ds(0, 2)], far.at[side, pl.ds(2, 2)],
                s_c2.at[side], r_c2.at[side], (mate, me),
            ).wait_recv()
            halo_out[side, 0] = lch[side]
            owners = (src, across, mate, flip(mate, 2))
            for n in range(4):
                halo_out[side, 1 + owners[n]] = far[side, n]

        @pl.when(jnp.logical_not(arrives(side)))
        def _():
            for n in range(5):
                halo_out[side, n] = jnp.zeros((nx, cols), F32)

    def sent(side, to):
        copy_u(side, to).wait_send()
        copy_c(lc, lch, side, to).wait_send()
        copy_far(side, to).wait_send()
        for k in range(4):
            copy_v(k, side, to).wait_send()

    both(sent)
    for side in (0, 1):
        @pl.when(arrives(side))
        def _():
            remote(lch.at[side], lch.at[side], s_core.at[side], r_core.at[side], (mate, me)).wait_send()
            remote(far.at[side, 0], far.at[side, 1], s_x.at[side], r_x.at[side], (across, me)).wait_send()
            remote(
                far.at[side, pl.ds(0, 2)], far.at[side, pl.ds(2, 2)],
                s_c2.at[side], r_c2.at[side], (mate, me),
            ).wait_send()
    wait_all(stat, s_all.at[0], slabs)
    wait_all(mom, s_all.at[1], slabs)


def first_solve(slabs, lc, pt, u):
    depth, nx, cols = lc.shape
    plane = (nx + 2 * PAD, cols)
    full = pl.BlockSpec(memory_space=VMEM)
    return pl.pallas_call(
        functools.partial(first_kernel, slabs),
        name="first_solve",
        out_shape=[
            jax.ShapeDtypeStruct((depth, nx, cols), F32),
            jax.ShapeDtypeStruct((2, 5, nx, cols), F32),
            jax.ShapeDtypeStruct((2, nx, cols), F32),
            jax.ShapeDtypeStruct((8, 128), F32),
        ],
        in_specs=[full] * 3,
        out_specs=[full] * 4,
        scratch_shapes=[VMEM((depth + 2, *plane), F32)] * 3
        + [
            VMEM((depth, nx, cols), F32),
            VMEM((depth, nx, cols), F32),
            VMEM((depth, *plane), F32),
            VMEM((depth + 1, nx, cols), F32),
        ]
        + [VMEM((depth + 2, *plane), F32)] * 4
        + [
            VMEM((2, nx, cols), F32),
            VMEM((2, nx, cols), F32),
            VMEM((2, 4, nx, cols), F32),
            VMEM((slabs, 8, 128), F32),
            VMEM((slabs, 8, 128), F32),
        ]
        + [DMA((2, 2)), DMA((2, 2))]
        + [DMA((2,))] * 8
        + [DMA((4, 2)), DMA((4, 2)), DMA((2,)), DMA((2,))],
        compiler_params=pltpu.CompilerParams(
            collective_id=0, has_side_effects=True, vmem_limit_bytes=56 << 20
        ),
    )(lc, pt, u)


def gather_kernel(group, nx, dipoles, bounds, keys, perm, field, out):
    out[...] = jnp.zeros_like(out)
    cols = field.shape[1]
    lane = lane_iota((1, cols))
    short = lane_iota((1, 128))
    start, stop, base = bounds[0], bounds[1], bounds[2]
    limit = field.shape[0] - 1
    top = keys.shape[0] - 1

    def body(g, carry):
        parts = []
        for e in range(group):
            j = start + g * group + e
            at = jnp.minimum(j, top)
            key, o = keys[at], perm[at]
            line = jnp.clip(key // cols - base, 0, limit)
            sign = jnp.where(j < stop, jnp.where(o < dipoles, 1.0, -1.0), 0.0)
            k = lax.rem(o, dipoles)
            picked = jnp.where(lane == lax.rem(key, cols), field[pl.ds(line, 1), :], 0.0)
            value = jnp.sum(picked, axis=1, keepdims=True) * sign
            parts.append((k // 128, jnp.where(short == lax.rem(k, 128), value, 0.0)))
        for line, value in parts:
            out[pl.ds(line, 1), :] = out[pl.ds(line, 1), :] + value
        return carry

    lax.fori_loop(0, (stop - start + group - 1) // group, body, 0)


def gather(bounds, keys, perm, field, dipoles):
    smem = pl.BlockSpec(memory_space=SMEM)
    full = pl.BlockSpec(memory_space=VMEM)
    return pl.pallas_call(
        functools.partial(gather_kernel, 8, field.shape[1], dipoles),
        name="gather",
        out_shape=jax.ShapeDtypeStruct((dipoles // 128, 128), F32),
        in_specs=[smem, smem, smem, full],
        out_specs=full,
        compiler_params=pltpu.CompilerParams(vmem_limit_bytes=24 << 20),
    )(bounds, keys, perm, field)


def share_kernel(slabs, part, out, buf, send_sem, recv_sem):
    src = lax.axis_index("src")
    me = lax.axis_index("slab")
    greet(src, me, slabs, ())
    buf[0] = part[...]
    send_all(buf, send_sem, recv_sem, src, me, slabs)
    wait_all(buf, recv_sem, slabs)
    out[...] = jnp.sum(buf[...], axis=0)
    wait_all(buf, send_sem, slabs)


def share(slabs, part):
    full = pl.BlockSpec(memory_space=VMEM)
    return pl.pallas_call(
        functools.partial(share_kernel, slabs),
        name="share_data",
        out_shape=jax.ShapeDtypeStruct(part.shape, F32),
        in_specs=[full],
        out_specs=full,
        scratch_shapes=[VMEM((slabs, *part.shape), F32), DMA(()), DMA(())],
        compiler_params=pltpu.CompilerParams(
            collective_id=1, has_side_effects=True, vmem_limit_bytes=16 << 20
        ),
    )(part)


def scatter_kernel(group, nx, dipoles, bounds, keys, perm, data, out):
    planes, _, cols = out.shape
    lane = lane_iota((1, cols))
    start, stop, base = bounds[0], bounds[1], bounds[2]
    top = keys.shape[0] - 1

    def clear(q, carry):
        out[q] = jnp.zeros(out.shape[1:], F32)
        return carry

    lax.fori_loop(0, planes, clear, 0)

    def body(g, carry):
        parts = []
        for e in range(group):
            j = start + g * group + e
            at = jnp.minimum(j, top)
            key, o = keys[at], perm[at]
            line = jnp.clip(key // cols - base, 0, planes * nx - 1)
            sign = jnp.where(j < stop, jnp.where(o < dipoles, 1.0, -1.0), 0.0)
            k = lax.rem(o, dipoles)
            value = data[k // 128, lax.rem(k, 128)] * sign
            parts.append((line // nx, PAD + lax.rem(line, nx), jnp.where(lane == lax.rem(key, cols), value, 0.0)))
        for q, line, value in parts:
            out[q, pl.ds(line, 1), :] = out[q, pl.ds(line, 1), :] + value
        return carry

    lax.fori_loop(0, (stop - start + group - 1) // group, body, 0)


def scatter(bounds, keys, perm, data, planes, nx, cols):
    smem = pl.BlockSpec(memory_space=SMEM)
    full = pl.BlockSpec(memory_space=VMEM)
    dipoles = data.shape[0] * 128
    return pl.pallas_call(
        functools.partial(scatter_kernel, 8, nx, dipoles),
        name="scatter",
        out_shape=jax.ShapeDtypeStruct((planes, nx + 2 * PAD, cols), F32),
        in_specs=[smem, smem, smem, smem],
        out_specs=full,
        compiler_params=pltpu.CompilerParams(vmem_limit_bytes=24 << 20),
    )(bounds, keys, perm, data)


def second_kernel(
    slabs, lc, halo, u, uh, mean_in, v0, out,
    sig, dg, hx, hy, hz, v1, v2, v3, adj, give, take, pair, cross, mom,
    s_all, r_all, s_give, r_give, s_pair, r_pair, s_out, r_out,
):
    src = lax.axis_index("src")
    me = lax.axis_index("slab")
    depth, nx, cols = lc.shape
    half = depth // 2
    core = lax.rem(src, 2)
    mate, across = flip(src, 1), flip(src, 2)
    greet(src, me, slabs, (mate, across))
    wide = depth + 2 * WIDE

    zero_pads(sig, nx)
    zero_pads(hy, nx)
    for ref in (v1, v2, v3, adj):
        zero_pads(ref, nx)

    def own(q, carry):
        for r, rows in chunks(nx):
            sig[q + WIDE + 1, pl.ds(PAD + r, rows), :] = jnp.exp(lc[q, pl.ds(r, rows), :])
        return carry

    lax.fori_loop(0, depth, own, 0)
    low_in, high_in = (me > 0).astype(F32), (me < slabs - 1).astype(F32)

    def sides(n, carry):
        for r, rows in chunks(nx):
            sig[WIDE - n, pl.ds(PAD + r, rows), :] = low_in * jnp.exp(halo[0, n, pl.ds(r, rows), :])
            sig[WIDE + 1 + depth + n, pl.ds(PAD + r, rows), :] = high_in * jnp.exp(halo[1, n, pl.ds(r, rows), :])
        return carry

    lax.fori_loop(0, WIDE + 1, sides, 0)
    first, last = WIDE - me * depth, WIDE + (slabs - me) * depth - 1
    make_coefs(sig, dg, hx, hy, hz, wide, first, last, nx)
    make_top(sig, hz, wide, first, last, nx)

    mean = mean_in[0:1, 0:1]
    scale = 6.0 * mean
    inv = 1.0 / scale
    fields = (v0, v1, v2, v3)
    zero = jnp.zeros((8, cols), F32)
    dots = []
    for k in range(3):
        shift = THETA[k] * mean * inv

        def step(q, accs, k=k, shift=shift, dotted=True):
            accs = list(accs)
            for r, rows in chunks(nx):
                here, image = operator(fields[k], q + 1, dg, hx, hy, hz, q + k + 1, r, rows)
                new = inv * image - shift * here
                fields[k + 1][q, pl.ds(PAD + r, rows), :] = new
                if not dotted:
                    continue
                if k == 0:
                    accs[0] = accs[0] + fold(here * here)
                for i in range(k + 1):
                    other = here if i == k else fields[i][q + k + 1 - i, pl.ds(PAD + r, rows), :]
                    accs[i + (k == 0)] = accs[i + (k == 0)] + fold(new * other)
                accs[-1] = accs[-1] + fold(new * new)
            return tuple(accs)

        planes = wide - 2 * (k + 1)
        rim = WIDE - (k + 1)
        plain = functools.partial(step, dotted=False)
        lax.fori_loop(0, rim, plain, ())
        dots.extend(lax.fori_loop(rim, rim + depth, step, (zero,) * (3 if k == 0 else k + 2)))
        lax.fori_loop(rim + depth, planes, plain, ())

    def energy(q, acc):
        for r, rows in chunks(nx):
            here, image = operator(v3, q + 1, dg, hx, hy, hz, q + WIDE, r, rows)
            acc = acc + fold(here * image)
        return acc

    dots.append(lax.fori_loop(0, depth, energy, zero))
    mom[0] = jnp.broadcast_to(pack_row(dots), (8, 128))
    send_all(mom, s_all, r_all, src, me, slabs)
    wait_all(mom, r_all, slabs)
    row = jnp.sum(mom[...], axis=0)[0:1]
    c = solve_small(row, scale, [t * mean for t in THETA])

    def combine(q, carry):
        for r, rows in chunks(nx):
            value = c[3] * v3[q, pl.ds(PAD + r, rows), :]
            for i in (0, 1, 2):
                value = value + c[i] * fields[i][q + 3 - i, pl.ds(PAD + r, rows), :]
            adj[q, pl.ds(PAD + r, rows), :] = value
        return carry

    lax.fori_loop(0, depth + 2, combine, 0)

    def partial(q, low, high, dst, slot):
        for r, rows in chunks(nx):
            f = u[q, pl.ds(r, rows), :]
            a = adj[q + 1, pl.ds(PAD + r, rows), :]
            lane = lane_iota(f.shape)
            fr = jnp.where(lane == cols - 1, 0.0, next_lane(f))
            ar = jnp.where(lane == cols - 1, 0.0, next_lane(a))
            flow = (f - fr) * (a - ar)
            total = flow + jnp.where(lane == 0, f * a, prev_lane(flow))
            if r + rows < nx:
                fu = u[q, pl.ds(r + 1, rows), :]
            else:
                fu = jnp.concatenate([u[q, pl.ds(r + 1, rows - 1), :], jnp.zeros((1, cols), F32)], axis=0)
            if r > 0:
                fd = u[q, pl.ds(r - 1, rows), :]
            else:
                fd = jnp.concatenate([jnp.zeros((1, cols), F32), u[q, pl.ds(0, rows - 1), :]], axis=0)
            total = total + (f - fu) * (a - adj[q + 1, pl.ds(PAD + r + 1, rows), :])
            total = total + (f - fd) * (a - adj[q + 1, pl.ds(PAD + r - 1, rows), :])
            total = total + (f - low[0][low[1], pl.ds(r, rows), :]) * (a - adj[q, pl.ds(PAD + r, rows), :])
            total = total + (f - high[0][high[1], pl.ds(r, rows), :]) * (a - adj[q + 2, pl.ds(PAD + r, rows), :])
            scaled = -0.5 * sig[q + WIDE + 1, pl.ds(PAD + r, rows), :] * total
            dst[slot, pl.ds(r, rows), :] = scaled

    def part_of(first_plane, dst, after):
        for n in range(half):
            @pl.when(first_plane == 0)
            def _():
                partial(n, (uh, 0) if n == 0 else (u, n - 1), (u, n + 1), dst, n)

            @pl.when(first_plane != 0)
            def _():
                q = half + n
                partial(q, (u, q - 1), (uh, 1) if q == depth - 1 else (u, q + 1), dst, n)

            after(n)

    def copy_give(n):
        return remote(give.at[n], take.at[n], s_give.at[n], r_give.at[n], (mate, me))

    def copy_pair(n):
        return remote(pair.at[n], cross.at[n], s_pair.at[n], r_pair.at[n], (across, me))

    def copy_out(n):
        slot = core * half + n
        return remote(out.at[slot], out.at[slot], s_out.at[n], r_out.at[n], (mate, me))

    part_of((1 - core) * half, give, lambda n: copy_give(n).start())

    def kept(n):
        copy_give(n).wait_recv()
        pair[n] = pair[n] + take[n]
        copy_pair(n).start()

    part_of(core * half, pair, kept)
    for n in range(half):
        copy_pair(n).wait_recv()
        out[core * half + n] = pair[n] + cross[n]
        copy_out(n).start()
    for n in range(half):
        copy_out(n).wait_recv()
    for n in range(half):
        copy_out(n).wait_send()
        copy_give(n).wait_send()
        copy_pair(n).wait_send()
    wait_all(mom, s_all, slabs)


def second_solve(slabs, lc, halo, u, uh, mean, v0):
    depth, nx, cols = lc.shape
    plane = (nx + 2 * PAD, cols)
    wide = depth + 2 * WIDE
    half = depth // 2
    full = pl.BlockSpec(memory_space=VMEM)
    return pl.pallas_call(
        functools.partial(second_kernel, slabs),
        name="second_solve",
        out_shape=jax.ShapeDtypeStruct((depth, nx, cols), F32),
        in_specs=[full] * 6,
        out_specs=full,
        scratch_shapes=[
            VMEM((wide + 2, *plane), F32),
            VMEM((wide, nx, cols), F32),
            VMEM((wide, nx, cols), F32),
            VMEM((wide, *plane), F32),
            VMEM((wide + 1, nx, cols), F32),
            VMEM((wide - 2, *plane), F32),
            VMEM((wide - 4, *plane), F32),
            VMEM((wide - 6, *plane), F32),
            VMEM((depth + 2, *plane), F32),
        ]
        + [VMEM((half, nx, cols), F32)] * 4
        + [VMEM((slabs, 8, 128), F32)]
        + [DMA(()), DMA(())]
        + [DMA((half,))] * 6,
        compiler_params=pltpu.CompilerParams(
            collective_id=2, has_side_effects=True, vmem_limit_bytes=58 << 20
        ),
    )(lc, halo, u, uh, mean, v0)


def shards(slabs, log_cond, perturb, potentials, rec_depth, rec_plan):
    depth, nx, cols = log_cond.shape
    plane = nx * cols
    dipoles = rec_depth.shape[1]
    me = lax.axis_index("slab")
    u = potentials[0]
    flat = (rec_depth * plane + rec_plan).reshape(-1)
    keys, perm = lax.sort_key_val(flat, jnp.arange(2 * dipoles, dtype=jnp.int32))
    planes = rec_depth.reshape(-1)

    def bounds(first, last):
        return jnp.stack([
            jnp.sum((planes < first).astype(jnp.int32)),
            jnp.sum((planes < last).astype(jnp.int32)),
            first * nx,
        ])

    tangent, halo, uh, mean = first_solve(slabs, log_cond, perturb, u)
    part = gather(
        bounds(me * depth, (me + 1) * depth), keys, perm, tangent.reshape(depth * nx, cols), dipoles
    )
    data = share(slabs, part)
    back = scatter(
        bounds(me * depth - WIDE, (me + 1) * depth + WIDE), keys, perm, data, depth + 2 * WIDE, nx, cols
    )
    return second_solve(slabs, log_cond, halo, u, uh, mean, back)


def solution(mesh):
    in_specs = (
        P("slab", None, None),
        P("slab", None, None),
        P("src", "slab", None, None),
        P(),
        P(),
    )
    return jax.shard_map(
        functools.partial(shards, mesh.shape["slab"]),
        mesh=mesh,
        in_specs=in_specs,
        out_specs=P("slab", None, None),
        check_vma=False,
    )
```

```python
import functools

import jax
import jax.numpy as jnp
from jax import lax
from jax.experimental import pallas as pl
from jax.experimental.pallas import tpu as pltpu
from jax.sharding import PartitionSpec as P

MESH = pl.DeviceIdType.MESH
F32 = jnp.float32
VMEM = pltpu.VMEM
SMEM = pltpu.SMEM
DMA = pltpu.SemaphoreType.DMA
PAD = 8
WIDE = 4
EARLY = 4
ROWS = 64
THETA = (6.0, 2.0, 10.0)


def lane_iota(shape):
    return lax.broadcasted_iota(jnp.int32, shape, len(shape) - 1)


def fold(value):
    rows, cols = value.shape
    return jnp.sum(value.reshape(rows // 8, 8, cols), axis=0)


def next_lane(value):
    return pltpu.roll(value, value.shape[1] - 1, 1)


def prev_lane(value):
    return pltpu.roll(value, 1, 1)


def chunks(count, start=0):
    out = []
    done = 0
    while done < count:
        rows = min(ROWS, count - done)
        out.append((start + done, rows))
        done += rows
    return out


def make_coefs(sig, dg, hx, hy, hz, start, stop, first, last, pieces, top=True):
    cols = sig.shape[-1]

    def body(q, carry):
        low_in = jnp.logical_and(q - 1 >= first, q <= last).astype(F32)
        for r, rows in pieces:
            here = sig[q + 1, pl.ds(PAD + r, rows), :]
            up = sig[q + 1, pl.ds(PAD + r + 1, rows), :]
            down = sig[q + 1, pl.ds(PAD + r - 1, rows), :]
            low = sig[q, pl.ds(PAD + r, rows), :]
            high = sig[q + 2, pl.ds(PAD + r, rows), :]
            lane = lane_iota(here.shape)
            right = jnp.where(lane == cols - 1, 0.0, next_lane(here))
            left = jnp.where(lane == 0, 0.0, prev_lane(here))
            hx[q, pl.ds(r, rows), :] = jnp.where(lane == cols - 1, 0.0, 0.5 * (here + right))
            hy[q, pl.ds(PAD + r, rows), :] = 0.5 * (here + up)
            hz[q, pl.ds(r, rows), :] = (0.5 * low_in) * (here + low)
            total = ((up + down) + (left + right)) + (low + high)
            dg[q, pl.ds(r, rows), :] = 3.0 * here + 0.5 * total
        return carry

    lax.fori_loop(start, stop, body, 0)
    if not top:
        return
    inside = jnp.logical_and(stop - 1 >= first, stop <= last).astype(F32)
    for r, rows in pieces:
        here = sig[stop + 1, pl.ds(PAD + r, rows), :]
        low = sig[stop, pl.ds(PAD + r, rows), :]
        hz[stop, pl.ds(r, rows), :] = (0.5 * inside) * (here + low)


def operator(v, p, dg, hx, hy, hz, q, r, rows):
    here = v[p, pl.ds(PAD + r, rows), :]
    wx = hx[q, pl.ds(r, rows), :]
    acc = dg[q, pl.ds(r, rows), :] * here
    acc = acc - wx * next_lane(here)
    acc = acc - prev_lane(wx * here)
    acc = acc - hy[q, pl.ds(PAD + r, rows), :] * v[p, pl.ds(PAD + r + 1, rows), :]
    acc = acc - hy[q, pl.ds(PAD + r - 1, rows), :] * v[p, pl.ds(PAD + r - 1, rows), :]
    acc = acc - hz[q, pl.ds(r, rows), :] * v[p - 1, pl.ds(PAD + r, rows), :]
    acc = acc - hz[q + 1, pl.ds(r, rows), :] * v[p + 1, pl.ds(PAD + r, rows), :]
    return here, acc


def zero_pads(ref, nx):
    zero = jnp.zeros((ref.shape[0], PAD, ref.shape[2]), F32)
    ref[:, pl.ds(0, PAD), :] = zero
    ref[:, pl.ds(PAD + nx, PAD), :] = zero


def splat(row, index):
    return jnp.sum(jnp.where(lane_iota(row.shape) == index, row, 0.0), axis=1, keepdims=True)


def solve_small(row, scale, thetas, n=0):
    gram = {}
    for i in range(4):
        for j in range(i + 1):
            gram[i, j] = gram[j, i] = splat(row, n)
            n += 1
    last = splat(row, n)
    mat = {}
    for i in range(4):
        for j in range(i + 1):
            if j == 3:
                mat[i, j] = last
            else:
                mat[i, j] = scale * gram[i, j + 1] + thetas[j] * gram[i, j]
    low, inv = {}, {}
    for j in range(4):
        pivot = mat[j, j]
        for k in range(j):
            pivot = pivot - low[j, k] * low[j, k] * mat["d", k]
        mat["d", j] = pivot
        good = pivot > 1e-7 * mat[j, j]
        inv[j] = jnp.where(good, 1.0 / jnp.where(good, pivot, 1.0), 0.0)
        for i in range(j + 1, 4):
            value = mat[i, j]
            for k in range(j):
                value = value - low[i, k] * low[j, k] * mat["d", k]
            low[i, j] = value * inv[j]
    y = []
    for i in range(4):
        value = gram[i, 0]
        for k in range(i):
            value = value - low[i, k] * y[k]
        y.append(value)
    c = [None] * 4
    for i in reversed(range(4)):
        value = y[i] * inv[i]
        for k in range(i + 1, 4):
            value = value - low[k, i] * c[k]
        c[i] = value
    return c


def pack_row(accs):
    lane = lane_iota((1, 128))
    row = jnp.zeros((1, 128), F32)
    for n, acc in enumerate(accs):
        total = jnp.sum(jnp.sum(acc, axis=0, keepdims=True), axis=1, keepdims=True)
        row = row + jnp.where(lane == n, total, 0.0)
    return row


def remote(src_ref, dst_ref, send_sem, recv_sem, target):
    return pltpu.make_async_remote_copy(
        src_ref=src_ref,
        dst_ref=dst_ref,
        send_sem=send_sem,
        recv_sem=recv_sem,
        device_id=target,
        device_id_type=MESH,
    )


def flip(src, bit):
    return src + bit - 2 * bit * (lax.rem(src // bit, 2))


def partners(me, slabs):
    near = 4
    fours = slabs // near
    place, four = lax.rem(me, near), me // near
    return (
        [four * near + lax.rem(place + d, near) for d in range(1, near)],
        [lax.rem(four + d, fours) * near + place for d in range(1, fours)],
    )


def pair_group(me):
    place = lax.rem(me, 4)
    return [me - place + lax.rem(place + d, 4) for d in range(4)]


def signal_all(src, me, slabs, others):
    barrier = pltpu.get_barrier_semaphore()
    targets = [(src, t) for group in partners(me, slabs) for t in group] + others
    for target in targets:
        pl.semaphore_signal(barrier, inc=1, device_id=target, device_id_type=MESH)
    return barrier, len(targets)


class Sum:
    def __init__(self, src, me, slabs, levels, across=None):
        groups = [[(src, t) for t in group] for group in partners(me, slabs)]
        if across is not None:
            groups[0] += [(across, t) for t in pair_group(me)]
        self.levels = [(level, group) for level, group in zip(levels, groups) if group]

    def send(self, n, value):
        (buf, send_sem, recv_sem), group = self.levels[n]
        buf[0] = value
        for d, target in enumerate(group):
            remote(buf.at[0], buf.at[d + 1], send_sem, recv_sem, target).start()

    def _wait(self, n, which):
        level, group = self.levels[n]
        rest = level[0].at[pl.ds(1, len(group))]
        pltpu.make_async_copy(rest, rest, level[which]).wait()

    def receive(self, n):
        self._wait(n, 2)
        return jnp.sum(self.levels[n][0][0][...], axis=0)

    def start(self, value):
        self.send(0, value)

    def middle(self):
        value = self.receive(0)
        if len(self.levels) > 1:
            self.send(1, value)
        return value

    def end(self, value):
        return self.receive(1) if len(self.levels) > 1 else value

    def whole(self, value):
        self.start(value)
        return self.end(self.middle())

    def close(self):
        for n in range(len(self.levels)):
            self._wait(n, 1)


def sum_scratch(slabs, shape, first=4):
    return [
        VMEM((first, *shape), F32), DMA(()), DMA(()),
        VMEM((max(slabs // 4, 2), *shape), F32), DMA(()), DMA(()),
    ]


def sum_levels(refs):
    return (refs[0:3], refs[3:6])


def first_kernel(
    slabs, lc_in, pt_in, u, tan, mean_out, lc_half, lc_near, u_mine, u_first, u_rest,
    lc, pt, lch, uh, sig, wgt, uw, dg, hx, hy, hz, v0, v1, v2, v3, pth, edge, relayed,
    s_load, s_take, s_first, r_first, s_c, r_c, s_x, r_x, s_core, r_core, s_v, r_v, s_e, r_e, s_out, r_in, *sums,
):
    src = lax.axis_index("src")
    me = lax.axis_index("slab")
    depth, nx, cols = lc.shape
    half = nx // 2
    has_low = me > 0
    has_high = me < slabs - 1
    core, side_x = lax.rem(src, 2), src // 2
    mate, across = flip(src, 1), flip(src, 2)
    inner_rows = pl.ds(PAD, nx)
    loads = [
        pltpu.make_async_copy(u, uw.at[pl.ds(1, depth), inner_rows], s_load.at[0]),
        pltpu.make_async_copy(lc_in, lc, s_load.at[1]),
        pltpu.make_async_copy(pt_in, pt, s_load.at[2]),
    ]
    for load in loads:
        load.start()
    ring = [(src, lax.rem(me + 1, slabs)), (src, lax.rem(me + slabs - 1, slabs))]
    barrier, count = signal_all(src, me, slabs, ring + [(mate, me)] + [(across, t) for t in (me, ring[0][1], ring[1][1])])
    pl.semaphore_wait(barrier, count)
    mean_sum = Sum(src, me, slabs, sum_levels(sums[0:6]))
    mom_sum = Sum(src, me, slabs, sum_levels(sums[6:12]))

    def arrives(side):
        return has_low if side == 0 else has_high

    def below(side):
        return me + 1 if side == 0 else me - 1

    def sends(side):
        return has_high if side == 0 else has_low

    def near(side):
        return depth - 1 if side == 0 else 0

    def part(n):
        return pl.ds(n * half, half)

    def copy_u(side, n, to, slot=None, onward=False):
        return routed(
            u.at[near(side), part(n)], uh.at[side, part(n)],
            s_first.at[side, n], r_first.at[side, n], to, side, slot, onward,
        )

    low_mid = slabs // 2 - 1
    by_relay = (
        jnp.logical_and(me == low_mid, side_x == 1),
        jnp.logical_and(me == low_mid + 1, side_x == 0),
    )

    def send(n, side, copy, slot):
        if n == 0:
            pl.when(sends(side))(lambda: copy(side, n, below(side)).start())
            return
        pl.when(jnp.logical_and(sends(side), jnp.logical_not(by_relay[side])))(
            lambda: copy(side, n, below(side)).start()
        )
        pl.when(by_relay[side])(lambda: copy(side, n, me, slot).start())

    def relay(copy, slot):
        for side in (0, 1):
            @pl.when(jnp.logical_and(me == low_mid, side_x == side))
            def _():
                remote(relayed.at[slot], relayed.at[slot], s_out.at[slot], r_in.at[slot], (across, me)).wait_recv()
                copy(side, 1, me, slot, True).start()

    def routed(ref, dst, send_sem, recv_sem, to, side, slot, onward):
        if slot is None:
            return remote(ref, dst, send_sem, recv_sem, (src, to))
        if onward:
            return remote(relayed.at[slot], dst, s_out.at[slot], recv_sem, (across, me + 1 - side))
        return remote(ref, relayed.at[slot], send_sem, r_in.at[slot], (across, me - side))

    my_rows = pl.ds(pl.multiple_of(half * side_x, PAD), half)
    their_rows = pl.ds(pl.multiple_of(half * (1 - side_x), PAD), half)

    def copy_c(ref, dst, side, to):
        return remote(
            ref.at[near(side), my_rows], dst.at[side, my_rows], s_c.at[side], r_c.at[side], (src, to)
        )

    def swap(ref, side, rows):
        return remote(ref.at[side, rows], ref.at[side, rows], s_x.at[side], r_x.at[side], (across, me))

    def forward(ref, side):
        return remote(ref.at[side], ref.at[side], s_core.at[side], r_core.at[side], (mate, me))

    def by_core(body):
        pl.when(core == 0)(lambda: body(lc_in, lch))
        pl.when(core == 1)(lambda: body(pt_in, pth))

    for side in (0, 1):
        @pl.when(sends(side))
        def _():
            by_core(lambda ref, dst: copy_c(ref, dst, side, below(side)).start())
    for n in (0, 1):
        for side in (0, 1):
            send(n, side, copy_u, 0)

    for ref in (sig, wgt, uw, hy, v0, v1, v2, v3):
        zero_pads(ref, nx)
    for load in loads:
        load.wait()

    def own(q, acc):
        for r, rows in chunks(nx):
            value = jnp.exp(lc[q, pl.ds(r, rows), :])
            sig[q + 1, pl.ds(PAD + r, rows), :] = value
            wgt[q + 1, pl.ds(PAD + r, rows), :] = value * pt[q, pl.ds(r, rows), :]
            acc = acc + fold(value)
        return acc

    acc = lax.fori_loop(0, depth, own, jnp.zeros((8, cols), F32))
    mean_sum.start(pack_row([acc]))

    fields = (v0, v1, v2, v3)
    for ref in fields:
        for side in (0, 1):
            def clear(ref=ref, side=side):
                ref[side * (depth + 1), pl.ds(PAD, nx), :] = jnp.zeros((nx, cols), F32)

            if ref is v3:
                clear()
            else:
                pl.when(jnp.logical_not(arrives(side)))(clear)
    mean_part = mean_sum.middle()

    for side in (0, 1):
        @pl.when(arrives(side))
        def _():
            def body(ref, dst):
                copy_c(ref, dst, side, me).wait_recv()
                swap(dst, side, my_rows).start()

            by_core(body)
    relay(copy_u, 0)
    for side in (0, 1):
        @pl.when(arrives(side))
        def _():
            def body(ref, dst):
                swap(dst, side, their_rows).wait_recv()
                forward(dst, side).start()

            by_core(body)

    def rhs_rows(q, pieces):
        for r, rows in pieces:
            c = wgt[q + 1, pl.ds(PAD + r, rows), :]
            f = uw[q + 1, pl.ds(PAD + r, rows), :]
            lane = lane_iota(c.shape)
            cr = jnp.where(lane == cols - 1, 0.0, next_lane(c))
            fr = jnp.where(lane == cols - 1, 0.0, next_lane(f))
            flow = (c + cr) * (f - fr)
            total = flow + jnp.where(lane == 0, c * f, -prev_lane(flow))
            for dq, dr in ((0, 1), (0, -1), (1, 0), (-1, 0)):
                cj = wgt[q + 1 + dq, pl.ds(PAD + r + dr, rows), :]
                fj = uw[q + 1 + dq, pl.ds(PAD + r + dr, rows), :]
                total = total + (c + cj) * (f - fj)
            v0[q + 1, pl.ds(PAD + r, rows), :] = -0.5 * total

    def copy_v(k, side, n, to, slot=None, onward=False):
        plane = depth if side == 0 else 1
        halo = 0 if side == 0 else depth + 1
        rows = pl.ds(PAD + n * half, half)
        ref = fields[k]
        return routed(
            ref.at[plane, rows], ref.at[halo, rows], s_v.at[k, side, n], r_v.at[k, side, n], to, side, slot, onward
        )

    def send_edge(k, side, n):
        send(n, 1 - side, functools.partial(copy_v, k), k + 1)

    for n in (0, 1):
        for side in (0, 1):
            plane = 0 if side == 0 else depth + 1

            @pl.when(arrives(side))
            def _():
                if n == 0:
                    pl.when(core == 0)(lambda: forward(pth, side).wait_recv())
                    pl.when(core == 1)(lambda: forward(lch, side).wait_recv())
                copy_u(side, n, me).wait_recv()
                for r, rows in chunks(half, n * half):
                    value = jnp.exp(lch[side, pl.ds(r, rows), :])
                    sig[plane, pl.ds(PAD + r, rows), :] = value
                    wgt[plane, pl.ds(PAD + r, rows), :] = value * pth[side, pl.ds(r, rows), :]
                    uw[plane, pl.ds(PAD + r, rows), :] = uh[side, pl.ds(r, rows), :]

            @pl.when(jnp.logical_not(arrives(side)))
            def _():
                for ref in (sig, wgt, uw):
                    ref[plane, pl.ds(PAD + n * half, half), :] = jnp.zeros((half, cols), F32)
                lch[side, part(n), :] = jnp.zeros((half, cols), F32)

            rhs_rows(0 if side == 0 else depth - 1, chunks(half, n * half))
            send_edge(0, side, n)

    frame_rows = half + PAD
    mine = half * side_x - PAD * side_x
    theirs = (half - PAD) - mine
    takes = []
    for n, (ref, dst, first, at) in enumerate((
        (lc, lc_half, 0, mine),
        (lch, lc_near, 0, mine),
        (uw, u_mine, 0, PAD + mine),
        (uw, u_first, 0, PAD + theirs),
        (uw, u_rest, EARLY, PAD + theirs),
    )):
        rows = pl.ds(pl.multiple_of(at, PAD), frame_rows)
        takes.append(pltpu.make_async_copy(ref.at[pl.ds(first, dst.shape[0]), rows], dst, s_take.at[n]))
    for take in takes:
        take.start()

    def inner(body, carry):
        return lax.fori_loop(1, depth - 1, body, carry)

    def rhs_plane(q, carry):
        rhs_rows(q, chunks(nx))
        return carry

    inner(rhs_plane, 0)
    first, last = -me * depth, (slabs - me) * depth - 1
    make_coefs(sig, dg, hx, hy, hz, 0, depth, first, last, chunks(nx))

    mean = splat(mean_sum.end(mean_part), 0) * (1.0 / (slabs * depth * nx * cols))
    mean_out[...] = jnp.broadcast_to(mean, (8, 128))
    scale = 6.0 * mean
    inv = 1.0 / scale

    zero = jnp.zeros((8, cols), F32)
    dots = []
    for k in range(3):
        shift = THETA[k] * mean * inv

        def step(q, accs, pieces=None, k=k, shift=shift):
            accs = list(accs)
            for r, rows in pieces or chunks(nx):
                here, image = operator(fields[k], q + 1, dg, hx, hy, hz, q, r, rows)
                new = inv * image - shift * here
                fields[k + 1][q + 1, pl.ds(PAD + r, rows), :] = new
                if k == 0:
                    accs[0] = accs[0] + fold(here * here)
                for i in range(k + 1):
                    other = here if i == k else fields[i][q + 1, pl.ds(PAD + r, rows), :]
                    accs[i + (k == 0)] = accs[i + (k == 0)] + fold(new * other)
                accs[-1] = accs[-1] + fold(new * new)
            return tuple(accs)

        accs = inner(step, (zero,) * (3 if k == 0 else k + 2))
        relay(functools.partial(copy_v, k), k + 1)
        for n in (0, 1):
            for side in (0, 1):
                pl.when(arrives(side))(lambda side=side, n=n, k=k: copy_v(k, side, n, me).wait_recv())
                accs = step(0 if side == 0 else depth - 1, accs, chunks(half, n * half))
                if k < 2:
                    send_edge(k + 1, side, n)
        dots.extend(accs)

    def copy_edge(side, to):
        plane = depth if side == 0 else 1
        return remote(
            v3.at[plane, pl.ds(PAD + side * half, half)], edge.at[side], s_e.at[side], r_e.at[side], (src, to)
        )

    for side in (0, 1):
        pl.when(sends(side))(lambda side=side: copy_edge(side, below(side)).start())
    def energy(q, acc):
        for r, rows in chunks(nx):
            here, image = operator(v3, q + 1, dg, hx, hy, hz, q, r, rows)
            acc = acc + fold(here * image)
        return acc

    acc = lax.fori_loop(0, depth, energy, zero)
    for side in (0, 1):
        got = arrives(side)
        pl.when(got)(lambda side=side: copy_edge(side, me).wait_recv())

        @pl.when(jnp.logical_not(got))
        def _():
            edge[side] = jnp.zeros((half, cols), F32)

        for r, rows in chunks(half):
            at = side * half + r
            face = hz[side * depth, pl.ds(at, rows), :] * v3[1 + side * (depth - 1), pl.ds(PAD + at, rows), :]
            acc = acc - 2.0 * fold(face * edge[side, pl.ds(r, rows), :])
    dots.append(acc)
    mom_sum.start(pack_row(dots))
    value = mom_sum.middle()

    row = mom_sum.end(value)
    c = solve_small(row, scale, [t * mean for t in THETA])

    def combine(q, carry):
        for r, rows in chunks(nx):
            value = c[0] * v0[q + 1, pl.ds(PAD + r, rows), :]
            for i in (1, 2, 3):
                value = value + c[i] * fields[i][q + 1, pl.ds(PAD + r, rows), :]
            tan[q, pl.ds(r, rows), :] = value
        return carry

    lax.fori_loop(0, depth, combine, 0)

    for take in takes:
        take.wait()
    for slot in range(4):
        pl.when(me == low_mid)(
            lambda slot=slot: remote(
                relayed.at[slot], relayed.at[slot], s_out.at[slot], r_in.at[slot], (across, me)
            ).wait_send()
        )
    for side in (0, 1):
        @pl.when(sends(side))
        def _():
            copy_c(lc_in, lch, side, me).wait_send()
            copy_edge(side, me).wait_send()
            for n in (0, 1):
                copy_u(side, n, me).wait_send()
                for k in range(3):
                    copy_v(k, side, n, me).wait_send()

        @pl.when(arrives(side))
        def _():
            swap(lch, side, my_rows).wait_send()
            forward(lch, side).wait_send()
    mean_sum.close()
    mom_sum.close()


def first_solve(slabs, lc, pt, u):
    depth, nx, cols = lc.shape
    plane = (nx + 2 * PAD, cols)
    half = nx // 2
    full = pl.BlockSpec(memory_space=VMEM)
    pair = (DMA((2,)), DMA((2,)))
    return pl.pallas_call(
        functools.partial(first_kernel, slabs),
        name="first_solve",
        out_shape=[
            jax.ShapeDtypeStruct((depth, nx, cols), F32),
            jax.ShapeDtypeStruct((8, 128), F32),
            *(
                jax.ShapeDtypeStruct((planes, half + PAD, cols), F32)
                for planes in (depth, 2, depth + 2, EARLY, depth + 2 - EARLY)
            ),
        ],
        in_specs=[pl.BlockSpec(memory_space=pltpu.HBM)] * 3,
        out_specs=[full] * 7,
        scratch_shapes=[VMEM((depth, nx, cols), F32)] * 2
        + [VMEM((2, nx, cols), F32)] * 2
        + [VMEM((depth + 2, *plane), F32)] * 3
        + [
            VMEM((depth, nx, cols), F32),
            VMEM((depth, nx, cols), F32),
            VMEM((depth, *plane), F32),
            VMEM((depth + 1, nx, cols), F32),
        ]
        + [VMEM((depth + 2, *plane), F32)] * 4
        + [VMEM((2, nx, cols), F32), VMEM((2, half, cols), F32), VMEM((4, half, cols), F32)]
        + [DMA((3,)), DMA((5,)), DMA((2, 2)), DMA((2, 2)), *pair, *pair, *pair]
        + [DMA((3, 2, 2)), DMA((3, 2, 2)), *pair, DMA((4,)), DMA((4,))]
        + sum_scratch(slabs, (1, 128)) * 2,
        compiler_params=pltpu.CompilerParams(
            collective_id=0, has_side_effects=True, vmem_limit_bytes=43 << 20
        ),
    )(lc, pt, u)


def search(keys, bound):
    size = keys.shape[0]

    def body(_, ends):
        low, high = ends
        mid = (low + high) // 2
        less = keys[jnp.minimum(mid, size - 1)] < bound
        open_ = low < high
        return (
            jnp.where(jnp.logical_and(open_, less), mid + 1, low),
            jnp.where(jnp.logical_and(open_, jnp.logical_not(less)), mid, high),
        )

    return lax.fori_loop(0, size.bit_length(), body, (jnp.int32(0), jnp.int32(size)))[0]


def bits(count):
    assert count & (count - 1) == 0
    return count.bit_length() - 1


def gather_kernel(group, depth, keys, plan, field, out):
    me = lax.axis_index("slab")
    out[...] = jnp.zeros_like(out)
    lines, cols = field.shape
    nx = lines // depth
    dipoles = plan.shape[1]
    entries = 2 * dipoles
    lane = lane_iota((1, cols))
    short = lane_iota((1, 128))
    start = search(keys, me * depth * entries)
    stop = search(keys, (me + 1) * depth * entries)
    base = me * lines

    def body(g, carry):
        parts = []
        for e in range(group):
            j = start + g * group + e
            key = keys[jnp.minimum(j, entries - 1)]
            o = key & (entries - 1)
            k = o & (dipoles - 1)
            cell = plan[o >> bits(dipoles), k]
            line = ((key >> bits(entries)) << bits(nx)) + (cell >> bits(cols)) - base
            inside = j < stop
            lane_at = jnp.where(inside, cell & (cols - 1), -1)
            picked = jnp.where(lane == lane_at, field[pl.ds(jnp.where(inside, line, 0), 1), :], 0.0)
            value = jnp.sum(picked, axis=1, keepdims=True)
            value = jnp.where(o < dipoles, value, -value)
            parts.append((k >> 7, jnp.where(short == (k & 127), value, 0.0)))
        for line, value in parts:
            out[pl.ds(line, 1), :] = out[pl.ds(line, 1), :] + value
        return carry

    lax.fori_loop(0, (stop - start + group - 1) // group, body, 0)


def gather(keys, plan, field, depth):
    smem = pl.BlockSpec(memory_space=SMEM)
    full = pl.BlockSpec(memory_space=VMEM)
    return pl.pallas_call(
        functools.partial(gather_kernel, 8, depth),
        name="gather",
        out_shape=jax.ShapeDtypeStruct((plan.shape[1] // 128, 128), F32),
        in_specs=[smem, smem, full],
        out_specs=full,
        compiler_params=pltpu.CompilerParams(vmem_limit_bytes=8 << 20),
    )(keys, plan, field)


def share_kernel(slabs, part, out, s_x, r_x, *sums):
    src = lax.axis_index("src")
    me = lax.axis_index("slab")
    side_x = src // 2
    across = flip(src, 2)
    barrier, count = signal_all(src, me, slabs, [(across, me)])
    pl.semaphore_wait(barrier, count)
    total = Sum(src, me, slabs, sum_levels(sums))
    value = total.whole(part[...])
    lines = value.shape[0]
    out[side_x, pl.ds(0, lines), :] = value
    out[side_x, pl.ds(lines, lines), :] = -value
    copy = remote(out.at[side_x], out.at[side_x], s_x, r_x, (across, me))
    copy.start()
    copy.wait()
    total.close()


def share(slabs, part):
    full = pl.BlockSpec(memory_space=VMEM)
    lines = part.shape[0]
    return pl.pallas_call(
        functools.partial(share_kernel, slabs),
        name="share_data",
        out_shape=jax.ShapeDtypeStruct((2, 2 * lines, 128), F32),
        in_specs=[full],
        out_specs=full,
        scratch_shapes=[DMA(()), DMA(())] + sum_scratch(slabs, part.shape),
        compiler_params=pltpu.CompilerParams(
            collective_id=1, has_side_effects=True, vmem_limit_bytes=8 << 20
        ),
    )(part)


def scatter_kernel(group, depth, nx, lines, keys, plan, data, *outs):
    me = lax.axis_index("slab")
    side_x = lax.axis_index("src") // 2
    total, cols = outs[0].shape
    planes = total // lines
    dipoles = plan.shape[1]
    entries = 2 * dipoles
    lane = lane_iota((1, cols))
    low = me * depth - WIDE
    start = search(keys, low * entries)
    stop = search(keys, (low + planes) * entries)
    row_base = (nx // 2) * side_x - 2 * PAD

    def clear(q, carry):
        for out in outs:
            out[pl.ds(pl.multiple_of(q * lines, 8), lines), :] = jnp.zeros((lines, cols), F32)
        return carry

    lax.fori_loop(0, planes, clear, 0)

    def body(g, carry):
        parts = []
        for e in range(group):
            j = start + g * group + e
            key = keys[jnp.minimum(j, entries - 1)]
            o = key & (entries - 1)
            cell = plan[o >> bits(dipoles), o & (dipoles - 1)]
            line = (cell >> bits(cols)) - row_base
            inside = jnp.logical_and(j < stop, jnp.logical_and(line >= PAD, line < lines - PAD))
            hit = lane == jnp.where(inside, cell & (cols - 1), -1)
            at = jnp.where(inside, ((key >> bits(entries)) - low) * lines + line, 0)
            parts.append((at, [jnp.where(hit, data[n, o >> 7, o & 127], 0.0) for n in (0, 1)]))
        for at, values in parts:
            for out, value in zip(outs, values):
                out[pl.ds(at, 1), :] = out[pl.ds(at, 1), :] + value
        return carry

    lax.fori_loop(0, (stop - start + group - 1) // group, body, 0)


def scatter(keys, plan, data, depth, nx, cols):
    smem = pl.BlockSpec(memory_space=SMEM)
    full = pl.BlockSpec(memory_space=VMEM)
    lines = nx // 2 + 4 * PAD
    planes = depth + 2 * WIDE
    back = pl.pallas_call(
        functools.partial(scatter_kernel, 8, depth, nx, lines),
        name="scatter",
        out_shape=[jax.ShapeDtypeStruct((planes * lines, cols), F32)] * 2,
        in_specs=[smem, smem, smem],
        out_specs=[full, full],
        compiler_params=pltpu.CompilerParams(vmem_limit_bytes=8 << 20),
    )(keys, plan, data)
    return [ref.reshape(planes, lines, cols) for ref in back]


def second_kernel(
    slabs, nx, lc_half, lc_near, u_mine, u_first, u_rest, mean_in, v00, v01, out,
    sig, dg, hx, hy, hz, v1, v2, v3, u2, adj, give, take, pair, far,
    s_load, s_u, r_u, s_far, r_far, s_c2, r_c2, s_give, r_give, s_x, r_x, s_own, r_own, s_fwd, r_fwd,
    *sums,
):
    src = lax.axis_index("src")
    me = lax.axis_index("slab")
    depth, _, cols = out.shape
    half = nx // 2
    frame = half + 2 * PAD
    frame_rows = half + PAD
    quarter = depth // 2
    core, side_x = lax.rem(src, 2), src // 2
    mate, across = flip(src, 1), flip(src, 2)
    wide = depth + 2 * WIDE
    ring = [(src, lax.rem(me + 1, slabs)), (src, lax.rem(me + slabs - 1, slabs))]
    barrier, count = signal_all(src, me, slabs, ring + [(mate, me)] + [(across, t) for t in pair_group(me)])
    total = Sum(src, me, slabs, sum_levels(sums), across)
    owned = chunks(half, PAD)
    rims = [(0, PAD), (PAD + half, PAD)]
    every = rims[:1] + owned + rims[1:]

    zero_pads(sig, frame)
    zero_pads(hy, frame)
    for ref in (v1, v2, v3):
        for j in (0, 1):
            zero_pads(ref.at[j], frame)

    outside = pl.ds(pl.multiple_of(PAD + (half + PAD) * side_x, PAD), PAD)
    u2[:, :, pl.ds(pl.multiple_of((half + PAD) * side_x, PAD), PAD), :] = jnp.zeros((2, depth + 2, PAD, cols), F32)
    frame_mine = pl.ds(pl.multiple_of(PAD * (1 - side_x), PAD), frame_rows)
    frame_theirs = pl.ds(pl.multiple_of(PAD * side_x, PAD), frame_rows)
    early = pl.ds(0, EARLY)
    late = pl.ds(EARLY, depth + 2 - EARLY)
    loads = [
        pltpu.make_async_copy(u_mine, u2.at[side_x, :, frame_mine], s_load.at[0]),
        pltpu.make_async_copy(u_first, u2.at[1 - side_x, early, frame_mine], s_load.at[1]),
    ]
    for load in loads:
        load.start()
    low_in, high_in = (me > 0).astype(F32), (me < slabs - 1).astype(F32)

    def conductivity(ref, count, first, factor=None):
        def body(n, carry):
            for r, rows in chunks(frame_rows):
                to = pl.multiple_of(PAD + PAD * (1 - side_x) + r, PAD)
                value = jnp.exp(ref[n, pl.ds(r, rows), :])
                sig[first + 1 + n, pl.ds(to, rows), :] = value if factor is None else factor * value
            sig[first + 1 + n, outside, :] = jnp.zeros((PAD, cols), F32)
            return carry

        lax.fori_loop(0, count, body, 0)

    conductivity(lc_half, depth, WIDE)
    conductivity(lc_near, 1, WIDE - 1, low_in)
    conductivity(lc_near.at[pl.ds(1, 1)], 1, WIDE + depth, high_in)

    arrives = (me > 0, me < slabs - 1)
    sends = (me < slabs - 1, me > 0)
    to_slab = (me + 1, me - 1)
    mine = (pl.ds(2 - 2 * core, 2), pl.ds(2 * core, 2))
    other = (pl.ds(2 * core, 2), pl.ds(2 - 2 * core, 2))

    def copy_far(side, to):
        planes = pl.ds(depth - 3 - 2 * core, 2) if side == 0 else pl.ds(1 + 2 * core, 2)
        return remote(lc_half.at[planes], far.at[side, mine[side]], s_far.at[side], r_far.at[side], (src, to))

    def share_far(side, planes):
        ref = far.at[side, planes]
        return remote(ref, ref, s_c2.at[side], r_c2.at[side], (mate, me))

    copy_rest = remote(u_rest, u2.at[side_x, late, frame_theirs], s_u, r_u, (across, me))
    pl.semaphore_wait(barrier, count)
    for side in (0, 1):
        pl.when(sends[side])(lambda side=side: copy_far(side, to_slab[side]).start())
    copy_rest.start()

    first, last = WIDE - me * depth, WIDE + (slabs - me) * depth - 1
    low_open, high_open = side_x.astype(F32), 1.0 - side_x.astype(F32)

    def coefs(start, stop, top=True):
        make_coefs(sig, dg, hx, hy, hz, start, stop, first, last, every, top)

        def close(q, carry):
            for line, factor in ((2 * PAD - 1, low_open), (2 * PAD + half - 1, high_open)):
                hy[q, pl.ds(line, 1), :] = hy[q, pl.ds(line, 1), :] * factor
            return carry

        lax.fori_loop(start, stop, close, 0)

    mean = mean_in[0:1, 0:1]
    scale = 6.0 * mean
    inv = 1.0 / scale
    zero = jnp.zeros((8, cols), F32)
    fields = [(v0, v1.at[j], v2.at[j], v3.at[j]) for j, v0 in enumerate((v00, v01))]
    sums_of = {}

    def run(k, start, stop, dotted):
        shift = THETA[k] * mean * inv
        for j in (0, 1):
            def step(q, accs, j=j):
                accs = list(accs)
                for r, rows in every:
                    here, image = operator(fields[j][k], q - k, dg, hx, hy, hz, q, r, rows)
                    new = inv * image - shift * here
                    fields[j][k + 1][q - k - 1, pl.ds(PAD + r, rows), :] = new
                    if not dotted or (r, rows) not in owned:
                        continue
                    if k == 0:
                        accs[0] = accs[0] + fold(here * here)
                    for i in range(k + 1):
                        other = here if i == k else fields[j][i][q - i, pl.ds(PAD + r, rows), :]
                        accs[i + (k == 0)] = accs[i + (k == 0)] + fold(new * other)
                    accs[-1] = accs[-1] + fold(new * new)
                return tuple(accs)

            accs = sums_of.get((j, k), (zero,) * (3 if k == 0 else k + 2)) if dotted else ()
            accs = lax.fori_loop(start, stop, step, accs)
            if dotted:
                sums_of[j, k] = accs

    top = WIDE + depth
    coefs(WIDE, top)
    run(0, WIDE, top, True)
    for side in (0, 1):
        @pl.when(arrives[side])
        def _():
            copy_far(side, me).wait_recv()
            share_far(side, mine[side]).start()

        @pl.when(jnp.logical_not(arrives[side]))
        def _():
            far[side] = jnp.zeros(far.shape[1:], F32)

    for k in (1, 2):
        run(k, WIDE + k, top - k, True)
    for side in (0, 1):
        pl.when(arrives[side])(lambda side=side: share_far(side, other[side]).wait_recv())
    conductivity(far.at[0], WIDE, -1, low_in)
    conductivity(far.at[1], WIDE, top + 1, high_in)
    coefs(0, WIDE, False)
    coefs(top, wide)
    for k in range(3):
        run(k, k + 1, WIDE, False)
        if k:
            run(k, WIDE, WIDE + k, True)
            run(k, top - k, top, True)
        run(k, top, wide - k - 1, False)
    dots = [[acc for k in range(3) for acc in sums_of[j, k]] for j in (0, 1)]

    for j in (0, 1):
        def energy(q, acc, j=j):
            for r, rows in owned:
                here, image = operator(v3.at[j], q + 1, dg, hx, hy, hz, q + WIDE, r, rows)
                acc = acc + fold(here * image)
            return acc

        dots[j].append(lax.fori_loop(0, depth, energy, zero))

    row = total.whole(pack_row(dots[0] + dots[1]))
    thetas = [t * mean for t in THETA]
    coef = [solve_small(row, scale, thetas, n) for n in (0, len(dots[0]))]

    def combine(q, carry):
        for j in (0, 1):
            c = coef[j]
            for r, rows in every:
                value = c[3] * v3[j, q, pl.ds(PAD + r, rows), :]
                for i, ref in enumerate(fields[j][:3]):
                    value = value + c[i] * ref[q + 3 - i, pl.ds(PAD + r, rows), :]
                adj[j, q, pl.ds(r, rows), :] = value
        return carry

    lax.fori_loop(0, depth + 2, combine, 0)
    for load in loads:
        load.wait()
    copy_rest.wait()
    for side in (0, 1):
        pl.when(sends[side])(lambda side=side: copy_far(side, me).wait_send())
        pl.when(arrives[side])(lambda side=side: share_far(side, mine[side]).wait_send())

    def partial(q, dst, slot):
        for r, rows in owned:
            total = jnp.zeros((rows, cols), F32)
            for j in (0, 1):
                f = u2[j, q + 1, pl.ds(r, rows), :]
                a = adj[j, q + 1, pl.ds(r, rows), :]
                lane = lane_iota(f.shape)
                fr = jnp.where(lane == cols - 1, 0.0, next_lane(f))
                ar = jnp.where(lane == cols - 1, 0.0, next_lane(a))
                flow = (f - fr) * (a - ar)
                total = total + (flow + jnp.where(lane == 0, f * a, prev_lane(flow)))
                for dq, dr in ((0, 1), (0, -1), (1, 0), (-1, 0)):
                    fj = u2[j, q + 1 + dq, pl.ds(r + dr, rows), :]
                    aj = adj[j, q + 1 + dq, pl.ds(r + dr, rows), :]
                    total = total + (f - fj) * (a - aj)
            scaled = -0.5 * sig[q + WIDE + 1, pl.ds(PAD + r, rows), :] * total
            dst[slot, pl.ds(r - PAD, rows), :] = scaled

    def copy_give(n):
        return remote(give.at[n], take.at[n], s_give.at[n], r_give.at[n], (mate, me))

    rows_mine = pl.ds(pl.multiple_of(half * side_x, PAD), half)
    rows_theirs = pl.ds(pl.multiple_of(half * (1 - side_x), PAD), half)

    def copy_x(n):
        ref = out.at[core * quarter + n, rows_mine]
        return remote(ref, ref, s_x.at[n], r_x.at[n], (across, me))

    def copy_own(n):
        ref = out.at[core * quarter + n, rows_mine]
        return remote(ref, ref, s_own.at[n], r_own.at[n], (mate, me))

    def copy_fwd(n):
        ref = out.at[core * quarter + n, rows_theirs]
        return remote(ref, ref, s_fwd.at[n], r_fwd.at[n], (mate, me))

    def giving(n, carry):
        partial((1 - core) * quarter + n, give, n)
        copy_give(n).start()
        return carry

    def keeping(n, carry):
        partial(core * quarter + n, pair, n)
        copy_give(n).wait_recv()
        for r, rows in chunks(half):
            at = pl.multiple_of(half * side_x + r, PAD)
            out[core * quarter + n, pl.ds(at, rows), :] = pair[n, pl.ds(r, rows), :] + take[n, pl.ds(r, rows), :]
        copy_x(n).start()
        copy_own(n).start()
        return carry

    def passing(n, carry):
        copy_x(n).wait_recv()
        copy_fwd(n).start()
        return carry

    def ending(n, carry):
        copy_own(n).wait_recv()
        copy_fwd(n).wait_recv()
        for copy in (copy_give, copy_x, copy_own, copy_fwd):
            copy(n).wait_send()
        return carry

    for body in (giving, keeping, passing, ending):
        lax.fori_loop(0, quarter, body, 0)
    total.close()


def second_solve(slabs, nx, lc_half, lc_near, u_mine, u_first, u_rest, mean, back):
    depth, _, cols = lc_half.shape
    half = nx // 2
    frame = half + 2 * PAD
    plane = (frame + 2 * PAD, cols)
    wide = depth + 2 * WIDE
    quarter = depth // 2
    full = pl.BlockSpec(memory_space=VMEM)
    anywhere = pl.BlockSpec(memory_space=pl.ANY)
    pair = [DMA((2,)), DMA((2,))]
    return pl.pallas_call(
        functools.partial(second_kernel, slabs, nx),
        name="second_solve",
        out_shape=jax.ShapeDtypeStruct((depth, nx, cols), F32),
        in_specs=[full, full, anywhere, anywhere, anywhere, full, full, full],
        out_specs=full,
        scratch_shapes=[
            VMEM((wide + 2, *plane), F32),
            VMEM((wide, frame, cols), F32),
            VMEM((wide, frame, cols), F32),
            VMEM((wide, *plane), F32),
            VMEM((wide + 1, frame, cols), F32),
            VMEM((2, wide - 2, *plane), F32),
            VMEM((2, wide - 4, *plane), F32),
            VMEM((2, wide - 6, *plane), F32),
            VMEM((2, depth + 2, frame, cols), F32),
            VMEM((2, depth + 2, frame, cols), F32),
        ]
        + [VMEM((quarter, half, cols), F32)] * 3
        + [VMEM((2, WIDE, half + PAD, cols), F32)]
        + [DMA((2,)), DMA(()), DMA(())]
        + pair * 2
        + [DMA((quarter,))] * 8
        + sum_scratch(slabs, (1, 128), 8),
        compiler_params=pltpu.CompilerParams(
            collective_id=2, has_side_effects=True, vmem_limit_bytes=42 << 20
        ),
    )(lc_half, lc_near, u_mine, u_first, u_rest, mean, *back)


def shards(slabs, log_cond, perturb, potentials, rec_depth, rec_plan):
    depth, nx, cols = log_cond.shape
    dipoles = rec_depth.shape[1]
    order = lax.broadcasted_iota(jnp.int32, rec_depth.shape, 0) * dipoles
    order = order + lax.broadcasted_iota(jnp.int32, rec_depth.shape, 1)
    keys = lax.sort((rec_depth * (2 * dipoles) + order).reshape(-1), is_stable=False)
    arguments = (pltpu.with_memory_space_constraint(a, pltpu.HBM) for a in (log_cond, perturb, potentials[0]))
    tangent, mean, lc_half, lc_near, u_mine, u_first, u_rest = first_solve(slabs, *arguments)
    part = gather(keys, rec_plan, tangent.reshape(depth * nx, cols), depth)
    data = share(slabs, part)
    u_first, data = lax.optimization_barrier((u_first, data))
    u_first = lax.ppermute(u_first, "src", [(i, (i + 2) % 4) for i in range(4)])
    back = scatter(keys, rec_plan, data, depth, nx, cols)
    return second_solve(slabs, nx, lc_half, lc_near, u_mine, u_first, u_rest, mean, back)


def solution(mesh):
    in_specs = (
        P("slab", None, None),
        P("slab", None, None),
        P("src", "slab", None, None),
        P(),
        P(),
    )
    return jax.shard_map(
        functools.partial(shards, mesh.shape["slab"]),
        mesh=mesh,
        in_specs=in_specs,
        out_specs=P("slab", None, None),
        check_vma=False,
    )
```

```python
import functools

import jax
import jax.numpy as jnp
from jax import lax
from jax.experimental import pallas as pl
from jax.experimental.pallas import tpu as pltpu
from jax.sharding import PartitionSpec as P

MESH = pl.DeviceIdType.MESH
F32 = jnp.float32
VMEM = pltpu.VMEM
SMEM = pltpu.SMEM
DMA = pltpu.SemaphoreType.DMA
PAD = 8
WIDE = 4
EARLY = 4
ROWS = 64
THETA = (6.0, 2.0, 10.0)


def lane_iota(shape):
    return lax.broadcasted_iota(jnp.int32, shape, len(shape) - 1)


def fold(value):
    rows, cols = value.shape
    return jnp.sum(value.reshape(rows // 8, 8, cols), axis=0)


def next_lane(value):
    return pltpu.roll(value, value.shape[1] - 1, 1)


def prev_lane(value):
    return pltpu.roll(value, 1, 1)


def chunks(count, start=0):
    out = []
    done = 0
    while done < count:
        rows = min(ROWS, count - done)
        out.append((start + done, rows))
        done += rows
    return out


def make_coefs(sig, dg, hx, hy, hz, start, stop, first, last, pieces, top=True):
    cols = sig.shape[-1]

    def body(q, carry):
        low_in = jnp.logical_and(q - 1 >= first, q <= last).astype(F32)
        for r, rows in pieces:
            here = sig[q + 1, pl.ds(PAD + r, rows), :]
            up = sig[q + 1, pl.ds(PAD + r + 1, rows), :]
            down = sig[q + 1, pl.ds(PAD + r - 1, rows), :]
            low = sig[q, pl.ds(PAD + r, rows), :]
            high = sig[q + 2, pl.ds(PAD + r, rows), :]
            lane = lane_iota(here.shape)
            right = jnp.where(lane == cols - 1, 0.0, next_lane(here))
            left = jnp.where(lane == 0, 0.0, prev_lane(here))
            hx[q, pl.ds(r, rows), :] = jnp.where(lane == cols - 1, 0.0, 0.5 * (here + right))
            hy[q, pl.ds(PAD + r, rows), :] = 0.5 * (here + up)
            hz[q, pl.ds(r, rows), :] = (0.5 * low_in) * (here + low)
            total = ((up + down) + (left + right)) + (low + high)
            dg[q, pl.ds(r, rows), :] = 3.0 * here + 0.5 * total
        return carry

    lax.fori_loop(start, stop, body, 0)
    if not top:
        return
    inside = jnp.logical_and(stop - 1 >= first, stop <= last).astype(F32)
    for r, rows in pieces:
        here = sig[stop + 1, pl.ds(PAD + r, rows), :]
        low = sig[stop, pl.ds(PAD + r, rows), :]
        hz[stop, pl.ds(r, rows), :] = (0.5 * inside) * (here + low)


def operator(v, p, dg, hx, hy, hz, q, r, rows):
    here = v[p, pl.ds(PAD + r, rows), :]
    wx = hx[q, pl.ds(r, rows), :]
    acc = dg[q, pl.ds(r, rows), :] * here
    acc = acc - wx * next_lane(here)
    acc = acc - prev_lane(wx * here)
    acc = acc - hy[q, pl.ds(PAD + r, rows), :] * v[p, pl.ds(PAD + r + 1, rows), :]
    acc = acc - hy[q, pl.ds(PAD + r - 1, rows), :] * v[p, pl.ds(PAD + r - 1, rows), :]
    acc = acc - hz[q, pl.ds(r, rows), :] * v[p - 1, pl.ds(PAD + r, rows), :]
    acc = acc - hz[q + 1, pl.ds(r, rows), :] * v[p + 1, pl.ds(PAD + r, rows), :]
    return here, acc


def zero_pads(ref, nx):
    zero = jnp.zeros((ref.shape[0], PAD, ref.shape[2]), F32)
    ref[:, pl.ds(0, PAD), :] = zero
    ref[:, pl.ds(PAD + nx, PAD), :] = zero


def splat(row, index):
    return jnp.sum(jnp.where(lane_iota(row.shape) == index, row, 0.0), axis=1, keepdims=True)


def solve_small(row, scale, thetas, n=0):
    gram = {}
    for i in range(4):
        for j in range(i + 1):
            gram[i, j] = gram[j, i] = splat(row, n)
            n += 1
    last = splat(row, n)
    mat = {}
    for i in range(4):
        for j in range(i + 1):
            if j == 3:
                mat[i, j] = last
            else:
                mat[i, j] = scale * gram[i, j + 1] + thetas[j] * gram[i, j]
    low, inv = {}, {}
    for j in range(4):
        pivot = mat[j, j]
        for k in range(j):
            pivot = pivot - low[j, k] * low[j, k] * mat["d", k]
        mat["d", j] = pivot
        good = pivot > 1e-7 * mat[j, j]
        inv[j] = jnp.where(good, 1.0 / jnp.where(good, pivot, 1.0), 0.0)
        for i in range(j + 1, 4):
            value = mat[i, j]
            for k in range(j):
                value = value - low[i, k] * low[j, k] * mat["d", k]
            low[i, j] = value * inv[j]
    y = []
    for i in range(4):
        value = gram[i, 0]
        for k in range(i):
            value = value - low[i, k] * y[k]
        y.append(value)
    c = [None] * 4
    for i in reversed(range(4)):
        value = y[i] * inv[i]
        for k in range(i + 1, 4):
            value = value - low[k, i] * c[k]
        c[i] = value
    return c


def pack_row(accs):
    lane = lane_iota((1, 128))
    row = jnp.zeros((1, 128), F32)
    for n, acc in enumerate(accs):
        total = jnp.sum(jnp.sum(acc, axis=0, keepdims=True), axis=1, keepdims=True)
        row = row + jnp.where(lane == n, total, 0.0)
    return row


def remote(src_ref, dst_ref, send_sem, recv_sem, target):
    return pltpu.make_async_remote_copy(
        src_ref=src_ref,
        dst_ref=dst_ref,
        send_sem=send_sem,
        recv_sem=recv_sem,
        device_id=target,
        device_id_type=MESH,
    )


def flip(src, bit):
    return src + bit - 2 * bit * (lax.rem(src // bit, 2))


def partners(me, slabs):
    near = 4
    fours = slabs // near
    place, four = lax.rem(me, near), me // near
    return (
        [four * near + lax.rem(place + d, near) for d in range(1, near)],
        [lax.rem(four + d, fours) * near + place for d in range(1, fours)],
    )


def pair_group(me):
    place = lax.rem(me, 4)
    return [me - place + lax.rem(place + d, 4) for d in range(4)]


def signal_all(src, me, slabs, others):
    barrier = pltpu.get_barrier_semaphore()
    targets = [(src, t) for group in partners(me, slabs) for t in group] + others
    for target in targets:
        pl.semaphore_signal(barrier, inc=1, device_id=target, device_id_type=MESH)
    return barrier, len(targets)


class Sum:
    def __init__(self, src, me, slabs, levels, across=None):
        groups = [[(src, t) for t in group] for group in partners(me, slabs)]
        if across is not None:
            groups[0] += [(across, t) for t in pair_group(me)]
        self.levels = [(level, group) for level, group in zip(levels, groups) if group]

    def send(self, n, value):
        (buf, send_sem, recv_sem), group = self.levels[n]
        buf[0] = value
        for d, target in enumerate(group):
            remote(buf.at[0], buf.at[d + 1], send_sem, recv_sem, target).start()

    def _wait(self, n, which):
        level, group = self.levels[n]
        rest = level[0].at[pl.ds(1, len(group))]
        pltpu.make_async_copy(rest, rest, level[which]).wait()

    def receive(self, n):
        self._wait(n, 2)
        return jnp.sum(self.levels[n][0][0][...], axis=0)

    def start(self, value):
        self.send(0, value)

    def middle(self):
        value = self.receive(0)
        if len(self.levels) > 1:
            self.send(1, value)
        return value

    def end(self, value):
        return self.receive(1) if len(self.levels) > 1 else value

    def whole(self, value):
        self.start(value)
        return self.end(self.middle())

    def close(self):
        for n in range(len(self.levels)):
            self._wait(n, 1)


def sum_scratch(slabs, shape, first=4):
    return [
        VMEM((first, *shape), F32), DMA(()), DMA(()),
        VMEM((max(slabs // 4, 2), *shape), F32), DMA(()), DMA(()),
    ]


def sum_levels(refs):
    return (refs[0:3], refs[3:6])


def first_kernel(
    slabs, lc_in, pt_in, u, tan, mean_out, lc_half, lc_near, u_mine, u_first, u_rest,
    lc, pt, lch, uh, sig, wgt, uw, dg, hx, hy, hz, v0, v1, v2, v3, pth, edge, relayed,
    s_load, s_take, s_first, r_first, s_c, r_c, s_x, r_x, s_core, r_core, s_v, r_v, s_e, r_e, s_out, r_in, *sums,
):
    src = lax.axis_index("src")
    me = lax.axis_index("slab")
    depth, nx, cols = lc.shape
    half = nx // 2
    has_low = me > 0
    has_high = me < slabs - 1
    core, side_x = lax.rem(src, 2), src // 2
    mate, across = flip(src, 1), flip(src, 2)
    inner_rows = pl.ds(PAD, nx)
    loads = [
        pltpu.make_async_copy(u, uw.at[pl.ds(1, depth), inner_rows], s_load.at[0]),
        pltpu.make_async_copy(lc_in, lc, s_load.at[1]),
        pltpu.make_async_copy(pt_in, pt, s_load.at[2]),
    ]
    for load in loads:
        load.start()
    ring = [(src, lax.rem(me + 1, slabs)), (src, lax.rem(me + slabs - 1, slabs))]
    barrier, count = signal_all(src, me, slabs, ring + [(mate, me)] + [(across, t) for t in (me, ring[0][1], ring[1][1])])
    pl.semaphore_wait(barrier, count)
    mean_sum = Sum(src, me, slabs, sum_levels(sums[0:6]))
    mom_sum = Sum(src, me, slabs, sum_levels(sums[6:12]))

    def arrives(side):
        return has_low if side == 0 else has_high

    def below(side):
        return me + 1 if side == 0 else me - 1

    def sends(side):
        return has_high if side == 0 else has_low

    def near(side):
        return depth - 1 if side == 0 else 0

    def part(n):
        return pl.ds(n * half, half)

    def copy_u(side, n, to, slot=None, onward=False):
        return routed(
            u.at[near(side), part(n)], uh.at[side, part(n)],
            s_first.at[side, n], r_first.at[side, n], to, slot, onward,
        )

    low_mid = slabs // 2 - 1

    def by_relay(side):
        return jnp.logical_and(me == low_mid + side, side_x == 1 - side)

    def is_relay(side):
        return jnp.logical_and(me == low_mid + side, side_x == side)

    def send(n, side, copy, slot):
        if n == 1:
            pl.when(sends(side))(lambda: copy(side, n, below(side)).start())
            return
        pl.when(jnp.logical_and(sends(side), jnp.logical_not(by_relay(side))))(
            lambda: copy(side, n, below(side)).start()
        )
        pl.when(by_relay(side))(lambda: copy(side, n, me, slot).start())

    def arrived(slot):
        return remote(relayed.at[slot], relayed.at[slot], s_out.at[slot], r_in.at[slot], (across, me))

    def relay(copy, slot):
        for side in (0, 1):
            @pl.when(is_relay(side))
            def _():
                arrived(slot).wait_recv()
                copy(side, 0, below(side), slot, True).start()

    def routed(ref, dst, send_sem, recv_sem, to, slot, onward):
        if slot is None:
            return remote(ref, dst, send_sem, recv_sem, (src, to))
        if onward:
            return remote(relayed.at[slot], dst, s_out.at[slot], recv_sem, (across, to))
        return remote(ref, relayed.at[slot], send_sem, r_in.at[slot], (across, me))

    my_rows = pl.ds(pl.multiple_of(half * side_x, PAD), half)
    their_rows = pl.ds(pl.multiple_of(half * (1 - side_x), PAD), half)

    def copy_c(ref, dst, side, to):
        return remote(
            ref.at[near(side), my_rows], dst.at[side, my_rows], s_c.at[side], r_c.at[side], (src, to)
        )

    def swap(ref, side, rows):
        return remote(ref.at[side, rows], ref.at[side, rows], s_x.at[side], r_x.at[side], (across, me))

    def forward(ref, side):
        return remote(ref.at[side], ref.at[side], s_core.at[side], r_core.at[side], (mate, me))

    def by_core(body):
        pl.when(core == 0)(lambda: body(lc_in, lch))
        pl.when(core == 1)(lambda: body(pt_in, pth))

    for side in (0, 1):
        @pl.when(sends(side))
        def _():
            by_core(lambda ref, dst: copy_c(ref, dst, side, below(side)).start())

    for ref in (sig, wgt, uw, hy, v0, v1, v2, v3):
        zero_pads(ref, nx)
    for load in loads:
        load.wait()

    for side in (0, 1):
        @pl.when(sends(side))
        def _():
            copy_c(lc_in, lch, side, me).wait_send()

    for n in (0, 1):
        for side in (0, 1):
            send(n, side, copy_u, 0)

    def own(q, acc):
        for r, rows in chunks(nx):
            value = jnp.exp(lc[q, pl.ds(r, rows), :])
            sig[q + 1, pl.ds(PAD + r, rows), :] = value
            wgt[q + 1, pl.ds(PAD + r, rows), :] = value * pt[q, pl.ds(r, rows), :]
            acc = acc + fold(value)
        return acc

    acc = lax.fori_loop(0, depth, own, jnp.zeros((8, cols), F32))
    mean_sum.start(pack_row([acc]))

    fields = (v0, v1, v2, v3)
    for ref in fields:
        for side in (0, 1):
            def clear(ref=ref, side=side):
                ref[side * (depth + 1), pl.ds(PAD, nx), :] = jnp.zeros((nx, cols), F32)

            if ref is v3:
                clear()
            else:
                pl.when(jnp.logical_not(arrives(side)))(clear)
    mean_part = mean_sum.middle()

    for side in (0, 1):
        @pl.when(arrives(side))
        def _():
            def body(ref, dst):
                copy_c(ref, dst, side, me).wait_recv()
                swap(dst, side, my_rows).start()

            by_core(body)
    relay(copy_u, 0)
    for side in (0, 1):
        @pl.when(arrives(side))
        def _():
            def body(ref, dst):
                swap(dst, side, their_rows).wait_recv()
                forward(dst, side).start()

            by_core(body)

    def rhs_rows(q, pieces):
        for r, rows in pieces:
            c = wgt[q + 1, pl.ds(PAD + r, rows), :]
            f = uw[q + 1, pl.ds(PAD + r, rows), :]
            lane = lane_iota(c.shape)
            cr = jnp.where(lane == cols - 1, 0.0, next_lane(c))
            fr = jnp.where(lane == cols - 1, 0.0, next_lane(f))
            flow = (c + cr) * (f - fr)
            total = flow + jnp.where(lane == 0, c * f, -prev_lane(flow))
            for dq, dr in ((0, 1), (0, -1), (1, 0), (-1, 0)):
                cj = wgt[q + 1 + dq, pl.ds(PAD + r + dr, rows), :]
                fj = uw[q + 1 + dq, pl.ds(PAD + r + dr, rows), :]
                total = total + (c + cj) * (f - fj)
            v0[q + 1, pl.ds(PAD + r, rows), :] = -0.5 * total

    def copy_v(k, side, n, to, slot=None, onward=False):
        plane = depth if side == 0 else 1
        halo = 0 if side == 0 else depth + 1
        rows = pl.ds(PAD + n * half, half)
        ref = fields[k]
        return routed(
            ref.at[plane, rows], ref.at[halo, rows], s_v.at[k, side, n], r_v.at[k, side, n], to, slot, onward
        )

    def send_edge(k, side, n):
        send(n, 1 - side, functools.partial(copy_v, k), k + 1)

    for n in (0, 1):
        for side in (0, 1):
            plane = 0 if side == 0 else depth + 1

            @pl.when(arrives(side))
            def _():
                if n == 0:
                    pl.when(core == 0)(lambda: forward(pth, side).wait_recv())
                    pl.when(core == 1)(lambda: forward(lch, side).wait_recv())
                copy_u(side, n, me).wait_recv()
                for r, rows in chunks(half, n * half):
                    value = jnp.exp(lch[side, pl.ds(r, rows), :])
                    sig[plane, pl.ds(PAD + r, rows), :] = value
                    wgt[plane, pl.ds(PAD + r, rows), :] = value * pth[side, pl.ds(r, rows), :]
                    uw[plane, pl.ds(PAD + r, rows), :] = uh[side, pl.ds(r, rows), :]

            @pl.when(jnp.logical_not(arrives(side)))
            def _():
                for ref in (sig, wgt, uw):
                    ref[plane, pl.ds(PAD + n * half, half), :] = jnp.zeros((half, cols), F32)
                lch[side, part(n), :] = jnp.zeros((half, cols), F32)

            rhs_rows(0 if side == 0 else depth - 1, chunks(half, n * half))
            send_edge(0, side, n)

    frame_rows = half + PAD
    mine = half * side_x - PAD * side_x
    theirs = (half - PAD) - mine
    takes = []
    for n, (ref, dst, first, at) in enumerate((
        (lc, lc_half, 0, mine),
        (lch, lc_near, 0, mine),
        (uw, u_mine, 0, PAD + mine),
        (uw, u_first, 0, PAD + theirs),
        (uw, u_rest, EARLY, PAD + theirs),
    )):
        rows = pl.ds(pl.multiple_of(at, PAD), frame_rows)
        takes.append(pltpu.make_async_copy(ref.at[pl.ds(first, dst.shape[0]), rows], dst, s_take.at[n]))
    for take in takes:
        take.start()

    def inner(body, carry):
        return lax.fori_loop(1, depth - 1, body, carry)

    def rhs_plane(q, carry):
        rhs_rows(q, chunks(nx))
        return carry

    inner(rhs_plane, 0)
    first, last = -me * depth, (slabs - me) * depth - 1
    make_coefs(sig, dg, hx, hy, hz, 0, depth, first, last, chunks(nx))

    mean = splat(mean_sum.end(mean_part), 0) * (1.0 / (slabs * depth * nx * cols))
    mean_out[...] = jnp.broadcast_to(mean, (8, 128))
    scale = 6.0 * mean
    inv = 1.0 / scale

    zero = jnp.zeros((8, cols), F32)
    dots = []
    for k in range(3):
        shift = THETA[k] * mean * inv

        def step(q, accs, pieces=None, k=k, shift=shift):
            accs = list(accs)
            for r, rows in pieces or chunks(nx):
                here, image = operator(fields[k], q + 1, dg, hx, hy, hz, q, r, rows)
                new = inv * image - shift * here
                fields[k + 1][q + 1, pl.ds(PAD + r, rows), :] = new
                if k == 0:
                    accs[0] = accs[0] + fold(here * here)
                for i in range(k + 1):
                    other = here if i == k else fields[i][q + 1, pl.ds(PAD + r, rows), :]
                    accs[i + (k == 0)] = accs[i + (k == 0)] + fold(new * other)
                accs[-1] = accs[-1] + fold(new * new)
            return tuple(accs)

        accs = inner(step, (zero,) * (3 if k == 0 else k + 2))
        relay(functools.partial(copy_v, k), k + 1)
        for n in (0, 1):
            for side in (0, 1):
                pl.when(arrives(side))(lambda side=side, n=n, k=k: copy_v(k, side, n, me).wait_recv())
                accs = step(0 if side == 0 else depth - 1, accs, chunks(half, n * half))
                if k < 2:
                    send_edge(k + 1, side, n)
        dots.extend(accs)

    def copy_edge(side, to):
        plane = depth if side == 0 else 1
        return remote(
            v3.at[plane, pl.ds(PAD + side * half, half)], edge.at[side], s_e.at[side], r_e.at[side], (src, to)
        )

    for side in (0, 1):
        pl.when(sends(side))(lambda side=side: copy_edge(side, below(side)).start())
    def energy(q, acc):
        for r, rows in chunks(nx):
            here, image = operator(v3, q + 1, dg, hx, hy, hz, q, r, rows)
            acc = acc + fold(here * image)
        return acc

    acc = lax.fori_loop(0, depth, energy, zero)
    for side in (0, 1):
        got = arrives(side)
        pl.when(got)(lambda side=side: copy_edge(side, me).wait_recv())

        @pl.when(jnp.logical_not(got))
        def _():
            edge[side] = jnp.zeros((half, cols), F32)

        for r, rows in chunks(half):
            at = side * half + r
            face = hz[side * depth, pl.ds(at, rows), :] * v3[1 + side * (depth - 1), pl.ds(PAD + at, rows), :]
            acc = acc - 2.0 * fold(face * edge[side, pl.ds(r, rows), :])
    dots.append(acc)
    mom_sum.start(pack_row(dots))
    value = mom_sum.middle()

    row = mom_sum.end(value)
    c = solve_small(row, scale, [t * mean for t in THETA])

    def combine(q, carry):
        for r, rows in chunks(nx):
            value = c[0] * v0[q + 1, pl.ds(PAD + r, rows), :]
            for i in (1, 2, 3):
                value = value + c[i] * fields[i][q + 1, pl.ds(PAD + r, rows), :]
            tan[q, pl.ds(r, rows), :] = value
        return carry

    lax.fori_loop(0, depth, combine, 0)

    for take in takes:
        take.wait()
    for side in (0, 1):
        @pl.when(is_relay(side))
        def _():
            for slot in range(4):
                arrived(slot).wait_send()

    for side in (0, 1):
        @pl.when(sends(side))
        def _():
            copy_edge(side, me).wait_send()
            for n in (0, 1):
                copy_u(side, n, me).wait_send()
                for k in range(3):
                    copy_v(k, side, n, me).wait_send()

        @pl.when(arrives(side))
        def _():
            swap(lch, side, my_rows).wait_send()
            forward(lch, side).wait_send()
    mean_sum.close()
    mom_sum.close()


def first_solve(slabs, lc, pt, u):
    depth, nx, cols = lc.shape
    plane = (nx + 2 * PAD, cols)
    half = nx // 2
    full = pl.BlockSpec(memory_space=VMEM)
    pair = (DMA((2,)), DMA((2,)))
    return pl.pallas_call(
        functools.partial(first_kernel, slabs),
        name="first_solve",
        out_shape=[
            jax.ShapeDtypeStruct((depth, nx, cols), F32),
            jax.ShapeDtypeStruct((8, 128), F32),
            *(
                jax.ShapeDtypeStruct((planes, half + PAD, cols), F32)
                for planes in (depth, 2, depth + 2, EARLY, depth + 2 - EARLY)
            ),
        ],
        in_specs=[pl.BlockSpec(memory_space=pltpu.HBM)] * 3,
        out_specs=[full] * 7,
        scratch_shapes=[VMEM((depth, nx, cols), F32)] * 2
        + [VMEM((2, nx, cols), F32)] * 2
        + [VMEM((depth + 2, *plane), F32)] * 3
        + [
            VMEM((depth, nx, cols), F32),
            VMEM((depth, nx, cols), F32),
            VMEM((depth, *plane), F32),
            VMEM((depth + 1, nx, cols), F32),
        ]
        + [VMEM((depth + 2, *plane), F32)] * 4
        + [VMEM((2, nx, cols), F32), VMEM((2, half, cols), F32), VMEM((4, half, cols), F32)]
        + [DMA((3,)), DMA((5,)), DMA((2, 2)), DMA((2, 2)), *pair, *pair, *pair]
        + [DMA((3, 2, 2)), DMA((3, 2, 2)), *pair, DMA((4,)), DMA((4,))]
        + sum_scratch(slabs, (1, 128)) * 2,
        compiler_params=pltpu.CompilerParams(
            collective_id=0, has_side_effects=True, vmem_limit_bytes=43 << 20
        ),
    )(lc, pt, u)


def search(keys, bound):
    size = keys.shape[0]

    def body(_, ends):
        low, high = ends
        mid = (low + high) // 2
        less = keys[jnp.minimum(mid, size - 1)] < bound
        open_ = low < high
        return (
            jnp.where(jnp.logical_and(open_, less), mid + 1, low),
            jnp.where(jnp.logical_and(open_, jnp.logical_not(less)), mid, high),
        )

    return lax.fori_loop(0, size.bit_length(), body, (jnp.int32(0), jnp.int32(size)))[0]


def bits(count):
    assert count & (count - 1) == 0
    return count.bit_length() - 1


def gather_kernel(group, depth, dipoles, keys, cells, field, out):
    me = lax.axis_index("slab")
    out[...] = jnp.zeros_like(out)
    lines, cols = field.shape
    nx = lines // depth
    entries = 2 * dipoles
    lane = lane_iota((1, cols))
    short = lane_iota((1, 128))
    start = search(keys, me * depth * entries)
    stop = search(keys, (me + 1) * depth * entries)
    base = me * lines

    def body(g, carry):
        parts = []
        least = start + g * group
        j = jnp.minimum(least, entries - group)
        for e in range(group):
            key, cell = keys[j + e], cells[j + e]
            o = key & (entries - 1)
            k = o & (dipoles - 1)
            line = ((key >> bits(entries)) << bits(nx)) + (cell >> bits(cols)) - base
            inside = jnp.logical_and(j + e >= least, j + e < stop)
            lane_at = jnp.where(inside, cell & (cols - 1), -1)
            picked = jnp.where(lane == lane_at, field[pl.ds(jnp.where(inside, line, 0), 1), :], 0.0)
            value = jnp.sum(picked, axis=1, keepdims=True)
            value = jnp.where(o < dipoles, value, -value)
            parts.append((k >> 7, jnp.where(short == (k & 127), value, 0.0)))
        for line, value in parts:
            out[pl.ds(line, 1), :] = out[pl.ds(line, 1), :] + value
        return carry

    lax.fori_loop(0, (stop - start + group - 1) // group, body, 0)


def gather(keys, cells, field, depth):
    smem = pl.BlockSpec(memory_space=SMEM)
    full = pl.BlockSpec(memory_space=VMEM)
    dipoles = keys.shape[0] // 2
    return pl.pallas_call(
        functools.partial(gather_kernel, 8, depth, dipoles),
        name="gather",
        out_shape=jax.ShapeDtypeStruct((dipoles // 128, 128), F32),
        in_specs=[smem, smem, full],
        out_specs=full,
        compiler_params=pltpu.CompilerParams(vmem_limit_bytes=8 << 20),
    )(keys, cells, field)


def share_kernel(slabs, part, out, s_x, r_x, *sums):
    src = lax.axis_index("src")
    me = lax.axis_index("slab")
    side_x = src // 2
    across = flip(src, 2)
    barrier, count = signal_all(src, me, slabs, [(across, me)])
    pl.semaphore_wait(barrier, count)
    total = Sum(src, me, slabs, sum_levels(sums))
    value = total.whole(part[...])
    lines = value.shape[0]
    out[side_x, pl.ds(0, lines), :] = value
    out[side_x, pl.ds(lines, lines), :] = -value
    copy = remote(out.at[side_x], out.at[side_x], s_x, r_x, (across, me))
    copy.start()
    copy.wait()
    total.close()


def share(slabs, part):
    full = pl.BlockSpec(memory_space=VMEM)
    lines = part.shape[0]
    return pl.pallas_call(
        functools.partial(share_kernel, slabs),
        name="share_data",
        out_shape=jax.ShapeDtypeStruct((2, 2 * lines, 128), F32),
        in_specs=[full],
        out_specs=full,
        scratch_shapes=[DMA(()), DMA(())] + sum_scratch(slabs, part.shape),
        compiler_params=pltpu.CompilerParams(
            collective_id=1, has_side_effects=True, vmem_limit_bytes=8 << 20
        ),
    )(part)


def scatter_kernel(group, depth, nx, lines, keys, cells, data, *outs):
    me = lax.axis_index("slab")
    side_x = lax.axis_index("src") // 2
    total, cols = outs[0].shape
    planes = total // lines
    entries = keys.shape[0]
    lane = lane_iota((1, cols))
    low = me * depth - WIDE
    start = search(keys, low * entries)
    stop = search(keys, (low + planes) * entries)
    row_base = (nx // 2) * side_x - 2 * PAD
    plane_base = low * lines + row_base

    def clear(q, carry):
        for out in outs:
            out[pl.ds(pl.multiple_of(q * lines, 8), lines), :] = jnp.zeros((lines, cols), F32)
        return carry

    lax.fori_loop(0, planes, clear, 0)

    def body(g, carry):
        parts = []
        least = start + g * group
        j = jnp.minimum(least, entries - group)
        for e in range(group):
            key, cell = keys[j + e], cells[j + e]
            o = key & (entries - 1)
            row = cell >> bits(cols)
            inside = jnp.logical_and(j + e >= least, j + e < stop)
            inside = jnp.logical_and(inside, jnp.logical_and(row >= row_base + PAD, row < row_base + lines - PAD))
            hit = lane == jnp.where(inside, cell & (cols - 1), -1)
            at = jnp.where(inside, (key >> bits(entries)) * lines + row - plane_base, 0)
            parts.append((at, [jnp.where(hit, data[o + n * entries], 0.0) for n in (0, 1)]))
        for at, values in parts:
            for out, value in zip(outs, values):
                out[pl.ds(at, 1), :] = out[pl.ds(at, 1), :] + value
        return carry

    lax.fori_loop(0, (stop - start + group - 1) // group, body, 0)


def scatter(keys, cells, data, depth, nx, cols):
    smem = pl.BlockSpec(memory_space=SMEM)
    full = pl.BlockSpec(memory_space=VMEM)
    lines = nx // 2 + 4 * PAD
    planes = depth + 2 * WIDE
    back = pl.pallas_call(
        functools.partial(scatter_kernel, 8, depth, nx, lines),
        name="scatter",
        out_shape=[jax.ShapeDtypeStruct((planes * lines, cols), F32)] * 2,
        in_specs=[smem, smem, smem],
        out_specs=[full, full],
        compiler_params=pltpu.CompilerParams(vmem_limit_bytes=8 << 20),
    )(keys, cells, data.reshape(-1))
    return [ref.reshape(planes, lines, cols) for ref in back]


def second_kernel(
    slabs, nx, lc_half, lc_near, u_mine, u_first, u_rest, mean_in, v00, v01, out,
    sig, dg, hx, hy, hz, v1, v2, v3, u2, adj, give, take, pair, far,
    s_load, s_u, r_u, s_far, r_far, s_c2, r_c2, s_give, r_give, s_x, r_x, s_own, r_own, s_fwd, r_fwd,
    *sums,
):
    src = lax.axis_index("src")
    me = lax.axis_index("slab")
    depth, _, cols = out.shape
    half = nx // 2
    frame = half + 2 * PAD
    frame_rows = half + PAD
    quarter = depth // 2
    core, side_x = lax.rem(src, 2), src // 2
    mate, across = flip(src, 1), flip(src, 2)
    wide = depth + 2 * WIDE
    ring = [(src, lax.rem(me + 1, slabs)), (src, lax.rem(me + slabs - 1, slabs))]
    barrier, count = signal_all(src, me, slabs, ring + [(mate, me)] + [(across, t) for t in pair_group(me)])
    total = Sum(src, me, slabs, sum_levels(sums), across)
    owned = chunks(half, PAD)
    rims = [(0, PAD), (PAD + half, PAD)]
    every = rims[:1] + owned + rims[1:]

    zero_pads(sig, frame)
    zero_pads(hy, frame)
    for ref in (v1, v2, v3):
        for j in (0, 1):
            zero_pads(ref.at[j], frame)

    outside = pl.ds(pl.multiple_of(PAD + (half + PAD) * side_x, PAD), PAD)
    u2[:, :, pl.ds(pl.multiple_of((half + PAD) * side_x, PAD), PAD), :] = jnp.zeros((2, depth + 2, PAD, cols), F32)
    frame_mine = pl.ds(pl.multiple_of(PAD * (1 - side_x), PAD), frame_rows)
    frame_theirs = pl.ds(pl.multiple_of(PAD * side_x, PAD), frame_rows)
    early = pl.ds(0, EARLY)
    late = pl.ds(EARLY, depth + 2 - EARLY)
    loads = [
        pltpu.make_async_copy(u_mine, u2.at[side_x, :, frame_mine], s_load.at[0]),
        pltpu.make_async_copy(u_first, u2.at[1 - side_x, early, frame_mine], s_load.at[1]),
    ]
    for load in loads:
        load.start()
    low_in, high_in = (me > 0).astype(F32), (me < slabs - 1).astype(F32)

    def conductivity(ref, count, first, factor=None):
        def body(n, carry):
            for r, rows in chunks(frame_rows):
                to = pl.multiple_of(PAD + PAD * (1 - side_x) + r, PAD)
                value = jnp.exp(ref[n, pl.ds(r, rows), :])
                sig[first + 1 + n, pl.ds(to, rows), :] = value if factor is None else factor * value
            sig[first + 1 + n, outside, :] = jnp.zeros((PAD, cols), F32)
            return carry

        lax.fori_loop(0, count, body, 0)

    conductivity(lc_half, depth, WIDE)
    conductivity(lc_near, 1, WIDE - 1, low_in)
    conductivity(lc_near.at[pl.ds(1, 1)], 1, WIDE + depth, high_in)

    arrives = (me > 0, me < slabs - 1)
    sends = (me < slabs - 1, me > 0)
    to_slab = (me + 1, me - 1)
    part = -(-frame_rows // (2 * PAD)) * PAD
    fetched = pl.ds(pl.multiple_of((frame_rows - part) * core, PAD), part)
    given = pl.ds(pl.multiple_of(part * core, PAD), frame_rows - part)
    taken = pl.ds(pl.multiple_of(part * (1 - core), PAD), frame_rows - part)

    def copy_far(side, to):
        planes = pl.ds(depth - WIDE if side == 0 else 1, WIDE - 1)
        return remote(lc_half.at[planes, fetched], far.at[side, :, fetched], s_far.at[side], r_far.at[side], (src, to))

    def share_far(side, rows):
        ref = far.at[side, :, rows]
        return remote(ref, ref, s_c2.at[side], r_c2.at[side], (mate, me))

    copy_rest = remote(u_rest, u2.at[side_x, late, frame_theirs], s_u, r_u, (across, me))
    pl.semaphore_wait(barrier, count)
    for side in (0, 1):
        pl.when(sends[side])(lambda side=side: copy_far(side, to_slab[side]).start())

    first, last = WIDE - me * depth, WIDE + (slabs - me) * depth - 1
    low_open, high_open = side_x.astype(F32), 1.0 - side_x.astype(F32)

    def coefs(start, stop, top=True):
        make_coefs(sig, dg, hx, hy, hz, start, stop, first, last, every, top)

        def close(q, carry):
            for line, factor in ((2 * PAD - 1, low_open), (2 * PAD + half - 1, high_open)):
                hy[q, pl.ds(line, 1), :] = hy[q, pl.ds(line, 1), :] * factor
            return carry

        lax.fori_loop(start, stop, close, 0)

    mean = mean_in[0:1, 0:1]
    scale = 6.0 * mean
    inv = 1.0 / scale
    zero = jnp.zeros((8, cols), F32)
    fields = [(v0, v1.at[j], v2.at[j], v3.at[j]) for j, v0 in enumerate((v00, v01))]
    sums_of = {}

    def run(k, start, stop, dotted):
        shift = THETA[k] * mean * inv
        for j in (0, 1):
            def step(q, accs, j=j):
                accs = list(accs)
                for r, rows in every:
                    here, image = operator(fields[j][k], q - k, dg, hx, hy, hz, q, r, rows)
                    new = inv * image - shift * here
                    fields[j][k + 1][q - k - 1, pl.ds(PAD + r, rows), :] = new
                    if not dotted or (r, rows) not in owned:
                        continue
                    if k == 0:
                        accs[0] = accs[0] + fold(here * here)
                    for i in range(k + 1):
                        other = here if i == k else fields[j][i][q - i, pl.ds(PAD + r, rows), :]
                        accs[i + (k == 0)] = accs[i + (k == 0)] + fold(new * other)
                    accs[-1] = accs[-1] + fold(new * new)
                return tuple(accs)

            accs = sums_of.get((j, k), (zero,) * (3 if k == 0 else k + 2)) if dotted else ()
            accs = lax.fori_loop(start, stop, step, accs)
            if dotted:
                sums_of[j, k] = accs

    top = WIDE + depth
    coefs(WIDE, top)
    run(0, WIDE, top, True)
    for side in (0, 1):
        @pl.when(arrives[side])
        def _():
            copy_far(side, me).wait_recv()
            share_far(side, given).start()

        @pl.when(jnp.logical_not(arrives[side]))
        def _():
            far[side] = jnp.zeros(far.shape[1:], F32)

    copy_rest.start()
    for k in (1, 2):
        run(k, WIDE + k, top - k, True)
    for side in (0, 1):
        pl.when(arrives[side])(lambda side=side: share_far(side, taken).wait_recv())
    conductivity(far.at[0], WIDE - 1, 0, low_in)
    conductivity(far.at[1], WIDE - 1, top + 1, high_in)
    coefs(1, WIDE, False)
    coefs(top, wide - 1)
    for k in range(3):
        run(k, k + 1, WIDE, False)
        if k:
            run(k, WIDE, WIDE + k, True)
            run(k, top - k, top, True)
        run(k, top, wide - k - 1, False)
    dots = [[acc for k in range(3) for acc in sums_of[j, k]] for j in (0, 1)]

    for j in (0, 1):
        def energy(q, acc, j=j):
            for r, rows in owned:
                here, image = operator(v3.at[j], q + 1, dg, hx, hy, hz, q + WIDE, r, rows)
                acc = acc + fold(here * image)
            return acc

        dots[j].append(lax.fori_loop(0, depth, energy, zero))

    row = total.whole(pack_row(dots[0] + dots[1]))
    thetas = [t * mean for t in THETA]
    coef = [solve_small(row, scale, thetas, n) for n in (0, len(dots[0]))]

    def combine(q, carry):
        for j in (0, 1):
            c = coef[j]
            for r, rows in every:
                value = c[3] * v3[j, q, pl.ds(PAD + r, rows), :]
                for i, ref in enumerate(fields[j][:3]):
                    value = value + c[i] * ref[q + 3 - i, pl.ds(PAD + r, rows), :]
                adj[j, q, pl.ds(r, rows), :] = value
        return carry

    lax.fori_loop(0, depth + 2, combine, 0)
    for load in loads:
        load.wait()
    copy_rest.wait()
    for side in (0, 1):
        pl.when(sends[side])(lambda side=side: copy_far(side, me).wait_send())
        pl.when(arrives[side])(lambda side=side: share_far(side, given).wait_send())

    def partial(q, dst, slot):
        for r, rows in owned:
            total = jnp.zeros((rows, cols), F32)
            for j in (0, 1):
                f = u2[j, q + 1, pl.ds(r, rows), :]
                a = adj[j, q + 1, pl.ds(r, rows), :]
                lane = lane_iota(f.shape)
                fr = jnp.where(lane == cols - 1, 0.0, next_lane(f))
                ar = jnp.where(lane == cols - 1, 0.0, next_lane(a))
                flow = (f - fr) * (a - ar)
                total = total + (flow + jnp.where(lane == 0, f * a, prev_lane(flow)))
                for dq, dr in ((0, 1), (0, -1), (1, 0), (-1, 0)):
                    fj = u2[j, q + 1 + dq, pl.ds(r + dr, rows), :]
                    aj = adj[j, q + 1 + dq, pl.ds(r + dr, rows), :]
                    total = total + (f - fj) * (a - aj)
            scaled = -0.5 * sig[q + WIDE + 1, pl.ds(PAD + r, rows), :] * total
            dst[slot, pl.ds(r - PAD, rows), :] = scaled

    def copy_give(n):
        return remote(give.at[n], take.at[n], s_give.at[n], r_give.at[n], (mate, me))

    rows_mine = pl.ds(pl.multiple_of(half * side_x, PAD), half)
    rows_theirs = pl.ds(pl.multiple_of(half * (1 - side_x), PAD), half)

    def copy_x(n):
        ref = out.at[core * quarter + n, rows_mine]
        return remote(ref, ref, s_x.at[n], r_x.at[n], (across, me))

    def copy_own(n):
        ref = out.at[core * quarter + n, rows_mine]
        return remote(ref, ref, s_own.at[n], r_own.at[n], (mate, me))

    def copy_fwd(n):
        ref = out.at[core * quarter + n, rows_theirs]
        return remote(ref, ref, s_fwd.at[n], r_fwd.at[n], (mate, me))

    def giving(n, carry):
        partial((1 - core) * quarter + n, give, n)
        copy_give(n).start()
        return carry

    def keeping(n, carry):
        partial(core * quarter + n, pair, n)
        copy_give(n).wait_recv()
        for r, rows in chunks(half):
            at = pl.multiple_of(half * side_x + r, PAD)
            out[core * quarter + n, pl.ds(at, rows), :] = pair[n, pl.ds(r, rows), :] + take[n, pl.ds(r, rows), :]
        copy_x(n).start()
        copy_own(n).start()
        return carry

    def passing(n, carry):
        copy_x(n).wait_recv()
        copy_fwd(n).start()
        return carry

    def ending(n, carry):
        copy_own(n).wait_recv()
        copy_fwd(n).wait_recv()
        for copy in (copy_give, copy_x, copy_own, copy_fwd):
            copy(n).wait_send()
        return carry

    for body in (giving, keeping, passing, ending):
        lax.fori_loop(0, quarter, body, 0)
    total.close()


def second_solve(slabs, nx, lc_half, lc_near, u_mine, u_first, u_rest, mean, back):
    depth, _, cols = lc_half.shape
    half = nx // 2
    frame = half + 2 * PAD
    plane = (frame + 2 * PAD, cols)
    wide = depth + 2 * WIDE
    quarter = depth // 2
    full = pl.BlockSpec(memory_space=VMEM)
    anywhere = pl.BlockSpec(memory_space=pl.ANY)
    pair = [DMA((2,)), DMA((2,))]
    return pl.pallas_call(
        functools.partial(second_kernel, slabs, nx),
        name="second_solve",
        out_shape=jax.ShapeDtypeStruct((depth, nx, cols), F32),
        in_specs=[full, full, anywhere, anywhere, anywhere, full, full, full],
        out_specs=full,
        scratch_shapes=[
            VMEM((wide + 2, *plane), F32),
            VMEM((wide, frame, cols), F32),
            VMEM((wide, frame, cols), F32),
            VMEM((wide, *plane), F32),
            VMEM((wide + 1, frame, cols), F32),
            VMEM((2, wide - 2, *plane), F32),
            VMEM((2, wide - 4, *plane), F32),
            VMEM((2, wide - 6, *plane), F32),
            VMEM((2, depth + 2, frame, cols), F32),
            VMEM((2, depth + 2, frame, cols), F32),
        ]
        + [VMEM((quarter, half, cols), F32)] * 3
        + [VMEM((2, WIDE - 1, half + PAD, cols), F32)]
        + [DMA((2,)), DMA(()), DMA(())]
        + pair * 2
        + [DMA((quarter,))] * 8
        + sum_scratch(slabs, (1, 128), 8),
        compiler_params=pltpu.CompilerParams(
            collective_id=2, has_side_effects=True, vmem_limit_bytes=42 << 20
        ),
    )(lc_half, lc_near, u_mine, u_first, u_rest, mean, *back)


def shards(slabs, log_cond, perturb, potentials, rec_depth, rec_plan):
    depth, nx, cols = log_cond.shape
    dipoles = rec_depth.shape[1]
    order = lax.broadcasted_iota(jnp.int32, rec_depth.shape, 0) * dipoles
    order = order + lax.broadcasted_iota(jnp.int32, rec_depth.shape, 1)
    keys = (rec_depth * (2 * dipoles) + order).reshape(-1)
    keys, cells = lax.sort((keys, rec_plan.reshape(-1)), num_keys=1, is_stable=False)
    arguments = (pltpu.with_memory_space_constraint(a, pltpu.HBM) for a in (log_cond, perturb, potentials[0]))
    tangent, mean, lc_half, lc_near, u_mine, u_first, u_rest = first_solve(slabs, *arguments)
    part = gather(keys, cells, tangent.reshape(depth * nx, cols), depth)
    data = share(slabs, part)
    u_first, data = lax.optimization_barrier((u_first, data))
    u_first = lax.ppermute(u_first, "src", [(i, (i + 2) % 4) for i in range(4)])
    back = scatter(keys, cells, data, depth, nx, cols)
    return second_solve(slabs, nx, lc_half, lc_near, u_mine, u_first, u_rest, mean, back)


def solution(mesh):
    in_specs = (
        P("slab", None, None),
        P("slab", None, None),
        P("src", "slab", None, None),
        P(),
        P(),
    )
    return jax.shard_map(
        functools.partial(shards, mesh.shape["slab"]),
        mesh=mesh,
        in_specs=in_specs,
        out_specs=P("slab", None, None),
        check_vma=False,
    )
```

```python
import functools

import jax
import jax.numpy as jnp
from jax import lax
from jax.experimental import pallas as pl
from jax.experimental.pallas import tpu as pltpu
from jax.sharding import PartitionSpec as P

MESH = pl.DeviceIdType.MESH
F32 = jnp.float32
VMEM = pltpu.VMEM
SMEM = pltpu.SMEM
DMA = pltpu.SemaphoreType.DMA
PAD = 8
WIDE = 4
EARLY = 4
ROWS = 64
THETA = (6.0, 2.0, 10.0)


def lane_iota(shape):
    return lax.broadcasted_iota(jnp.int32, shape, len(shape) - 1)


def fold(value):
    rows, cols = value.shape
    return jnp.sum(value.reshape(rows // 8, 8, cols), axis=0)


def next_lane(value):
    half = value.shape[1] // 2
    even, odd = value[:, :half], value[:, half:]
    return jnp.concatenate([odd, pltpu.roll(even, half - 1, 1)], axis=1)


def prev_lane(value):
    half = value.shape[1] // 2
    even, odd = value[:, :half], value[:, half:]
    return jnp.concatenate([pltpu.roll(odd, 1, 1), even], axis=1)


def lane_of(column, cols):
    return (column >> 1) + (column & 1) * (cols // 2)


def order_matrix(cols, back):
    row = lax.broadcasted_iota(jnp.int32, (cols, cols), 0)
    col = lax.broadcasted_iota(jnp.int32, (cols, cols), 1)
    hit = row == lane_of(col, cols) if back else col == lane_of(row, cols)
    return jnp.where(hit, 1.0, 0.0).astype(jnp.bfloat16)


def reorder(value, matrix):
    total = None
    for _ in range(3):
        piece = value.astype(jnp.bfloat16)
        value = value - piece.astype(F32)
        moved = jnp.dot(piece, matrix, preferred_element_type=F32)
        total = moved if total is None else total + moved
    return total


def chunks(count, start=0):
    out = []
    done = 0
    while done < count:
        rows = min(ROWS, count - done)
        out.append((start + done, rows))
        done += rows
    return out


def make_coefs(sig, dg, hx, hy, hz, start, stop, first, last, pieces, top=True):
    cols = sig.shape[-1]

    def body(q, carry):
        low_in = jnp.logical_and(q - 1 >= first, q <= last).astype(F32)
        for r, rows in pieces:
            here = sig[q + 1, pl.ds(PAD + r, rows), :]
            up = sig[q + 1, pl.ds(PAD + r + 1, rows), :]
            down = sig[q + 1, pl.ds(PAD + r - 1, rows), :]
            low = sig[q, pl.ds(PAD + r, rows), :]
            high = sig[q + 2, pl.ds(PAD + r, rows), :]
            lane = lane_iota(here.shape)
            right = jnp.where(lane == cols - 1, 0.0, next_lane(here))
            left = jnp.where(lane == 0, 0.0, prev_lane(here))
            hx[q, pl.ds(r, rows), :] = jnp.where(lane == cols - 1, 0.0, 0.5 * (here + right))
            hy[q, pl.ds(PAD + r, rows), :] = 0.5 * (here + up)
            hz[q, pl.ds(r, rows), :] = (0.5 * low_in) * (here + low)
            total = ((up + down) + (left + right)) + (low + high)
            dg[q, pl.ds(r, rows), :] = 3.0 * here + 0.5 * total
        return carry

    lax.fori_loop(start, stop, body, 0)
    if not top:
        return
    inside = jnp.logical_and(stop - 1 >= first, stop <= last).astype(F32)
    for r, rows in pieces:
        here = sig[stop + 1, pl.ds(PAD + r, rows), :]
        low = sig[stop, pl.ds(PAD + r, rows), :]
        hz[stop, pl.ds(r, rows), :] = (0.5 * inside) * (here + low)


def operator(v, p, dg, hx, hy, hz, q, r, rows):
    here = v[p, pl.ds(PAD + r, rows), :]
    wx = hx[q, pl.ds(r, rows), :]
    acc = dg[q, pl.ds(r, rows), :] * here
    acc = acc - wx * next_lane(here)
    acc = acc - prev_lane(wx * here)
    acc = acc - hy[q, pl.ds(PAD + r, rows), :] * v[p, pl.ds(PAD + r + 1, rows), :]
    acc = acc - hy[q, pl.ds(PAD + r - 1, rows), :] * v[p, pl.ds(PAD + r - 1, rows), :]
    acc = acc - hz[q, pl.ds(r, rows), :] * v[p - 1, pl.ds(PAD + r, rows), :]
    acc = acc - hz[q + 1, pl.ds(r, rows), :] * v[p + 1, pl.ds(PAD + r, rows), :]
    return here, acc


def zero_pads(ref, nx):
    zero = jnp.zeros((ref.shape[0], PAD, ref.shape[2]), F32)
    ref[:, pl.ds(0, PAD), :] = zero
    ref[:, pl.ds(PAD + nx, PAD), :] = zero


def splat(row, index):
    return jnp.sum(jnp.where(lane_iota(row.shape) == index, row, 0.0), axis=1, keepdims=True)


def solve_small(row, scale, thetas, n=0):
    gram = {}
    for i in range(4):
        for j in range(i + 1):
            gram[i, j] = gram[j, i] = splat(row, n)
            n += 1
    last = splat(row, n)
    mat = {}
    for i in range(4):
        for j in range(i + 1):
            if j == 3:
                mat[i, j] = last
            else:
                mat[i, j] = scale * gram[i, j + 1] + thetas[j] * gram[i, j]
    low, inv = {}, {}
    for j in range(4):
        pivot = mat[j, j]
        for k in range(j):
            pivot = pivot - low[j, k] * low[j, k] * mat["d", k]
        mat["d", j] = pivot
        good = pivot > 1e-7 * mat[j, j]
        inv[j] = jnp.where(good, 1.0 / jnp.where(good, pivot, 1.0), 0.0)
        for i in range(j + 1, 4):
            value = mat[i, j]
            for k in range(j):
                value = value - low[i, k] * low[j, k] * mat["d", k]
            low[i, j] = value * inv[j]
    y = []
    for i in range(4):
        value = gram[i, 0]
        for k in range(i):
            value = value - low[i, k] * y[k]
        y.append(value)
    c = [None] * 4
    for i in reversed(range(4)):
        value = y[i] * inv[i]
        for k in range(i + 1, 4):
            value = value - low[k, i] * c[k]
        c[i] = value
    return c


def pack_row(accs):
    lane = lane_iota((1, 128))
    row = jnp.zeros((1, 128), F32)
    for n, acc in enumerate(accs):
        total = jnp.sum(jnp.sum(acc, axis=0, keepdims=True), axis=1, keepdims=True)
        row = row + jnp.where(lane == n, total, 0.0)
    return row


def remote(src_ref, dst_ref, send_sem, recv_sem, target):
    return pltpu.make_async_remote_copy(
        src_ref=src_ref,
        dst_ref=dst_ref,
        send_sem=send_sem,
        recv_sem=recv_sem,
        device_id=target,
        device_id_type=MESH,
    )


def flip(src, bit):
    return src + bit - 2 * bit * (lax.rem(src // bit, 2))


def partners(me, slabs):
    near = 4
    fours = slabs // near
    place, four = lax.rem(me, near), me // near
    return (
        [four * near + lax.rem(place + d, near) for d in range(1, near)],
        [lax.rem(four + d, fours) * near + place for d in range(1, fours)],
    )


def pair_group(me):
    place = lax.rem(me, 4)
    return [me - place + lax.rem(place + d, 4) for d in range(4)]


def signal_all(src, me, slabs, others):
    barrier = pltpu.get_barrier_semaphore()
    targets = [(src, t) for group in partners(me, slabs) for t in group] + others
    for target in targets:
        pl.semaphore_signal(barrier, inc=1, device_id=target, device_id_type=MESH)
    return barrier, len(targets)


class Sum:
    def __init__(self, src, me, slabs, levels, across=None):
        groups = [[(src, t) for t in group] for group in partners(me, slabs)]
        if across is not None:
            groups[0] += [(across, t) for t in pair_group(me)]
        self.levels = [(level, group) for level, group in zip(levels, groups) if group]

    def send(self, n, value):
        (buf, send_sem, recv_sem), group = self.levels[n]
        buf[0] = value
        for d, target in enumerate(group):
            remote(buf.at[0], buf.at[d + 1], send_sem, recv_sem, target).start()

    def _wait(self, n, which):
        level, group = self.levels[n]
        rest = level[0].at[pl.ds(1, len(group))]
        pltpu.make_async_copy(rest, rest, level[which]).wait()

    def receive(self, n):
        self._wait(n, 2)
        return jnp.sum(self.levels[n][0][0][...], axis=0)

    def start(self, value):
        self.send(0, value)

    def middle(self):
        value = self.receive(0)
        if len(self.levels) > 1:
            self.send(1, value)
        return value

    def end(self, value):
        return self.receive(1) if len(self.levels) > 1 else value

    def whole(self, value):
        self.start(value)
        return self.end(self.middle())

    def close(self):
        for n in range(len(self.levels)):
            self._wait(n, 1)


def sum_scratch(slabs, shape, first=4):
    return [
        VMEM((first, *shape), F32), DMA(()), DMA(()),
        VMEM((max(slabs // 4, 2), *shape), F32), DMA(()), DMA(()),
    ]


def sum_levels(refs):
    return (refs[0:3], refs[3:6])


def first_kernel(
    slabs, lc_in, pt_in, u, tan, mean_out, lc_half, lc_near, u_mine, u_first, u_rest,
    lc, pt, lch, uh, sig, wgt, uw, dg, hx, hy, hz, v0, v1, v2, v3, pth, edge, order,
    s_load, s_take, s_first, r_first, s_c, r_c, s_x, r_x, s_core, r_core, s_v, r_v, s_e, r_e, *sums,
):
    src = lax.axis_index("src")
    me = lax.axis_index("slab")
    depth, nx, cols = lc.shape
    half = nx // 2
    has_low = me > 0
    has_high = me < slabs - 1
    core, side_x = lax.rem(src, 2), src // 2
    mate, across = flip(src, 1), flip(src, 2)
    inner_rows = pl.ds(PAD, nx)
    loads = [
        pltpu.make_async_copy(u, uw.at[pl.ds(1, depth), inner_rows], s_load.at[0]),
        pltpu.make_async_copy(lc_in, lc, s_load.at[1]),
        pltpu.make_async_copy(pt_in, pt, s_load.at[2]),
    ]
    for load in loads:
        load.start()
    ring = [(src, lax.rem(me + 1, slabs)), (src, lax.rem(me + slabs - 1, slabs))]
    barrier, count = signal_all(src, me, slabs, ring + [(mate, me), (across, me)])
    order[...] = order_matrix(cols, False)

    def shuffle(q, carry):
        for n in (0, 1):
            for ref, plane, first in ((lc, q, 0), (pt, q, 0), (uw, q + 1, PAD)):
                rows = pl.ds(first + n * half, half)
                ref[plane, rows, :] = reorder(ref[plane, rows, :], order[...])
        return carry

    for load in loads:
        load.wait()
    lax.fori_loop(0, 2, lambda i, c: shuffle(i * (depth - 1), c), 0)
    pl.semaphore_wait(barrier, count)
    mean_sum = Sum(src, me, slabs, sum_levels(sums[0:6]))
    mom_sum = Sum(src, me, slabs, sum_levels(sums[6:12]))

    def arrives(side):
        return has_low if side == 0 else has_high

    def below(side):
        return me + 1 if side == 0 else me - 1

    def sends(side):
        return has_high if side == 0 else has_low

    def near(side):
        return depth - 1 if side == 0 else 0

    def part(n):
        return pl.ds(n * half, half)

    def copy_u(side, n, to):
        return remote(
            uw.at[1 + near(side), pl.ds(PAD + n * half, half)], uh.at[side, part(n)],
            s_first.at[side, n], r_first.at[side, n], (src, to),
        )

    my_rows = pl.ds(pl.multiple_of(half * side_x, PAD), half)
    their_rows = pl.ds(pl.multiple_of(half * (1 - side_x), PAD), half)

    def copy_c(ref, dst, side, to):
        return remote(
            ref.at[near(side), my_rows], dst.at[side, my_rows], s_c.at[side], r_c.at[side], (src, to)
        )

    def swap(ref, side, rows):
        return remote(ref.at[side, rows], ref.at[side, rows], s_x.at[side], r_x.at[side], (across, me))

    def forward(ref, side):
        return remote(ref.at[side], ref.at[side], s_core.at[side], r_core.at[side], (mate, me))

    def by_core(body):
        pl.when(core == 0)(lambda: body(lc, lch))
        pl.when(core == 1)(lambda: body(pt, pth))

    for side in (0, 1):
        @pl.when(sends(side))
        def _():
            by_core(lambda ref, dst: copy_c(ref, dst, side, below(side)).start())

    for ref in (sig, wgt, uw, hy, v0, v1, v2, v3):
        zero_pads(ref, nx)
    for side in (0, 1):
        @pl.when(sends(side))
        def _():
            copy_c(lc, lch, side, me).wait_send()

    for n in (0, 1):
        for side in (0, 1):
            pl.when(sends(side))(lambda side=side, n=n: copy_u(side, n, below(side)).start())

    def own(q, acc):
        for r, rows in chunks(nx):
            value = jnp.exp(lc[q, pl.ds(r, rows), :])
            sig[q + 1, pl.ds(PAD + r, rows), :] = value
            wgt[q + 1, pl.ds(PAD + r, rows), :] = value * pt[q, pl.ds(r, rows), :]
            acc = acc + fold(value)
        return acc

    lax.fori_loop(1, depth - 1, shuffle, 0)
    acc = lax.fori_loop(0, depth, own, jnp.zeros((8, cols), F32))
    mean_sum.start(pack_row([acc]))

    fields = (v0, v1, v2, v3)
    for ref in fields:
        for side in (0, 1):
            def clear(ref=ref, side=side):
                ref[side * (depth + 1), pl.ds(PAD, nx), :] = jnp.zeros((nx, cols), F32)

            if ref is v3:
                clear()
            else:
                pl.when(jnp.logical_not(arrives(side)))(clear)
    mean_part = mean_sum.middle()

    for side in (0, 1):
        @pl.when(arrives(side))
        def _():
            def body(ref, dst):
                copy_c(ref, dst, side, me).wait_recv()
                swap(dst, side, my_rows).start()

            by_core(body)
    for side in (0, 1):
        @pl.when(arrives(side))
        def _():
            def body(ref, dst):
                swap(dst, side, their_rows).wait_recv()
                forward(dst, side).start()

            by_core(body)

    def rhs_rows(q, pieces):
        for r, rows in pieces:
            c = wgt[q + 1, pl.ds(PAD + r, rows), :]
            f = uw[q + 1, pl.ds(PAD + r, rows), :]
            lane = lane_iota(c.shape)
            cr = jnp.where(lane == cols - 1, 0.0, next_lane(c))
            fr = jnp.where(lane == cols - 1, 0.0, next_lane(f))
            flow = (c + cr) * (f - fr)
            total = flow + jnp.where(lane == 0, c * f, -prev_lane(flow))
            for dq, dr in ((0, 1), (0, -1), (1, 0), (-1, 0)):
                cj = wgt[q + 1 + dq, pl.ds(PAD + r + dr, rows), :]
                fj = uw[q + 1 + dq, pl.ds(PAD + r + dr, rows), :]
                total = total + (c + cj) * (f - fj)
            v0[q + 1, pl.ds(PAD + r, rows), :] = -0.5 * total

    def copy_v(k, side, n, to):
        plane = depth if side == 0 else 1
        halo = 0 if side == 0 else depth + 1
        rows = pl.ds(PAD + n * half, half)
        ref = fields[k]
        return remote(
            ref.at[plane, rows], ref.at[halo, rows], s_v.at[k, side, n], r_v.at[k, side, n], (src, to)
        )

    def send_edge(k, side, n):
        out = 1 - side

        @pl.when(sends(out))
        def _():
            copy_v(k, out, n, below(out)).start()

    for n in (0, 1):
        for side in (0, 1):
            plane = 0 if side == 0 else depth + 1

            @pl.when(arrives(side))
            def _():
                if n == 0:
                    pl.when(core == 0)(lambda: forward(pth, side).wait_recv())
                    pl.when(core == 1)(lambda: forward(lch, side).wait_recv())
                copy_u(side, n, me).wait_recv()
                for r, rows in chunks(half, n * half):
                    value = jnp.exp(lch[side, pl.ds(r, rows), :])
                    sig[plane, pl.ds(PAD + r, rows), :] = value
                    wgt[plane, pl.ds(PAD + r, rows), :] = value * pth[side, pl.ds(r, rows), :]
                    uw[plane, pl.ds(PAD + r, rows), :] = uh[side, pl.ds(r, rows), :]

            @pl.when(jnp.logical_not(arrives(side)))
            def _():
                for ref in (sig, wgt, uw):
                    ref[plane, pl.ds(PAD + n * half, half), :] = jnp.zeros((half, cols), F32)
                lch[side, part(n), :] = jnp.zeros((half, cols), F32)

            rhs_rows(0 if side == 0 else depth - 1, chunks(half, n * half))
            send_edge(0, side, n)

    frame_rows = half + PAD
    mine = half * side_x - PAD * side_x
    theirs = (half - PAD) - mine
    takes = []
    for n, (ref, dst, first, at) in enumerate((
        (lc, lc_half, 0, mine),
        (lch, lc_near, 0, mine),
        (uw, u_mine, 0, PAD + mine),
        (uw, u_first, 0, PAD + theirs),
        (uw, u_rest, EARLY, PAD + theirs),
    )):
        rows = pl.ds(pl.multiple_of(at, PAD), frame_rows)
        takes.append(pltpu.make_async_copy(ref.at[pl.ds(first, dst.shape[0]), rows], dst, s_take.at[n]))
    for take in takes:
        take.start()

    def inner(body, carry):
        return lax.fori_loop(1, depth - 1, body, carry)

    def rhs_plane(q, carry):
        rhs_rows(q, chunks(nx))
        return carry

    inner(rhs_plane, 0)
    first, last = -me * depth, (slabs - me) * depth - 1
    make_coefs(sig, dg, hx, hy, hz, 0, depth, first, last, chunks(nx))

    mean = splat(mean_sum.end(mean_part), 0) * (1.0 / (slabs * depth * nx * cols))
    mean_out[...] = jnp.broadcast_to(mean, (8, 128))
    scale = 6.0 * mean
    inv = 1.0 / scale

    zero = jnp.zeros((8, cols), F32)
    dots = []
    for k in range(3):
        shift = THETA[k] * mean * inv

        def step(q, accs, pieces=None, k=k, shift=shift):
            accs = list(accs)
            for r, rows in pieces or chunks(nx):
                here, image = operator(fields[k], q + 1, dg, hx, hy, hz, q, r, rows)
                new = inv * image - shift * here
                fields[k + 1][q + 1, pl.ds(PAD + r, rows), :] = new
                if k == 0:
                    accs[0] = accs[0] + fold(here * here)
                for i in range(k + 1):
                    other = here if i == k else fields[i][q + 1, pl.ds(PAD + r, rows), :]
                    accs[i + (k == 0)] = accs[i + (k == 0)] + fold(new * other)
                accs[-1] = accs[-1] + fold(new * new)
            return tuple(accs)

        accs = inner(step, (zero,) * (3 if k == 0 else k + 2))
        for n in (0, 1):
            for side in (0, 1):
                pl.when(arrives(side))(lambda side=side, n=n, k=k: copy_v(k, side, n, me).wait_recv())
                accs = step(0 if side == 0 else depth - 1, accs, chunks(half, n * half))
                if k < 2:
                    send_edge(k + 1, side, n)
        dots.extend(accs)

    def copy_edge(side, to):
        plane = depth if side == 0 else 1
        return remote(
            v3.at[plane, pl.ds(PAD + side * half, half)], edge.at[side], s_e.at[side], r_e.at[side], (src, to)
        )

    for side in (0, 1):
        pl.when(sends(side))(lambda side=side: copy_edge(side, below(side)).start())
    def energy(q, acc):
        for r, rows in chunks(nx):
            here, image = operator(v3, q + 1, dg, hx, hy, hz, q, r, rows)
            acc = acc + fold(here * image)
        return acc

    acc = lax.fori_loop(0, depth, energy, zero)
    for side in (0, 1):
        got = arrives(side)
        pl.when(got)(lambda side=side: copy_edge(side, me).wait_recv())

        @pl.when(jnp.logical_not(got))
        def _():
            edge[side] = jnp.zeros((half, cols), F32)

        for r, rows in chunks(half):
            at = side * half + r
            face = hz[side * depth, pl.ds(at, rows), :] * v3[1 + side * (depth - 1), pl.ds(PAD + at, rows), :]
            acc = acc - 2.0 * fold(face * edge[side, pl.ds(r, rows), :])
    dots.append(acc)
    mom_sum.start(pack_row(dots))
    value = mom_sum.middle()

    row = mom_sum.end(value)
    c = solve_small(row, scale, [t * mean for t in THETA])

    def combine(q, carry):
        for r, rows in chunks(nx):
            value = c[0] * v0[q + 1, pl.ds(PAD + r, rows), :]
            for i in (1, 2, 3):
                value = value + c[i] * fields[i][q + 1, pl.ds(PAD + r, rows), :]
            tan[q, pl.ds(r, rows), :] = value
        return carry

    lax.fori_loop(0, depth, combine, 0)

    for take in takes:
        take.wait()
    for side in (0, 1):
        @pl.when(sends(side))
        def _():
            copy_edge(side, me).wait_send()
            for n in (0, 1):
                copy_u(side, n, me).wait_send()
                for k in range(3):
                    copy_v(k, side, n, me).wait_send()

        @pl.when(arrives(side))
        def _():
            swap(lch, side, my_rows).wait_send()
            forward(lch, side).wait_send()
    mean_sum.close()
    mom_sum.close()


def first_solve(slabs, lc, pt, u):
    depth, nx, cols = lc.shape
    plane = (nx + 2 * PAD, cols)
    half = nx // 2
    full = pl.BlockSpec(memory_space=VMEM)
    pair = (DMA((2,)), DMA((2,)))
    return pl.pallas_call(
        functools.partial(first_kernel, slabs),
        name="first_solve",
        out_shape=[
            jax.ShapeDtypeStruct((depth, nx, cols), F32),
            jax.ShapeDtypeStruct((8, 128), F32),
            *(
                jax.ShapeDtypeStruct((planes, half + PAD, cols), F32)
                for planes in (depth, 2, depth + 2, EARLY, depth + 2 - EARLY)
            ),
        ],
        in_specs=[pl.BlockSpec(memory_space=pltpu.HBM)] * 3,
        out_specs=[full] * 7,
        scratch_shapes=[VMEM((depth, nx, cols), F32)] * 2
        + [VMEM((2, nx, cols), F32)] * 2
        + [VMEM((depth + 2, *plane), F32)] * 3
        + [
            VMEM((depth, nx, cols), F32),
            VMEM((depth, nx, cols), F32),
            VMEM((depth, *plane), F32),
            VMEM((depth + 1, nx, cols), F32),
        ]
        + [VMEM((depth + 2, *plane), F32)] * 4
        + [VMEM((2, nx, cols), F32), VMEM((2, half, cols), F32), VMEM((cols, cols), jnp.bfloat16)]
        + [DMA((3,)), DMA((5,)), DMA((2, 2)), DMA((2, 2)), *pair, *pair, *pair]
        + [DMA((3, 2, 2)), DMA((3, 2, 2)), *pair]
        + sum_scratch(slabs, (1, 128)) * 2,
        compiler_params=pltpu.CompilerParams(
            collective_id=0, has_side_effects=True, vmem_limit_bytes=43 << 20
        ),
    )(lc, pt, u)


def search(keys, bound):
    size = keys.shape[0]

    def body(_, ends):
        low, high = ends
        mid = (low + high) // 2
        less = keys[jnp.minimum(mid, size - 1)] < bound
        open_ = low < high
        return (
            jnp.where(jnp.logical_and(open_, less), mid + 1, low),
            jnp.where(jnp.logical_and(open_, jnp.logical_not(less)), mid, high),
        )

    return lax.fori_loop(0, size.bit_length(), body, (jnp.int32(0), jnp.int32(size)))[0]


def bits(count):
    assert count & (count - 1) == 0
    return count.bit_length() - 1


def gather_kernel(group, depth, dipoles, keys, cells, field, out):
    me = lax.axis_index("slab")
    out[...] = jnp.zeros_like(out)
    lines, cols = field.shape
    nx = lines // depth
    entries = 2 * dipoles
    lane = lane_iota((1, cols))
    short = lane_iota((1, 128))
    start = search(keys, me * depth * entries)
    stop = search(keys, (me + 1) * depth * entries)
    base = me * lines

    def body(g, carry):
        parts = []
        least = start + g * group
        j = jnp.minimum(least, entries - group)
        for e in range(group):
            key, cell = keys[j + e], cells[j + e]
            o = key & (entries - 1)
            k = o & (dipoles - 1)
            line = ((key >> bits(entries)) << bits(nx)) + (cell >> bits(cols)) - base
            inside = jnp.logical_and(j + e >= least, j + e < stop)
            lane_at = jnp.where(inside, lane_of(cell & (cols - 1), cols), -1)
            picked = jnp.where(lane == lane_at, field[pl.ds(jnp.where(inside, line, 0), 1), :], 0.0)
            value = jnp.sum(picked, axis=1, keepdims=True)
            value = jnp.where(o < dipoles, value, -value)
            parts.append((k >> 7, jnp.where(short == (k & 127), value, 0.0)))
        for line, value in parts:
            out[pl.ds(line, 1), :] = out[pl.ds(line, 1), :] + value
        return carry

    lax.fori_loop(0, (stop - start + group - 1) // group, body, 0)


def gather(keys, cells, field, depth):
    smem = pl.BlockSpec(memory_space=SMEM)
    full = pl.BlockSpec(memory_space=VMEM)
    dipoles = keys.shape[0] // 2
    return pl.pallas_call(
        functools.partial(gather_kernel, 8, depth, dipoles),
        name="gather",
        out_shape=jax.ShapeDtypeStruct((dipoles // 128, 128), F32),
        in_specs=[smem, smem, full],
        out_specs=full,
        compiler_params=pltpu.CompilerParams(vmem_limit_bytes=8 << 20),
    )(keys, cells, field)


def share_kernel(slabs, part, out, s_x, r_x, *sums):
    src = lax.axis_index("src")
    me = lax.axis_index("slab")
    side_x = src // 2
    across = flip(src, 2)
    barrier, count = signal_all(src, me, slabs, [(across, me)])
    pl.semaphore_wait(barrier, count)
    total = Sum(src, me, slabs, sum_levels(sums))
    value = total.whole(part[...])
    lines = value.shape[0]
    out[side_x, pl.ds(0, lines), :] = value
    out[side_x, pl.ds(lines, lines), :] = -value
    copy = remote(out.at[side_x], out.at[side_x], s_x, r_x, (across, me))
    copy.start()
    copy.wait()
    total.close()


def share(slabs, part):
    full = pl.BlockSpec(memory_space=VMEM)
    lines = part.shape[0]
    return pl.pallas_call(
        functools.partial(share_kernel, slabs),
        name="share_data",
        out_shape=jax.ShapeDtypeStruct((2, 2 * lines, 128), F32),
        in_specs=[full],
        out_specs=full,
        scratch_shapes=[DMA(()), DMA(())] + sum_scratch(slabs, part.shape),
        compiler_params=pltpu.CompilerParams(
            collective_id=1, has_side_effects=True, vmem_limit_bytes=8 << 20
        ),
    )(part)


def scatter_kernel(group, depth, nx, lines, keys, cells, data, *outs):
    me = lax.axis_index("slab")
    side_x = lax.axis_index("src") // 2
    total, cols = outs[0].shape
    planes = total // lines
    entries = keys.shape[0]
    lane = lane_iota((1, cols))
    low = me * depth - WIDE
    start = search(keys, low * entries)
    stop = search(keys, (low + planes) * entries)
    row_base = (nx // 2) * side_x - 2 * PAD
    plane_base = low * lines + row_base

    def clear(q, carry):
        for out in outs:
            out[pl.ds(pl.multiple_of(q * lines, 8), lines), :] = jnp.zeros((lines, cols), F32)
        return carry

    lax.fori_loop(0, planes, clear, 0)

    def body(g, carry):
        parts = []
        least = start + g * group
        j = jnp.minimum(least, entries - group)
        for e in range(group):
            key, cell = keys[j + e], cells[j + e]
            o = key & (entries - 1)
            row = cell >> bits(cols)
            inside = jnp.logical_and(j + e >= least, j + e < stop)
            inside = jnp.logical_and(inside, jnp.logical_and(row >= row_base + PAD, row < row_base + lines - PAD))
            hit = lane == jnp.where(inside, lane_of(cell & (cols - 1), cols), -1)
            at = jnp.where(inside, (key >> bits(entries)) * lines + row - plane_base, 0)
            parts.append((at, [jnp.where(hit, data[o + n * entries], 0.0) for n in (0, 1)]))
        for at, values in parts:
            for out, value in zip(outs, values):
                out[pl.ds(at, 1), :] = out[pl.ds(at, 1), :] + value
        return carry

    lax.fori_loop(0, (stop - start + group - 1) // group, body, 0)


def scatter(keys, cells, data, depth, nx, cols):
    smem = pl.BlockSpec(memory_space=SMEM)
    full = pl.BlockSpec(memory_space=VMEM)
    lines = nx // 2 + 4 * PAD
    planes = depth + 2 * WIDE
    back = pl.pallas_call(
        functools.partial(scatter_kernel, 8, depth, nx, lines),
        name="scatter",
        out_shape=[jax.ShapeDtypeStruct((planes * lines, cols), F32)] * 2,
        in_specs=[smem, smem, smem],
        out_specs=[full, full],
        compiler_params=pltpu.CompilerParams(vmem_limit_bytes=8 << 20),
    )(keys, cells, data.reshape(-1))
    return [ref.reshape(planes, lines, cols) for ref in back]


def second_kernel(
    slabs, nx, lc_half, lc_near, u_mine, u_first, u_rest, mean_in, v00, v01, out,
    sig, dg, hx, hy, hz, v1, v2, v3, u2, adj, give, take, pair, far, order,
    s_load, s_u, r_u, s_far, r_far, s_c2, r_c2, s_give, r_give, s_x, r_x, s_own, r_own, s_fwd, r_fwd,
    *sums,
):
    src = lax.axis_index("src")
    me = lax.axis_index("slab")
    depth, _, cols = out.shape
    half = nx // 2
    frame = half + 2 * PAD
    frame_rows = half + PAD
    quarter = depth // 2
    core, side_x = lax.rem(src, 2), src // 2
    mate, across = flip(src, 1), flip(src, 2)
    wide = depth + 2 * WIDE
    ring = [(src, lax.rem(me + 1, slabs)), (src, lax.rem(me + slabs - 1, slabs))]
    barrier, count = signal_all(src, me, slabs, ring + [(mate, me)] + [(across, t) for t in pair_group(me)])
    total = Sum(src, me, slabs, sum_levels(sums), across)
    order[...] = order_matrix(cols, True)
    owned = chunks(half, PAD)
    rims = [(0, PAD), (PAD + half, PAD)]
    every = rims[:1] + owned + rims[1:]

    zero_pads(sig, frame)
    zero_pads(hy, frame)
    for ref in (v1, v2, v3):
        for j in (0, 1):
            zero_pads(ref.at[j], frame)

    outside = pl.ds(pl.multiple_of(PAD + (half + PAD) * side_x, PAD), PAD)
    u2[:, :, pl.ds(pl.multiple_of((half + PAD) * side_x, PAD), PAD), :] = jnp.zeros((2, depth + 2, PAD, cols), F32)
    frame_mine = pl.ds(pl.multiple_of(PAD * (1 - side_x), PAD), frame_rows)
    frame_theirs = pl.ds(pl.multiple_of(PAD * side_x, PAD), frame_rows)
    early = pl.ds(0, EARLY)
    late = pl.ds(EARLY, depth + 2 - EARLY)
    loads = [
        pltpu.make_async_copy(u_mine, u2.at[side_x, :, frame_mine], s_load.at[0]),
        pltpu.make_async_copy(u_first, u2.at[1 - side_x, early, frame_mine], s_load.at[1]),
    ]
    for load in loads:
        load.start()
    low_in, high_in = (me > 0).astype(F32), (me < slabs - 1).astype(F32)

    def conductivity(ref, count, first, factor=None):
        def body(n, carry):
            for r, rows in chunks(frame_rows):
                to = pl.multiple_of(PAD + PAD * (1 - side_x) + r, PAD)
                value = jnp.exp(ref[n, pl.ds(r, rows), :])
                sig[first + 1 + n, pl.ds(to, rows), :] = value if factor is None else factor * value
            sig[first + 1 + n, outside, :] = jnp.zeros((PAD, cols), F32)
            return carry

        lax.fori_loop(0, count, body, 0)

    conductivity(lc_half, depth, WIDE)
    conductivity(lc_near, 1, WIDE - 1, low_in)
    conductivity(lc_near.at[pl.ds(1, 1)], 1, WIDE + depth, high_in)

    arrives = (me > 0, me < slabs - 1)
    sends = (me < slabs - 1, me > 0)
    to_slab = (me + 1, me - 1)
    part = -(-frame_rows // (2 * PAD)) * PAD
    fetched = pl.ds(pl.multiple_of((frame_rows - part) * core, PAD), part)
    given = pl.ds(pl.multiple_of(part * core, PAD), frame_rows - part)
    taken = pl.ds(pl.multiple_of(part * (1 - core), PAD), frame_rows - part)

    def copy_far(side, to):
        planes = pl.ds(depth - WIDE if side == 0 else 1, WIDE - 1)
        return remote(lc_half.at[planes, fetched], far.at[side, :, fetched], s_far.at[side], r_far.at[side], (src, to))

    def share_far(side, rows):
        ref = far.at[side, :, rows]
        return remote(ref, ref, s_c2.at[side], r_c2.at[side], (mate, me))

    copy_rest = remote(u_rest, u2.at[side_x, late, frame_theirs], s_u, r_u, (across, me))
    pl.semaphore_wait(barrier, count)
    for side in (0, 1):
        pl.when(sends[side])(lambda side=side: copy_far(side, to_slab[side]).start())

    first, last = WIDE - me * depth, WIDE + (slabs - me) * depth - 1
    low_open, high_open = side_x.astype(F32), 1.0 - side_x.astype(F32)

    def coefs(start, stop, top=True):
        make_coefs(sig, dg, hx, hy, hz, start, stop, first, last, every, top)

        def close(q, carry):
            for line, factor in ((2 * PAD - 1, low_open), (2 * PAD + half - 1, high_open)):
                hy[q, pl.ds(line, 1), :] = hy[q, pl.ds(line, 1), :] * factor
            return carry

        lax.fori_loop(start, stop, close, 0)

    mean = mean_in[0:1, 0:1]
    scale = 6.0 * mean
    inv = 1.0 / scale
    zero = jnp.zeros((8, cols), F32)
    fields = [(v0, v1.at[j], v2.at[j], v3.at[j]) for j, v0 in enumerate((v00, v01))]
    sums_of = {}

    def run(k, start, stop, dotted):
        shift = THETA[k] * mean * inv
        for j in (0, 1):
            def step(q, accs, j=j):
                accs = list(accs)
                for r, rows in every:
                    here, image = operator(fields[j][k], q - k, dg, hx, hy, hz, q, r, rows)
                    new = inv * image - shift * here
                    fields[j][k + 1][q - k - 1, pl.ds(PAD + r, rows), :] = new
                    if not dotted or (r, rows) not in owned:
                        continue
                    if k == 0:
                        accs[0] = accs[0] + fold(here * here)
                    for i in range(k + 1):
                        other = here if i == k else fields[j][i][q - i, pl.ds(PAD + r, rows), :]
                        accs[i + (k == 0)] = accs[i + (k == 0)] + fold(new * other)
                    accs[-1] = accs[-1] + fold(new * new)
                return tuple(accs)

            accs = sums_of.get((j, k), (zero,) * (3 if k == 0 else k + 2)) if dotted else ()
            accs = lax.fori_loop(start, stop, step, accs)
            if dotted:
                sums_of[j, k] = accs

    top = WIDE + depth
    coefs(WIDE, top)
    run(0, WIDE, top, True)
    for side in (0, 1):
        @pl.when(arrives[side])
        def _():
            copy_far(side, me).wait_recv()
            share_far(side, given).start()

        @pl.when(jnp.logical_not(arrives[side]))
        def _():
            far[side] = jnp.zeros(far.shape[1:], F32)

    copy_rest.start()
    for k in (1, 2):
        run(k, WIDE + k, top - k, True)
    for side in (0, 1):
        pl.when(arrives[side])(lambda side=side: share_far(side, taken).wait_recv())
    conductivity(far.at[0], WIDE - 1, 0, low_in)
    conductivity(far.at[1], WIDE - 1, top + 1, high_in)
    coefs(1, WIDE, False)
    coefs(top, wide - 1)
    for k in range(3):
        run(k, k + 1, WIDE, False)
        if k:
            run(k, WIDE, WIDE + k, True)
            run(k, top - k, top, True)
        run(k, top, wide - k - 1, False)
    dots = [[acc for k in range(3) for acc in sums_of[j, k]] for j in (0, 1)]

    for j in (0, 1):
        def energy(q, acc, j=j):
            for r, rows in owned:
                here, image = operator(v3.at[j], q + 1, dg, hx, hy, hz, q + WIDE, r, rows)
                acc = acc + fold(here * image)
            return acc

        dots[j].append(lax.fori_loop(0, depth, energy, zero))

    row = total.whole(pack_row(dots[0] + dots[1]))
    thetas = [t * mean for t in THETA]
    coef = [solve_small(row, scale, thetas, n) for n in (0, len(dots[0]))]

    def combine(q, carry):
        for j in (0, 1):
            c = coef[j]
            for r, rows in every:
                value = c[3] * v3[j, q, pl.ds(PAD + r, rows), :]
                for i, ref in enumerate(fields[j][:3]):
                    value = value + c[i] * ref[q + 3 - i, pl.ds(PAD + r, rows), :]
                adj[j, q, pl.ds(r, rows), :] = value
        return carry

    lax.fori_loop(0, depth + 2, combine, 0)
    for load in loads:
        load.wait()
    copy_rest.wait()
    for side in (0, 1):
        pl.when(sends[side])(lambda side=side: copy_far(side, me).wait_send())
        pl.when(arrives[side])(lambda side=side: share_far(side, given).wait_send())

    def partial(q, dst, slot):
        for r, rows in owned:
            total = jnp.zeros((rows, cols), F32)
            for j in (0, 1):
                f = u2[j, q + 1, pl.ds(r, rows), :]
                a = adj[j, q + 1, pl.ds(r, rows), :]
                lane = lane_iota(f.shape)
                fr = jnp.where(lane == cols - 1, 0.0, next_lane(f))
                ar = jnp.where(lane == cols - 1, 0.0, next_lane(a))
                flow = (f - fr) * (a - ar)
                total = total + (flow + jnp.where(lane == 0, f * a, prev_lane(flow)))
                for dq, dr in ((0, 1), (0, -1), (1, 0), (-1, 0)):
                    fj = u2[j, q + 1 + dq, pl.ds(r + dr, rows), :]
                    aj = adj[j, q + 1 + dq, pl.ds(r + dr, rows), :]
                    total = total + (f - fj) * (a - aj)
            scaled = -0.5 * sig[q + WIDE + 1, pl.ds(PAD + r, rows), :] * total
            dst[slot, pl.ds(r - PAD, rows), :] = scaled

    def copy_give(n):
        return remote(give.at[n], take.at[n], s_give.at[n], r_give.at[n], (mate, me))

    rows_mine = pl.ds(pl.multiple_of(half * side_x, PAD), half)
    rows_theirs = pl.ds(pl.multiple_of(half * (1 - side_x), PAD), half)

    def copy_x(n):
        ref = out.at[core * quarter + n, rows_mine]
        return remote(ref, ref, s_x.at[n], r_x.at[n], (across, me))

    def copy_own(n):
        ref = out.at[core * quarter + n, rows_mine]
        return remote(ref, ref, s_own.at[n], r_own.at[n], (mate, me))

    def copy_fwd(n):
        ref = out.at[core * quarter + n, rows_theirs]
        return remote(ref, ref, s_fwd.at[n], r_fwd.at[n], (mate, me))

    def giving(n, carry):
        partial((1 - core) * quarter + n, give, n)
        copy_give(n).start()
        return carry

    def keeping(n, carry):
        partial(core * quarter + n, pair, n)
        copy_give(n).wait_recv()
        for r, rows in ((0, half),):
            at = pl.multiple_of(half * side_x + r, PAD)
            value = pair[n, pl.ds(r, rows), :] + take[n, pl.ds(r, rows), :]
            out[core * quarter + n, pl.ds(at, rows), :] = reorder(value, order[...])
        copy_x(n).start()
        copy_own(n).start()
        return carry

    def passing(n, carry):
        copy_x(n).wait_recv()
        copy_fwd(n).start()
        return carry

    def ending(n, carry):
        copy_own(n).wait_recv()
        copy_fwd(n).wait_recv()
        for copy in (copy_give, copy_x, copy_own, copy_fwd):
            copy(n).wait_send()
        return carry

    for body in (giving, keeping, passing, ending):
        lax.fori_loop(0, quarter, body, 0)
    total.close()


def second_solve(slabs, nx, lc_half, lc_near, u_mine, u_first, u_rest, mean, back):
    depth, _, cols = lc_half.shape
    half = nx // 2
    frame = half + 2 * PAD
    plane = (frame + 2 * PAD, cols)
    wide = depth + 2 * WIDE
    quarter = depth // 2
    full = pl.BlockSpec(memory_space=VMEM)
    anywhere = pl.BlockSpec(memory_space=pl.ANY)
    pair = [DMA((2,)), DMA((2,))]
    return pl.pallas_call(
        functools.partial(second_kernel, slabs, nx),
        name="second_solve",
        out_shape=jax.ShapeDtypeStruct((depth, nx, cols), F32),
        in_specs=[full, full, anywhere, anywhere, anywhere, full, full, full],
        out_specs=full,
        scratch_shapes=[
            VMEM((wide + 2, *plane), F32),
            VMEM((wide, frame, cols), F32),
            VMEM((wide, frame, cols), F32),
            VMEM((wide, *plane), F32),
            VMEM((wide + 1, frame, cols), F32),
            VMEM((2, wide - 2, *plane), F32),
            VMEM((2, wide - 4, *plane), F32),
            VMEM((2, wide - 6, *plane), F32),
            VMEM((2, depth + 2, frame, cols), F32),
            VMEM((2, depth + 2, frame, cols), F32),
        ]
        + [VMEM((quarter, half, cols), F32)] * 3
        + [VMEM((2, WIDE - 1, half + PAD, cols), F32), VMEM((cols, cols), jnp.bfloat16)]
        + [DMA((2,)), DMA(()), DMA(())]
        + pair * 2
        + [DMA((quarter,))] * 8
        + sum_scratch(slabs, (1, 128), 8),
        compiler_params=pltpu.CompilerParams(
            collective_id=2, has_side_effects=True, vmem_limit_bytes=42 << 20
        ),
    )(lc_half, lc_near, u_mine, u_first, u_rest, mean, *back)


def shards(slabs, log_cond, perturb, potentials, rec_depth, rec_plan):
    depth, nx, cols = log_cond.shape
    dipoles = rec_depth.shape[1]
    order = lax.broadcasted_iota(jnp.int32, rec_depth.shape, 0) * dipoles
    order = order + lax.broadcasted_iota(jnp.int32, rec_depth.shape, 1)
    keys = (rec_depth * (2 * dipoles) + order).reshape(-1)
    keys, cells = lax.sort((keys, rec_plan.reshape(-1)), num_keys=1, is_stable=False)
    arguments = (pltpu.with_memory_space_constraint(a, pltpu.HBM) for a in (log_cond, perturb, potentials[0]))
    tangent, mean, lc_half, lc_near, u_mine, u_first, u_rest = first_solve(slabs, *arguments)
    part = gather(keys, cells, tangent.reshape(depth * nx, cols), depth)
    data = share(slabs, part)
    u_first, data = lax.optimization_barrier((u_first, data))
    u_first = lax.ppermute(u_first, "src", [(i, (i + 2) % 4) for i in range(4)])
    back = scatter(keys, cells, data, depth, nx, cols)
    return second_solve(slabs, nx, lc_half, lc_near, u_mine, u_first, u_rest, mean, back)


def solution(mesh):
    in_specs = (
        P("slab", None, None),
        P("slab", None, None),
        P("src", "slab", None, None),
        P(),
        P(),
    )
    return jax.shard_map(
        functools.partial(shards, mesh.shape["slab"]),
        mesh=mesh,
        in_specs=in_specs,
        out_specs=P("slab", None, None),
        check_vma=False,
    )
```

```python
import functools

import jax
import jax.numpy as jnp
from jax import lax
from jax.experimental import pallas as pl
from jax.experimental.pallas import tpu as pltpu
from jax.sharding import PartitionSpec as P

MESH = pl.DeviceIdType.MESH
F32 = jnp.float32
VMEM = pltpu.VMEM
SMEM = pltpu.SMEM
DMA = pltpu.SemaphoreType.DMA
PAD = 8
WIDE = 4
EARLY = 4
ROWS = 64
THETA = (6.0, 2.0, 10.0)


def lane_iota(shape):
    return lax.broadcasted_iota(jnp.int32, shape, len(shape) - 1)


def fold(value):
    rows, cols = value.shape
    return jnp.sum(value.reshape(rows // 8, 8, cols), axis=0)


def next_lane(value):
    half = value.shape[1] // 2
    even, odd = value[:, :half], value[:, half:]
    return jnp.concatenate([odd, pltpu.roll(even, half - 1, 1)], axis=1)


def prev_lane(value):
    half = value.shape[1] // 2
    even, odd = value[:, :half], value[:, half:]
    return jnp.concatenate([pltpu.roll(odd, 1, 1), even], axis=1)


def lane_of(column, cols):
    return (column >> 1) + (column & 1) * (cols // 2)


def order_matrix(cols, back):
    row = lax.broadcasted_iota(jnp.int32, (cols, cols), 0)
    col = lax.broadcasted_iota(jnp.int32, (cols, cols), 1)
    hit = row == lane_of(col, cols) if back else col == lane_of(row, cols)
    return jnp.where(hit, 1.0, 0.0).astype(jnp.bfloat16)


def reorder(value, matrix):
    total = None
    for _ in range(3):
        piece = value.astype(jnp.bfloat16)
        value = value - piece.astype(F32)
        moved = jnp.dot(piece, matrix, preferred_element_type=F32)
        total = moved if total is None else total + moved
    return total


def chunks(count, start=0):
    out = []
    done = 0
    while done < count:
        rows = min(ROWS, count - done)
        out.append((start + done, rows))
        done += rows
    return out


def make_coefs(sig, dg, hx, hy, hz, start, stop, first, last, pieces, top=True):
    cols = sig.shape[-1]

    def body(q, carry):
        low_in = jnp.logical_and(q - 1 >= first, q <= last).astype(F32)
        for r, rows in pieces:
            here = sig[q + 1, pl.ds(PAD + r, rows), :]
            up = sig[q + 1, pl.ds(PAD + r + 1, rows), :]
            down = sig[q + 1, pl.ds(PAD + r - 1, rows), :]
            low = sig[q, pl.ds(PAD + r, rows), :]
            high = sig[q + 2, pl.ds(PAD + r, rows), :]
            lane = lane_iota(here.shape)
            right = jnp.where(lane == cols - 1, 0.0, next_lane(here))
            left = jnp.where(lane == 0, 0.0, prev_lane(here))
            hx[q, pl.ds(r, rows), :] = jnp.where(lane == cols - 1, 0.0, 0.5 * (here + right))
            hy[q, pl.ds(PAD + r, rows), :] = 0.5 * (here + up)
            hz[q, pl.ds(r, rows), :] = (0.5 * low_in) * (here + low)
            total = ((up + down) + (left + right)) + (low + high)
            dg[q, pl.ds(r, rows), :] = 3.0 * here + 0.5 * total
        return carry

    lax.fori_loop(start, stop, body, 0)
    if not top:
        return
    inside = jnp.logical_and(stop - 1 >= first, stop <= last).astype(F32)
    for r, rows in pieces:
        here = sig[stop + 1, pl.ds(PAD + r, rows), :]
        low = sig[stop, pl.ds(PAD + r, rows), :]
        hz[stop, pl.ds(r, rows), :] = (0.5 * inside) * (here + low)


def operator(v, p, dg, hx, hy, hz, q, r, rows):
    here = v[p, pl.ds(PAD + r, rows), :]
    wx = hx[q, pl.ds(r, rows), :]
    acc = dg[q, pl.ds(r, rows), :] * here
    acc = acc - wx * next_lane(here)
    acc = acc - prev_lane(wx * here)
    acc = acc - hy[q, pl.ds(PAD + r, rows), :] * v[p, pl.ds(PAD + r + 1, rows), :]
    acc = acc - hy[q, pl.ds(PAD + r - 1, rows), :] * v[p, pl.ds(PAD + r - 1, rows), :]
    acc = acc - hz[q, pl.ds(r, rows), :] * v[p - 1, pl.ds(PAD + r, rows), :]
    acc = acc - hz[q + 1, pl.ds(r, rows), :] * v[p + 1, pl.ds(PAD + r, rows), :]
    return here, acc


def zero_pads(ref, nx):
    zero = jnp.zeros((ref.shape[0], PAD, ref.shape[2]), F32)
    ref[:, pl.ds(0, PAD), :] = zero
    ref[:, pl.ds(PAD + nx, PAD), :] = zero


def splat(row, index):
    return jnp.sum(jnp.where(lane_iota(row.shape) == index, row, 0.0), axis=1, keepdims=True)


def solve_small(row, scale, thetas, n=0):
    gram = {}
    for i in range(4):
        for j in range(i + 1):
            gram[i, j] = gram[j, i] = splat(row, n)
            n += 1
    last = splat(row, n)
    mat = {}
    for i in range(4):
        for j in range(i + 1):
            if j == 3:
                mat[i, j] = last
            else:
                mat[i, j] = scale * gram[i, j + 1] + thetas[j] * gram[i, j]
    low, inv = {}, {}
    for j in range(4):
        pivot = mat[j, j]
        for k in range(j):
            pivot = pivot - low[j, k] * low[j, k] * mat["d", k]
        mat["d", j] = pivot
        good = pivot > 1e-7 * mat[j, j]
        inv[j] = jnp.where(good, 1.0 / jnp.where(good, pivot, 1.0), 0.0)
        for i in range(j + 1, 4):
            value = mat[i, j]
            for k in range(j):
                value = value - low[i, k] * low[j, k] * mat["d", k]
            low[i, j] = value * inv[j]
    y = []
    for i in range(4):
        value = gram[i, 0]
        for k in range(i):
            value = value - low[i, k] * y[k]
        y.append(value)
    c = [None] * 4
    for i in reversed(range(4)):
        value = y[i] * inv[i]
        for k in range(i + 1, 4):
            value = value - low[k, i] * c[k]
        c[i] = value
    return c


def pack_row(accs):
    lane = lane_iota((1, 128))
    row = jnp.zeros((1, 128), F32)
    for n, acc in enumerate(accs):
        total = jnp.sum(jnp.sum(acc, axis=0, keepdims=True), axis=1, keepdims=True)
        row = row + jnp.where(lane == n, total, 0.0)
    return row


def remote(src_ref, dst_ref, send_sem, recv_sem, target):
    return pltpu.make_async_remote_copy(
        src_ref=src_ref,
        dst_ref=dst_ref,
        send_sem=send_sem,
        recv_sem=recv_sem,
        device_id=target,
        device_id_type=MESH,
    )


def flip(src, bit):
    return src + bit - 2 * bit * (lax.rem(src // bit, 2))


def partners(me, slabs):
    near = 4
    fours = slabs // near
    place, four = lax.rem(me, near), me // near
    return (
        [four * near + lax.rem(place + d, near) for d in range(1, near)],
        [lax.rem(four + d, fours) * near + place for d in range(1, fours)],
    )


def pair_group(me):
    place = lax.rem(me, 4)
    return [me - place + lax.rem(place + d, 4) for d in range(4)]


def signal_all(src, me, slabs, others):
    barrier = pltpu.get_barrier_semaphore()
    targets = [(src, t) for group in partners(me, slabs) for t in group] + others
    for target in targets:
        pl.semaphore_signal(barrier, inc=1, device_id=target, device_id_type=MESH)
    return barrier, len(targets)


class Sum:
    def __init__(self, src, me, slabs, levels, across=None):
        groups = [[(src, t) for t in group] for group in partners(me, slabs)]
        if across is not None:
            groups[0] += [(across, t) for t in pair_group(me)]
        self.levels = [(level, group) for level, group in zip(levels, groups) if group]

    def send(self, n, value):
        (buf, send_sem, recv_sem), group = self.levels[n]
        buf[0] = value
        for d, target in enumerate(group):
            remote(buf.at[0], buf.at[d + 1], send_sem, recv_sem, target).start()

    def _wait(self, n, which):
        level, group = self.levels[n]
        rest = level[0].at[pl.ds(1, len(group))]
        pltpu.make_async_copy(rest, rest, level[which]).wait()

    def receive(self, n):
        self._wait(n, 2)
        return jnp.sum(self.levels[n][0][0][...], axis=0)

    def start(self, value):
        self.send(0, value)

    def middle(self):
        value = self.receive(0)
        if len(self.levels) > 1:
            self.send(1, value)
        return value

    def end(self, value):
        return self.receive(1) if len(self.levels) > 1 else value

    def whole(self, value):
        self.start(value)
        return self.end(self.middle())

    def close(self):
        for n in range(len(self.levels)):
            self._wait(n, 1)


def sum_scratch(slabs, shape, first=4):
    return [
        VMEM((first, *shape), F32), DMA(()), DMA(()),
        VMEM((max(slabs // 4, 2), *shape), F32), DMA(()), DMA(()),
    ]


def sum_levels(refs):
    return (refs[0:3], refs[3:6])


def first_kernel(
    slabs, lc_in, pt_in, u, tan, mean_out, lc_half, lc_near, u_mine, u_first, u_rest,
    lc, pt, lch, uh, sig, wgt, uw, dg, hx, hy, hz, v0, v1, v2, v3, pth, edge, order,
    s_load, s_take, s_first, r_first, s_c, r_c, s_x, r_x, s_core, r_core, s_v, r_v, s_e, r_e, *sums,
):
    src = lax.axis_index("src")
    me = lax.axis_index("slab")
    depth, nx, cols = lc.shape
    half = nx // 2
    has_low = me > 0
    has_high = me < slabs - 1
    core, side_x = lax.rem(src, 2), src // 2
    mate, across = flip(src, 1), flip(src, 2)
    inner_rows = pl.ds(PAD, nx)
    loads = [
        pltpu.make_async_copy(u, uw.at[pl.ds(1, depth), inner_rows], s_load.at[0]),
        pltpu.make_async_copy(lc_in, lc, s_load.at[1]),
        pltpu.make_async_copy(pt_in, pt, s_load.at[2]),
    ]
    for load in loads:
        load.start()
    ring = [(src, lax.rem(me + 1, slabs)), (src, lax.rem(me + slabs - 1, slabs))]
    barrier, count = signal_all(src, me, slabs, ring + [(mate, me), (across, me)])
    order[...] = order_matrix(cols, False)

    def shuffle(q, carry):
        for n in (0, 1):
            for ref, plane, first in ((lc, q, 0), (pt, q, 0), (uw, q + 1, PAD)):
                rows = pl.ds(first + n * half, half)
                ref[plane, rows, :] = reorder(ref[plane, rows, :], order[...])
        return carry

    for load in loads:
        load.wait()
    lax.fori_loop(0, 2, lambda i, c: shuffle(i * (depth - 1), c), 0)
    pl.semaphore_wait(barrier, count)
    mean_sum = Sum(src, me, slabs, sum_levels(sums[0:6]))
    mom_sum = Sum(src, me, slabs, sum_levels(sums[6:12]))

    def arrives(side):
        return has_low if side == 0 else has_high

    def below(side):
        return me + 1 if side == 0 else me - 1

    def sends(side):
        return has_high if side == 0 else has_low

    def near(side):
        return depth - 1 if side == 0 else 0

    def part(n):
        return pl.ds(n * half, half)

    def copy_u(side, n, to):
        return remote(
            uw.at[1 + near(side), pl.ds(PAD + n * half, half)], uh.at[side, part(n)],
            s_first.at[side, n], r_first.at[side, n], (src, to),
        )

    my_rows = pl.ds(pl.multiple_of(half * side_x, PAD), half)
    their_rows = pl.ds(pl.multiple_of(half * (1 - side_x), PAD), half)

    def copy_c(ref, dst, side, to):
        return remote(
            ref.at[near(side), my_rows], dst.at[side, my_rows], s_c.at[side], r_c.at[side], (src, to)
        )

    def swap(ref, side, rows):
        return remote(ref.at[side, rows], ref.at[side, rows], s_x.at[side], r_x.at[side], (across, me))

    def forward(ref, side):
        return remote(ref.at[side], ref.at[side], s_core.at[side], r_core.at[side], (mate, me))

    def by_core(body):
        pl.when(core == 0)(lambda: body(lc, lch))
        pl.when(core == 1)(lambda: body(pt, pth))

    for side in (0, 1):
        @pl.when(sends(side))
        def _():
            by_core(lambda ref, dst: copy_c(ref, dst, side, below(side)).start())

    for ref in (sig, wgt, uw, hy, v0, v1, v2, v3):
        zero_pads(ref, nx)
    for side in (0, 1):
        @pl.when(sends(side))
        def _():
            copy_c(lc, lch, side, me).wait_send()

    for n in (0, 1):
        for side in (0, 1):
            pl.when(sends(side))(lambda side=side, n=n: copy_u(side, n, below(side)).start())

    def own(q, acc):
        for r, rows in chunks(nx):
            value = jnp.exp(lc[q, pl.ds(r, rows), :])
            sig[q + 1, pl.ds(PAD + r, rows), :] = value
            wgt[q + 1, pl.ds(PAD + r, rows), :] = value * pt[q, pl.ds(r, rows), :]
            acc = acc + fold(value)
        return acc

    lax.fori_loop(1, depth - 1, shuffle, 0)
    acc = lax.fori_loop(0, depth, own, jnp.zeros((8, cols), F32))
    mean_sum.start(pack_row([acc]))

    fields = (v0, v1, v2, v3)
    for ref in fields:
        for side in (0, 1):
            def clear(ref=ref, side=side):
                ref[side * (depth + 1), pl.ds(PAD, nx), :] = jnp.zeros((nx, cols), F32)

            if ref is v3:
                clear()
            else:
                pl.when(jnp.logical_not(arrives(side)))(clear)
    mean_part = mean_sum.middle()

    for side in (0, 1):
        @pl.when(arrives(side))
        def _():
            def body(ref, dst):
                copy_c(ref, dst, side, me).wait_recv()
                swap(dst, side, my_rows).start()

            by_core(body)
    for side in (0, 1):
        @pl.when(arrives(side))
        def _():
            def body(ref, dst):
                swap(dst, side, their_rows).wait_recv()
                forward(dst, side).start()

            by_core(body)

    def rhs_rows(q, pieces):
        for r, rows in pieces:
            c = wgt[q + 1, pl.ds(PAD + r, rows), :]
            f = uw[q + 1, pl.ds(PAD + r, rows), :]
            lane = lane_iota(c.shape)
            cr = jnp.where(lane == cols - 1, 0.0, next_lane(c))
            fr = jnp.where(lane == cols - 1, 0.0, next_lane(f))
            flow = (c + cr) * (f - fr)
            total = flow + jnp.where(lane == 0, c * f, -prev_lane(flow))
            for dq, dr in ((0, 1), (0, -1), (1, 0), (-1, 0)):
                cj = wgt[q + 1 + dq, pl.ds(PAD + r + dr, rows), :]
                fj = uw[q + 1 + dq, pl.ds(PAD + r + dr, rows), :]
                total = total + (c + cj) * (f - fj)
            v0[q + 1, pl.ds(PAD + r, rows), :] = -0.5 * total

    def copy_v(k, side, n, to):
        plane = depth if side == 0 else 1
        halo = 0 if side == 0 else depth + 1
        rows = pl.ds(PAD + n * half, half)
        ref = fields[k]
        return remote(
            ref.at[plane, rows], ref.at[halo, rows], s_v.at[k, side, n], r_v.at[k, side, n], (src, to)
        )

    def send_edge(k, side, n):
        out = 1 - side

        @pl.when(sends(out))
        def _():
            copy_v(k, out, n, below(out)).start()

    for n in (0, 1):
        for side in (0, 1):
            plane = 0 if side == 0 else depth + 1

            @pl.when(arrives(side))
            def _():
                if n == 0:
                    pl.when(core == 0)(lambda: forward(pth, side).wait_recv())
                    pl.when(core == 1)(lambda: forward(lch, side).wait_recv())
                copy_u(side, n, me).wait_recv()
                for r, rows in chunks(half, n * half):
                    value = jnp.exp(lch[side, pl.ds(r, rows), :])
                    sig[plane, pl.ds(PAD + r, rows), :] = value
                    wgt[plane, pl.ds(PAD + r, rows), :] = value * pth[side, pl.ds(r, rows), :]
                    uw[plane, pl.ds(PAD + r, rows), :] = uh[side, pl.ds(r, rows), :]

            @pl.when(jnp.logical_not(arrives(side)))
            def _():
                for ref in (sig, wgt, uw):
                    ref[plane, pl.ds(PAD + n * half, half), :] = jnp.zeros((half, cols), F32)
                lch[side, part(n), :] = jnp.zeros((half, cols), F32)

            rhs_rows(0 if side == 0 else depth - 1, chunks(half, n * half))
            send_edge(0, side, n)

    frame_rows = half + PAD
    mine = half * side_x - PAD * side_x
    theirs = (half - PAD) - mine
    takes = []
    for n, (ref, dst, first, at) in enumerate((
        (lc, lc_half, 0, mine),
        (lch, lc_near, 0, mine),
        (uw, u_mine, 0, PAD + mine),
        (uw, u_first, 0, PAD + theirs),
        (uw, u_rest, EARLY, PAD + theirs),
    )):
        rows = pl.ds(pl.multiple_of(at, PAD), frame_rows)
        takes.append(pltpu.make_async_copy(ref.at[pl.ds(first, dst.shape[0]), rows], dst, s_take.at[n]))
    for take in takes:
        take.start()

    def inner(body, carry):
        return lax.fori_loop(1, depth - 1, body, carry)

    def rhs_plane(q, carry):
        rhs_rows(q, chunks(nx))
        return carry

    inner(rhs_plane, 0)
    first, last = -me * depth, (slabs - me) * depth - 1
    make_coefs(sig, dg, hx, hy, hz, 0, depth, first, last, chunks(nx))

    mean = splat(mean_sum.end(mean_part), 0) * (1.0 / (slabs * depth * nx * cols))
    mean_out[...] = jnp.broadcast_to(mean, (8, 128))
    scale = 6.0 * mean
    inv = 1.0 / scale

    zero = jnp.zeros((8, cols), F32)
    dots = []
    for k in range(3):
        shift = THETA[k] * mean * inv

        def step(q, accs, pieces=None, k=k, shift=shift):
            accs = list(accs)
            for r, rows in pieces or chunks(nx):
                here, image = operator(fields[k], q + 1, dg, hx, hy, hz, q, r, rows)
                new = inv * image - shift * here
                fields[k + 1][q + 1, pl.ds(PAD + r, rows), :] = new
                if k == 0:
                    accs[0] = accs[0] + fold(here * here)
                for i in range(k + 1):
                    other = here if i == k else fields[i][q + 1, pl.ds(PAD + r, rows), :]
                    accs[i + (k == 0)] = accs[i + (k == 0)] + fold(new * other)
                accs[-1] = accs[-1] + fold(new * new)
            return tuple(accs)

        accs = inner(step, (zero,) * (3 if k == 0 else k + 2))
        for n in (0, 1):
            for side in (0, 1):
                pl.when(arrives(side))(lambda side=side, n=n, k=k: copy_v(k, side, n, me).wait_recv())
                accs = step(0 if side == 0 else depth - 1, accs, chunks(half, n * half))
                if k < 2:
                    send_edge(k + 1, side, n)
        dots.extend(accs)

    def copy_edge(side, to):
        plane = depth if side == 0 else 1
        return remote(
            v3.at[plane, pl.ds(PAD + side * half, half)], edge.at[side], s_e.at[side], r_e.at[side], (src, to)
        )

    for side in (0, 1):
        pl.when(sends(side))(lambda side=side: copy_edge(side, below(side)).start())
    def energy(q, acc):
        for r, rows in chunks(nx):
            here, image = operator(v3, q + 1, dg, hx, hy, hz, q, r, rows)
            acc = acc + fold(here * image)
        return acc

    acc = lax.fori_loop(0, depth, energy, zero)
    for side in (0, 1):
        got = arrives(side)
        pl.when(got)(lambda side=side: copy_edge(side, me).wait_recv())

        @pl.when(jnp.logical_not(got))
        def _():
            edge[side] = jnp.zeros((half, cols), F32)

        for r, rows in chunks(half):
            at = side * half + r
            face = hz[side * depth, pl.ds(at, rows), :] * v3[1 + side * (depth - 1), pl.ds(PAD + at, rows), :]
            acc = acc - 2.0 * fold(face * edge[side, pl.ds(r, rows), :])
    dots.append(acc)
    mom_sum.start(pack_row(dots))
    value = mom_sum.middle()

    row = mom_sum.end(value)
    c = solve_small(row, scale, [t * mean for t in THETA])

    def combine(q, carry):
        for r, rows in chunks(nx):
            value = c[0] * v0[q + 1, pl.ds(PAD + r, rows), :]
            for i in (1, 2, 3):
                value = value + c[i] * fields[i][q + 1, pl.ds(PAD + r, rows), :]
            tan[q, pl.ds(r, rows), :] = value
        return carry

    lax.fori_loop(0, depth, combine, 0)

    for take in takes:
        take.wait()
    for side in (0, 1):
        @pl.when(sends(side))
        def _():
            copy_edge(side, me).wait_send()
            for n in (0, 1):
                copy_u(side, n, me).wait_send()
                for k in range(3):
                    copy_v(k, side, n, me).wait_send()

        @pl.when(arrives(side))
        def _():
            swap(lch, side, my_rows).wait_send()
            forward(lch, side).wait_send()
    mean_sum.close()
    mom_sum.close()


def first_solve(slabs, lc, pt, u):
    depth, nx, cols = lc.shape
    plane = (nx + 2 * PAD, cols)
    half = nx // 2
    full = pl.BlockSpec(memory_space=VMEM)
    pair = (DMA((2,)), DMA((2,)))
    return pl.pallas_call(
        functools.partial(first_kernel, slabs),
        name="first_solve",
        out_shape=[
            jax.ShapeDtypeStruct((depth, nx, cols), F32),
            jax.ShapeDtypeStruct((8, 128), F32),
            *(
                jax.ShapeDtypeStruct((planes, half + PAD, cols), F32)
                for planes in (depth, 2, depth + 2, EARLY, depth + 2 - EARLY)
            ),
        ],
        in_specs=[pl.BlockSpec(memory_space=pltpu.HBM)] * 3,
        out_specs=[full] * 7,
        scratch_shapes=[VMEM((depth, nx, cols), F32)] * 2
        + [VMEM((2, nx, cols), F32)] * 2
        + [VMEM((depth + 2, *plane), F32)] * 3
        + [
            VMEM((depth, nx, cols), F32),
            VMEM((depth, nx, cols), F32),
            VMEM((depth, *plane), F32),
            VMEM((depth + 1, nx, cols), F32),
        ]
        + [VMEM((depth + 2, *plane), F32)] * 4
        + [VMEM((2, nx, cols), F32), VMEM((2, half, cols), F32), VMEM((cols, cols), jnp.bfloat16)]
        + [DMA((3,)), DMA((5,)), DMA((2, 2)), DMA((2, 2)), *pair, *pair, *pair]
        + [DMA((3, 2, 2)), DMA((3, 2, 2)), *pair]
        + sum_scratch(slabs, (1, 128)) * 2,
        compiler_params=pltpu.CompilerParams(
            collective_id=0, has_side_effects=True, vmem_limit_bytes=43 << 20
        ),
    )(lc, pt, u)


def over_window(group, ordered, first_key, last_key, keys, cells, keys_s, cells_s, sems, body):
    start, stop = (
        jnp.sum(jnp.where(ordered[...] < bound, 1.0, 0.0)).astype(jnp.int32) for bound in (first_key, last_key)
    )
    size = keys_s.shape[0]

    def piece(w, carry):
        base = pl.multiple_of(w * size, size)
        copies = [
            pltpu.make_async_copy(ref.at[pl.ds(base, size)], dst, sems.at[n])
            for n, (ref, dst) in enumerate(((keys, keys_s), (cells, cells_s)))
        ]
        for copy in copies:
            copy.start()
        for copy in copies:
            copy.wait()
        low = jnp.maximum(start - base, 0)
        high = jnp.minimum(stop - base, size)

        def step(g, carry):
            body(low + g * group, high)
            return carry

        return lax.fori_loop(0, (high - low + group - 1) // group, step, carry)

    lax.fori_loop(start // size, (stop + size - 1) // size, piece, 0)


def window_scratch(entries):
    size = min(1024, entries)
    return [SMEM((size,), jnp.int32), SMEM((size,), jnp.int32), DMA((2,))]


def bits(count):
    assert count & (count - 1) == 0
    return count.bit_length() - 1


def gather_kernel(group, depth, dipoles, ordered, keys, cells, field, out, keys_s, cells_s, sems):
    me = lax.axis_index("slab")
    out[...] = jnp.zeros_like(out)
    lines, cols = field.shape
    nx = lines // depth
    entries = 2 * dipoles
    lane = lane_iota((1, cols))
    short = lane_iota((1, 128))
    base = me * lines

    def body(least, stop):
        parts = []
        j = jnp.minimum(least, keys_s.shape[0] - group)
        for e in range(group):
            key, cell = keys_s[j + e], cells_s[j + e]
            o = key & (entries - 1)
            k = o & (dipoles - 1)
            line = ((key >> bits(entries)) << bits(nx)) + (cell >> bits(cols)) - base
            inside = jnp.logical_and(j + e >= least, j + e < stop)
            lane_at = jnp.where(inside, lane_of(cell & (cols - 1), cols), -1)
            picked = jnp.where(lane == lane_at, field[pl.ds(jnp.where(inside, line, 0), 1), :], 0.0)
            value = jnp.sum(picked, axis=1, keepdims=True)
            value = jnp.where(o < dipoles, value, -value)
            parts.append((k >> 7, jnp.where(short == (k & 127), value, 0.0)))
        for line, value in parts:
            out[pl.ds(line, 1), :] = out[pl.ds(line, 1), :] + value

    first = me * depth * entries
    over_window(group, ordered, first, first + depth * entries, keys, cells, keys_s, cells_s, sems, body)


def gather(keys, cells, field, depth):
    anywhere = pl.BlockSpec(memory_space=pl.ANY)
    full = pl.BlockSpec(memory_space=VMEM)
    entries = keys.shape[0]
    return pl.pallas_call(
        functools.partial(gather_kernel, 16, depth, entries // 2),
        name="gather",
        out_shape=jax.ShapeDtypeStruct((entries // 256, 128), F32),
        in_specs=[full, anywhere, anywhere, full],
        out_specs=full,
        scratch_shapes=window_scratch(entries),
        compiler_params=pltpu.CompilerParams(vmem_limit_bytes=8 << 20),
    )(keys.reshape(-1, 128), keys, cells, field)


def share_kernel(slabs, part, out, s_x, r_x, *sums):
    src = lax.axis_index("src")
    me = lax.axis_index("slab")
    side_x = src // 2
    across = flip(src, 2)
    barrier, count = signal_all(src, me, slabs, [(across, me)])
    pl.semaphore_wait(barrier, count)
    total = Sum(src, me, slabs, sum_levels(sums))
    out[side_x] = total.whole(part[...])
    copy = remote(out.at[side_x], out.at[side_x], s_x, r_x, (across, me))
    copy.start()
    copy.wait()
    total.close()


def share(slabs, part):
    full = pl.BlockSpec(memory_space=VMEM)
    return pl.pallas_call(
        functools.partial(share_kernel, slabs),
        name="share_data",
        out_shape=jax.ShapeDtypeStruct((2, *part.shape), F32),
        in_specs=[full],
        out_specs=full,
        scratch_shapes=[DMA(()), DMA(())] + sum_scratch(slabs, part.shape),
        compiler_params=pltpu.CompilerParams(
            collective_id=1, has_side_effects=True, vmem_limit_bytes=8 << 20
        ),
    )(part)


def scatter_kernel(group, depth, nx, lines, ordered, keys, cells, data, out0, out1, keys_s, cells_s, sems):
    me = lax.axis_index("slab")
    side_x = lax.axis_index("src") // 2
    outs = (out0, out1)
    total, cols = out0.shape
    planes = total // lines
    entries = keys.shape[0]
    dipoles = entries // 2
    lane = lane_iota((1, cols))
    low = me * depth - WIDE
    row_base = (nx // 2) * side_x - 2 * PAD
    plane_base = low * lines + row_base

    def clear(q, carry):
        for out in outs:
            out[pl.ds(pl.multiple_of(q * lines, 8), lines), :] = jnp.zeros((lines, cols), F32)
        return carry

    lax.fori_loop(0, planes, clear, 0)

    def body(least, stop):
        parts = []
        j = jnp.minimum(least, keys_s.shape[0] - group)
        for e in range(group):
            key, cell = keys_s[j + e], cells_s[j + e]
            o = key & (entries - 1)
            k = o & (dipoles - 1)
            row = cell >> bits(cols)
            inside = jnp.logical_and(j + e >= least, j + e < stop)
            inside = jnp.logical_and(inside, jnp.logical_and(row >= row_base + PAD, row < row_base + lines - PAD))
            hit = lane == jnp.where(inside, lane_of(cell & (cols - 1), cols), -1)
            at = jnp.where(inside, (key >> bits(entries)) * lines + row - plane_base, 0)
            sign = jnp.where(o < dipoles, 1.0, -1.0)
            parts.append((at, [jnp.where(hit, data[k + n * dipoles] * sign, 0.0) for n in (0, 1)]))
        for at, values in parts:
            for out, value in zip(outs, values):
                out[pl.ds(at, 1), :] = out[pl.ds(at, 1), :] + value

    over_window(
        group, ordered, low * entries, (low + planes) * entries, keys, cells, keys_s, cells_s, sems, body
    )


def scatter(keys, cells, data, depth, nx, cols):
    smem = pl.BlockSpec(memory_space=SMEM)
    anywhere = pl.BlockSpec(memory_space=pl.ANY)
    full = pl.BlockSpec(memory_space=VMEM)
    lines = nx // 2 + 4 * PAD
    planes = depth + 2 * WIDE
    back = pl.pallas_call(
        functools.partial(scatter_kernel, 8, depth, nx, lines),
        name="scatter",
        out_shape=[jax.ShapeDtypeStruct((planes * lines, cols), F32)] * 2,
        in_specs=[full, anywhere, anywhere, smem],
        out_specs=[full, full],
        scratch_shapes=window_scratch(keys.shape[0]),
        compiler_params=pltpu.CompilerParams(vmem_limit_bytes=8 << 20),
    )(keys.reshape(-1, 128), keys, cells, data.reshape(-1))
    return [ref.reshape(planes, lines, cols) for ref in back]


def second_kernel(
    slabs, nx, lc_half, lc_near, u_mine, u_first, u_rest, mean_in, v00, v01, out,
    sig, dg, hx, hy, hz, v1, v2, v3, u2, adj, give, take, pair, far, order,
    s_load, s_u, r_u, s_far, r_far, s_c2, r_c2, s_give, r_give, s_x, r_x, s_own, r_own, s_fwd, r_fwd,
    *sums,
):
    src = lax.axis_index("src")
    me = lax.axis_index("slab")
    depth, _, cols = out.shape
    half = nx // 2
    frame = half + 2 * PAD
    frame_rows = half + PAD
    quarter = depth // 2
    core, side_x = lax.rem(src, 2), src // 2
    mate, across = flip(src, 1), flip(src, 2)
    wide = depth + 2 * WIDE
    ring = [(src, lax.rem(me + 1, slabs)), (src, lax.rem(me + slabs - 1, slabs))]
    barrier, count = signal_all(src, me, slabs, ring + [(mate, me)] + [(across, t) for t in pair_group(me)])
    total = Sum(src, me, slabs, sum_levels(sums), across)
    order[...] = order_matrix(cols, True)
    owned = chunks(half, PAD)
    rims = [(0, PAD), (PAD + half, PAD)]
    every = rims[:1] + owned + rims[1:]

    zero_pads(sig, frame)
    zero_pads(hy, frame)
    for ref in (v1, v2, v3):
        for j in (0, 1):
            zero_pads(ref.at[j], frame)

    outside = pl.ds(pl.multiple_of(PAD + (half + PAD) * side_x, PAD), PAD)
    u2[:, :, pl.ds(pl.multiple_of((half + PAD) * side_x, PAD), PAD), :] = jnp.zeros((2, depth + 2, PAD, cols), F32)
    frame_mine = pl.ds(pl.multiple_of(PAD * (1 - side_x), PAD), frame_rows)
    frame_theirs = pl.ds(pl.multiple_of(PAD * side_x, PAD), frame_rows)
    early = pl.ds(0, EARLY)
    late = pl.ds(EARLY, depth + 2 - EARLY)
    loads = [
        pltpu.make_async_copy(u_mine, u2.at[side_x, :, frame_mine], s_load.at[0]),
        pltpu.make_async_copy(u_first, u2.at[1 - side_x, early, frame_mine], s_load.at[1]),
    ]
    for load in loads:
        load.start()
    low_in, high_in = (me > 0).astype(F32), (me < slabs - 1).astype(F32)

    def conductivity(ref, count, first, factor=None):
        def body(n, carry):
            for r, rows in chunks(frame_rows):
                to = pl.multiple_of(PAD + PAD * (1 - side_x) + r, PAD)
                value = jnp.exp(ref[n, pl.ds(r, rows), :])
                sig[first + 1 + n, pl.ds(to, rows), :] = value if factor is None else factor * value
            sig[first + 1 + n, outside, :] = jnp.zeros((PAD, cols), F32)
            return carry

        lax.fori_loop(0, count, body, 0)

    conductivity(lc_half, depth, WIDE)
    conductivity(lc_near, 1, WIDE - 1, low_in)
    conductivity(lc_near.at[pl.ds(1, 1)], 1, WIDE + depth, high_in)

    arrives = (me > 0, me < slabs - 1)
    sends = (me < slabs - 1, me > 0)
    to_slab = (me + 1, me - 1)
    part = -(-frame_rows // (2 * PAD)) * PAD
    fetched = pl.ds(pl.multiple_of((frame_rows - part) * core, PAD), part)
    given = pl.ds(pl.multiple_of(part * core, PAD), frame_rows - part)
    taken = pl.ds(pl.multiple_of(part * (1 - core), PAD), frame_rows - part)

    def copy_far(side, to):
        planes = pl.ds(depth - WIDE if side == 0 else 1, WIDE - 1)
        return remote(lc_half.at[planes, fetched], far.at[side, :, fetched], s_far.at[side], r_far.at[side], (src, to))

    def share_far(side, rows):
        ref = far.at[side, :, rows]
        return remote(ref, ref, s_c2.at[side], r_c2.at[side], (mate, me))

    copy_rest = remote(u_rest, u2.at[side_x, late, frame_theirs], s_u, r_u, (across, me))
    pl.semaphore_wait(barrier, count)
    for side in (0, 1):
        pl.when(sends[side])(lambda side=side: copy_far(side, to_slab[side]).start())
    copy_rest.start()

    first, last = WIDE - me * depth, WIDE + (slabs - me) * depth - 1
    low_open, high_open = side_x.astype(F32), 1.0 - side_x.astype(F32)

    def coefs(start, stop, top=True):
        make_coefs(sig, dg, hx, hy, hz, start, stop, first, last, every, top)

        def close(q, carry):
            for line, factor in ((2 * PAD - 1, low_open), (2 * PAD + half - 1, high_open)):
                hy[q, pl.ds(line, 1), :] = hy[q, pl.ds(line, 1), :] * factor
            return carry

        lax.fori_loop(start, stop, close, 0)

    mean = mean_in[0:1, 0:1]
    scale = 6.0 * mean
    inv = 1.0 / scale
    zero = jnp.zeros((8, cols), F32)
    fields = [(v0, v1.at[j], v2.at[j], v3.at[j]) for j, v0 in enumerate((v00, v01))]
    sums_of = {}

    def run(k, start, stop, dotted):
        shift = THETA[k] * mean * inv
        for j in (0, 1):
            def step(q, accs, j=j):
                accs = list(accs)
                for r, rows in every:
                    here, image = operator(fields[j][k], q - k, dg, hx, hy, hz, q, r, rows)
                    new = inv * image - shift * here
                    fields[j][k + 1][q - k - 1, pl.ds(PAD + r, rows), :] = new
                    if not dotted or (r, rows) not in owned:
                        continue
                    if k == 0:
                        accs[0] = accs[0] + fold(here * here)
                    for i in range(k + 1):
                        other = here if i == k else fields[j][i][q - i, pl.ds(PAD + r, rows), :]
                        accs[i + (k == 0)] = accs[i + (k == 0)] + fold(new * other)
                    accs[-1] = accs[-1] + fold(new * new)
                return tuple(accs)

            accs = sums_of.get((j, k), (zero,) * (3 if k == 0 else k + 2)) if dotted else ()
            accs = lax.fori_loop(start, stop, step, accs)
            if dotted:
                sums_of[j, k] = accs

    top = WIDE + depth
    coefs(WIDE, top)
    run(0, WIDE, top, True)
    run(1, WIDE + 1, top - 1, True)
    for side in (0, 1):
        @pl.when(arrives[side])
        def _():
            copy_far(side, me).wait_recv()
            share_far(side, given).start()

        @pl.when(jnp.logical_not(arrives[side]))
        def _():
            far[side] = jnp.zeros(far.shape[1:], F32)

    run(2, WIDE + 2, top - 2, True)
    for side in (0, 1):
        pl.when(arrives[side])(lambda side=side: share_far(side, taken).wait_recv())
    conductivity(far.at[0], WIDE - 1, 0, low_in)
    conductivity(far.at[1], WIDE - 1, top + 1, high_in)
    coefs(1, WIDE, False)
    coefs(top, wide - 1)
    for k in range(3):
        run(k, k + 1, WIDE, False)
        if k:
            run(k, WIDE, WIDE + k, True)
            run(k, top - k, top, True)
        run(k, top, wide - k - 1, False)
    dots = [[acc for k in range(3) for acc in sums_of[j, k]] for j in (0, 1)]

    for j in (0, 1):
        def energy(q, acc, j=j):
            for r, rows in owned:
                here, image = operator(v3.at[j], q + 1, dg, hx, hy, hz, q + WIDE, r, rows)
                acc = acc + fold(here * image)
            return acc

        dots[j].append(lax.fori_loop(0, depth, energy, zero))

    row = total.whole(pack_row(dots[0] + dots[1]))
    thetas = [t * mean for t in THETA]
    coef = [solve_small(row, scale, thetas, n) for n in (0, len(dots[0]))]

    def combine(q, carry):
        for j in (0, 1):
            c = coef[j]
            for r, rows in every:
                value = c[3] * v3[j, q, pl.ds(PAD + r, rows), :]
                for i, ref in enumerate(fields[j][:3]):
                    value = value + c[i] * ref[q + 3 - i, pl.ds(PAD + r, rows), :]
                adj[j, q, pl.ds(r, rows), :] = value
        return carry

    lax.fori_loop(0, depth + 2, combine, 0)
    for load in loads:
        load.wait()
    copy_rest.wait()
    for side in (0, 1):
        pl.when(sends[side])(lambda side=side: copy_far(side, me).wait_send())
        pl.when(arrives[side])(lambda side=side: share_far(side, given).wait_send())

    def partial(q, dst, slot):
        for r, rows in owned:
            total = jnp.zeros((rows, cols), F32)
            for j in (0, 1):
                f = u2[j, q + 1, pl.ds(r, rows), :]
                a = adj[j, q + 1, pl.ds(r, rows), :]
                lane = lane_iota(f.shape)
                fr = jnp.where(lane == cols - 1, 0.0, next_lane(f))
                ar = jnp.where(lane == cols - 1, 0.0, next_lane(a))
                flow = (f - fr) * (a - ar)
                total = total + (flow + jnp.where(lane == 0, f * a, prev_lane(flow)))
                for dq, dr in ((0, 1), (0, -1), (1, 0), (-1, 0)):
                    fj = u2[j, q + 1 + dq, pl.ds(r + dr, rows), :]
                    aj = adj[j, q + 1 + dq, pl.ds(r + dr, rows), :]
                    total = total + (f - fj) * (a - aj)
            scaled = -0.5 * sig[q + WIDE + 1, pl.ds(PAD + r, rows), :] * total
            dst[slot, pl.ds(r - PAD, rows), :] = scaled

    def copy_give(n):
        return remote(give.at[n], take.at[n], s_give.at[n], r_give.at[n], (mate, me))

    rows_mine = pl.ds(pl.multiple_of(half * side_x, PAD), half)
    rows_theirs = pl.ds(pl.multiple_of(half * (1 - side_x), PAD), half)

    def copy_x(n):
        ref = out.at[core * quarter + n, rows_mine]
        return remote(ref, ref, s_x.at[n], r_x.at[n], (across, me))

    def copy_own(n):
        ref = out.at[core * quarter + n, rows_mine]
        return remote(ref, ref, s_own.at[n], r_own.at[n], (mate, me))

    def copy_fwd(n):
        ref = out.at[core * quarter + n, rows_theirs]
        return remote(ref, ref, s_fwd.at[n], r_fwd.at[n], (mate, me))

    def giving(n, carry):
        partial((1 - core) * quarter + n, give, n)
        copy_give(n).start()
        return carry

    def keeping(n, carry):
        partial(core * quarter + n, pair, n)
        copy_give(n).wait_recv()
        for r, rows in ((0, half),):
            at = pl.multiple_of(half * side_x + r, PAD)
            value = pair[n, pl.ds(r, rows), :] + take[n, pl.ds(r, rows), :]
            out[core * quarter + n, pl.ds(at, rows), :] = reorder(value, order[...])
        copy_x(n).start()
        copy_own(n).start()
        return carry

    def passing(n, carry):
        copy_x(n).wait_recv()
        copy_fwd(n).start()
        return carry

    def ending(n, carry):
        copy_own(n).wait_recv()
        copy_fwd(n).wait_recv()
        for copy in (copy_give, copy_x, copy_own, copy_fwd):
            copy(n).wait_send()
        return carry

    def in_turn(n, carry):
        giving(n + 1, carry)
        return keeping(n, carry)

    giving(0, 0)
    lax.fori_loop(0, quarter - 1, in_turn, 0)
    keeping(quarter - 1, 0)
    for body in (passing, ending):
        lax.fori_loop(0, quarter, body, 0)
    total.close()


def second_solve(slabs, nx, lc_half, lc_near, u_mine, u_first, u_rest, mean, back):
    depth, _, cols = lc_half.shape
    half = nx // 2
    frame = half + 2 * PAD
    plane = (frame + 2 * PAD, cols)
    wide = depth + 2 * WIDE
    quarter = depth // 2
    full = pl.BlockSpec(memory_space=VMEM)
    anywhere = pl.BlockSpec(memory_space=pl.ANY)
    pair = [DMA((2,)), DMA((2,))]
    return pl.pallas_call(
        functools.partial(second_kernel, slabs, nx),
        name="second_solve",
        out_shape=jax.ShapeDtypeStruct((depth, nx, cols), F32),
        in_specs=[full, full, anywhere, anywhere, anywhere, full, full, full],
        out_specs=full,
        scratch_shapes=[
            VMEM((wide + 2, *plane), F32),
            VMEM((wide, frame, cols), F32),
            VMEM((wide, frame, cols), F32),
            VMEM((wide, *plane), F32),
            VMEM((wide + 1, frame, cols), F32),
            VMEM((2, wide - 2, *plane), F32),
            VMEM((2, wide - 4, *plane), F32),
            VMEM((2, wide - 6, *plane), F32),
            VMEM((2, depth + 2, frame, cols), F32),
            VMEM((2, depth + 2, frame, cols), F32),
        ]
        + [VMEM((quarter, half, cols), F32)] * 3
        + [VMEM((2, WIDE - 1, half + PAD, cols), F32), VMEM((cols, cols), jnp.bfloat16)]
        + [DMA((2,)), DMA(()), DMA(())]
        + pair * 2
        + [DMA((quarter,))] * 8
        + sum_scratch(slabs, (1, 128), 8),
        compiler_params=pltpu.CompilerParams(
            collective_id=2, has_side_effects=True, vmem_limit_bytes=42 << 20
        ),
    )(lc_half, lc_near, u_mine, u_first, u_rest, mean, *back)


def shards(slabs, log_cond, perturb, potentials, rec_depth, rec_plan):
    depth, nx, cols = log_cond.shape
    dipoles = rec_depth.shape[1]
    order = lax.broadcasted_iota(jnp.int32, rec_depth.shape, 0) * dipoles
    order = order + lax.broadcasted_iota(jnp.int32, rec_depth.shape, 1)
    keys = (rec_depth * (2 * dipoles) + order).reshape(-1)
    keys, cells = lax.sort((keys, rec_plan.reshape(-1)), num_keys=1, is_stable=False)
    arguments = (pltpu.with_memory_space_constraint(a, pltpu.HBM) for a in (log_cond, perturb, potentials[0]))
    tangent, mean, lc_half, lc_near, u_mine, u_first, u_rest = first_solve(slabs, *arguments)
    part = gather(keys, cells, tangent.reshape(depth * nx, cols), depth)
    data = share(slabs, part)
    u_first, data = lax.optimization_barrier((u_first, data))
    u_first = lax.ppermute(u_first, "src", [(i, (i + 2) % 4) for i in range(4)])
    back = scatter(keys, cells, data, depth, nx, cols)
    return second_solve(slabs, nx, lc_half, lc_near, u_mine, u_first, u_rest, mean, back)


def solution(mesh):
    in_specs = (
        P("slab", None, None),
        P("slab", None, None),
        P("src", "slab", None, None),
        P(),
        P(),
    )
    return jax.shard_map(
        functools.partial(shards, mesh.shape["slab"]),
        mesh=mesh,
        in_specs=in_specs,
        out_specs=P("slab", None, None),
        check_vma=False,
    )
```

```python
import functools

import jax
import jax.numpy as jnp
from jax import lax
from jax.experimental import pallas as pl
from jax.experimental.pallas import tpu as pltpu
from jax.sharding import PartitionSpec as P

MESH = pl.DeviceIdType.MESH
F32 = jnp.float32
VMEM = pltpu.VMEM
SMEM = pltpu.SMEM
DMA = pltpu.SemaphoreType.DMA
PAD = 8
WIDE = 4
EARLY = 4
ROWS = 64
THETA = (6.0, 2.0, 10.0)


def lane_iota(shape):
    return lax.broadcasted_iota(jnp.int32, shape, len(shape) - 1)


def fold(value):
    rows, cols = value.shape
    return jnp.sum(value.reshape(rows // 8, 8, cols), axis=0)


def next_lane(value):
    half = value.shape[1] // 2
    even, odd = value[:, :half], value[:, half:]
    return jnp.concatenate([odd, pltpu.roll(even, half - 1, 1)], axis=1)


def prev_lane(value):
    half = value.shape[1] // 2
    even, odd = value[:, :half], value[:, half:]
    return jnp.concatenate([pltpu.roll(odd, 1, 1), even], axis=1)


def lane_of(column, cols):
    return (column >> 1) + (column & 1) * (cols // 2)


def order_matrix(cols, back):
    row = lax.broadcasted_iota(jnp.int32, (cols, cols), 0)
    col = lax.broadcasted_iota(jnp.int32, (cols, cols), 1)
    hit = row == lane_of(col, cols) if back else col == lane_of(row, cols)
    return jnp.where(hit, 1.0, 0.0).astype(jnp.bfloat16)


def reorder(value, matrix):
    total = None
    for _ in range(3):
        piece = value.astype(jnp.bfloat16)
        value = value - piece.astype(F32)
        moved = jnp.dot(piece, matrix, preferred_element_type=F32)
        total = moved if total is None else total + moved
    return total


def chunks(count, start=0):
    out = []
    done = 0
    while done < count:
        rows = min(ROWS, count - done)
        out.append((start + done, rows))
        done += rows
    return out


def make_coefs(sig, dg, hx, hy, hz, start, stop, first, last, pieces, top=True):
    cols = sig.shape[-1]

    def body(q, carry):
        low_in = jnp.logical_and(q - 1 >= first, q <= last).astype(F32)
        for r, rows in pieces:
            here = sig[q + 1, pl.ds(PAD + r, rows), :]
            up = sig[q + 1, pl.ds(PAD + r + 1, rows), :]
            down = sig[q + 1, pl.ds(PAD + r - 1, rows), :]
            low = sig[q, pl.ds(PAD + r, rows), :]
            high = sig[q + 2, pl.ds(PAD + r, rows), :]
            lane = lane_iota(here.shape)
            right = jnp.where(lane == cols - 1, 0.0, next_lane(here))
            left = jnp.where(lane == 0, 0.0, prev_lane(here))
            hx[q, pl.ds(r, rows), :] = jnp.where(lane == cols - 1, 0.0, 0.5 * (here + right))
            hy[q, pl.ds(PAD + r, rows), :] = 0.5 * (here + up)
            hz[q, pl.ds(r, rows), :] = (0.5 * low_in) * (here + low)
            total = ((up + down) + (left + right)) + (low + high)
            dg[q, pl.ds(r, rows), :] = 3.0 * here + 0.5 * total
        return carry

    lax.fori_loop(start, stop, body, 0)
    if not top:
        return
    inside = jnp.logical_and(stop - 1 >= first, stop <= last).astype(F32)
    for r, rows in pieces:
        here = sig[stop + 1, pl.ds(PAD + r, rows), :]
        low = sig[stop, pl.ds(PAD + r, rows), :]
        hz[stop, pl.ds(r, rows), :] = (0.5 * inside) * (here + low)


def operator(v, p, dg, hx, hy, hz, q, r, rows):
    here = v[p, pl.ds(PAD + r, rows), :]
    wx = hx[q, pl.ds(r, rows), :]
    acc = dg[q, pl.ds(r, rows), :] * here
    acc = acc - wx * next_lane(here)
    acc = acc - prev_lane(wx * here)
    acc = acc - hy[q, pl.ds(PAD + r, rows), :] * v[p, pl.ds(PAD + r + 1, rows), :]
    acc = acc - hy[q, pl.ds(PAD + r - 1, rows), :] * v[p, pl.ds(PAD + r - 1, rows), :]
    acc = acc - hz[q, pl.ds(r, rows), :] * v[p - 1, pl.ds(PAD + r, rows), :]
    acc = acc - hz[q + 1, pl.ds(r, rows), :] * v[p + 1, pl.ds(PAD + r, rows), :]
    return here, acc


def zero_pads(ref, nx):
    zero = jnp.zeros((ref.shape[0], PAD, ref.shape[2]), F32)
    ref[:, pl.ds(0, PAD), :] = zero
    ref[:, pl.ds(PAD + nx, PAD), :] = zero


def splat(row, index):
    return jnp.sum(jnp.where(lane_iota(row.shape) == index, row, 0.0), axis=1, keepdims=True)


def solve_small(row, scale, thetas, n=0):
    gram = {}
    for i in range(4):
        for j in range(i + 1):
            gram[i, j] = gram[j, i] = splat(row, n)
            n += 1
    last = splat(row, n)
    mat = {}
    for i in range(4):
        for j in range(i + 1):
            if j == 3:
                mat[i, j] = last
            else:
                mat[i, j] = scale * gram[i, j + 1] + thetas[j] * gram[i, j]
    low, inv = {}, {}
    for j in range(4):
        pivot = mat[j, j]
        for k in range(j):
            pivot = pivot - low[j, k] * low[j, k] * mat["d", k]
        mat["d", j] = pivot
        good = pivot > 1e-7 * mat[j, j]
        inv[j] = jnp.where(good, 1.0 / jnp.where(good, pivot, 1.0), 0.0)
        for i in range(j + 1, 4):
            value = mat[i, j]
            for k in range(j):
                value = value - low[i, k] * low[j, k] * mat["d", k]
            low[i, j] = value * inv[j]
    y = []
    for i in range(4):
        value = gram[i, 0]
        for k in range(i):
            value = value - low[i, k] * y[k]
        y.append(value)
    c = [None] * 4
    for i in reversed(range(4)):
        value = y[i] * inv[i]
        for k in range(i + 1, 4):
            value = value - low[k, i] * c[k]
        c[i] = value
    return c


def pack_row(accs):
    lane = lane_iota((1, 128))
    row = jnp.zeros((1, 128), F32)
    for n, acc in enumerate(accs):
        total = jnp.sum(jnp.sum(acc, axis=0, keepdims=True), axis=1, keepdims=True)
        row = row + jnp.where(lane == n, total, 0.0)
    return row


def remote(src_ref, dst_ref, send_sem, recv_sem, target):
    return pltpu.make_async_remote_copy(
        src_ref=src_ref,
        dst_ref=dst_ref,
        send_sem=send_sem,
        recv_sem=recv_sem,
        device_id=target,
        device_id_type=MESH,
    )


def flip(src, bit):
    return src + bit - 2 * bit * (lax.rem(src // bit, 2))


def partners(me, slabs):
    near = 4
    fours = slabs // near
    place, four = lax.rem(me, near), me // near
    return (
        [four * near + lax.rem(place + d, near) for d in range(1, near)],
        [lax.rem(four + d, fours) * near + place for d in range(1, fours)],
    )


def pair_group(me):
    place = lax.rem(me, 4)
    return [me - place + lax.rem(place + d, 4) for d in range(4)]


def signal_all(src, me, slabs, others):
    barrier = pltpu.get_barrier_semaphore()
    targets = [(src, t) for group in partners(me, slabs) for t in group] + others
    for target in targets:
        pl.semaphore_signal(barrier, inc=1, device_id=target, device_id_type=MESH)
    return barrier, len(targets)


class Sum:
    def __init__(self, src, me, slabs, levels, across=None):
        groups = [[(src, t) for t in group] for group in partners(me, slabs)]
        if across is not None:
            groups[0] += [(across, t) for t in pair_group(me)]
        self.levels = [(level, group) for level, group in zip(levels, groups) if group]

    def send(self, n, value):
        (buf, send_sem, recv_sem), group = self.levels[n]
        buf[0] = value
        for d, target in enumerate(group):
            remote(buf.at[0], buf.at[d + 1], send_sem, recv_sem, target).start()

    def _wait(self, n, which):
        level, group = self.levels[n]
        rest = level[0].at[pl.ds(1, len(group))]
        pltpu.make_async_copy(rest, rest, level[which]).wait()

    def receive(self, n):
        self._wait(n, 2)
        return jnp.sum(self.levels[n][0][0][...], axis=0)

    def start(self, value):
        self.send(0, value)

    def middle(self):
        value = self.receive(0)
        if len(self.levels) > 1:
            self.send(1, value)
        return value

    def end(self, value):
        return self.receive(1) if len(self.levels) > 1 else value

    def whole(self, value):
        self.start(value)
        return self.end(self.middle())

    def close(self):
        for n in range(len(self.levels)):
            self._wait(n, 1)


def sum_scratch(slabs, shape, first=4):
    return [
        VMEM((first, *shape), F32), DMA(()), DMA(()),
        VMEM((max(slabs // 4, 2), *shape), F32), DMA(()), DMA(()),
    ]


def sum_levels(refs):
    return (refs[0:3], refs[3:6])


def first_kernel(
    slabs, lc_in, pt_in, u, u_low, u_high, tan, mean_out, lc_half, lc_near, u_mine, u_first, u_rest,
    lc, pt, lch, uh, sig, wgt, uw, dg, hx, hy, hz, v0, v1, v2, v3, pth, edge, order,
    s_load, s_take, s_c, r_c, s_x, r_x, s_core, r_core, s_v, r_v, s_e, r_e, *sums,
):
    src = lax.axis_index("src")
    me = lax.axis_index("slab")
    depth, nx, cols = lc.shape
    half = nx // 2
    has_low = me > 0
    has_high = me < slabs - 1
    core, side_x = lax.rem(src, 2), src // 2
    mate, across = flip(src, 1), flip(src, 2)
    inner_rows = pl.ds(PAD, nx)
    loads = [
        pltpu.make_async_copy(u, uw.at[pl.ds(1, depth), inner_rows], s_load.at[0]),
        pltpu.make_async_copy(lc_in, lc, s_load.at[1]),
        pltpu.make_async_copy(pt_in, pt, s_load.at[2]),
    ]
    for load in loads:
        load.start()
    ring = [(src, lax.rem(me + 1, slabs)), (src, lax.rem(me + slabs - 1, slabs))]
    barrier, count = signal_all(src, me, slabs, ring + [(mate, me), (across, me)])
    order[...] = order_matrix(cols, False)

    def shuffle(q, carry):
        for n in (0, 1):
            for ref, plane, first in ((lc, q, 0), (pt, q, 0), (uw, q + 1, PAD)):
                rows = pl.ds(first + n * half, half)
                ref[plane, rows, :] = reorder(ref[plane, rows, :], order[...])
        return carry

    for load in loads:
        load.wait()
    lax.fori_loop(0, 2, lambda i, c: shuffle(i * (depth - 1), c), 0)
    for side, ref in ((0, u_low), (1, u_high)):
        for n in (0, 1):
            rows = pl.ds(n * half, half)
            uh[side, rows, :] = reorder(ref[0, rows, :], order[...])
    pl.semaphore_wait(barrier, count)
    mean_sum = Sum(src, me, slabs, sum_levels(sums[0:6]))
    mom_sum = Sum(src, me, slabs, sum_levels(sums[6:12]))

    def arrives(side):
        return has_low if side == 0 else has_high

    def below(side):
        return me + 1 if side == 0 else me - 1

    def sends(side):
        return has_high if side == 0 else has_low

    def near(side):
        return depth - 1 if side == 0 else 0

    def part(n):
        return pl.ds(n * half, half)

    my_rows = pl.ds(pl.multiple_of(half * side_x, PAD), half)
    their_rows = pl.ds(pl.multiple_of(half * (1 - side_x), PAD), half)

    def copy_c(ref, dst, side, to):
        return remote(
            ref.at[near(side), my_rows], dst.at[side, my_rows], s_c.at[side], r_c.at[side], (src, to)
        )

    def swap(ref, side, rows):
        return remote(ref.at[side, rows], ref.at[side, rows], s_x.at[side], r_x.at[side], (across, me))

    def forward(ref, side):
        return remote(ref.at[side], ref.at[side], s_core.at[side], r_core.at[side], (mate, me))

    def by_core(body):
        pl.when(core == 0)(lambda: body(lc, lch))
        pl.when(core == 1)(lambda: body(pt, pth))

    for side in (0, 1):
        @pl.when(sends(side))
        def _():
            by_core(lambda ref, dst: copy_c(ref, dst, side, below(side)).start())

    for ref in (sig, wgt, uw, hy, v0, v1, v2, v3):
        zero_pads(ref, nx)
    def own(q, acc):
        for r, rows in chunks(nx):
            value = jnp.exp(lc[q, pl.ds(r, rows), :])
            sig[q + 1, pl.ds(PAD + r, rows), :] = value
            wgt[q + 1, pl.ds(PAD + r, rows), :] = value * pt[q, pl.ds(r, rows), :]
            acc = acc + fold(value)
        return acc

    lax.fori_loop(1, depth - 1, shuffle, 0)
    acc = lax.fori_loop(0, depth, own, jnp.zeros((8, cols), F32))
    mean_sum.start(pack_row([acc]))

    fields = (v0, v1, v2, v3)
    for ref in fields:
        for side in (0, 1):
            def clear(ref=ref, side=side):
                ref[side * (depth + 1), pl.ds(PAD, nx), :] = jnp.zeros((nx, cols), F32)

            if ref is v3:
                clear()
            else:
                pl.when(jnp.logical_not(arrives(side)))(clear)
    mean_part = mean_sum.middle()

    for side in (0, 1):
        @pl.when(arrives(side))
        def _():
            def body(ref, dst):
                copy_c(ref, dst, side, me).wait_recv()
                swap(dst, side, my_rows).start()

            by_core(body)
    for side in (0, 1):
        @pl.when(arrives(side))
        def _():
            def body(ref, dst):
                swap(dst, side, their_rows).wait_recv()
                forward(dst, side).start()

            by_core(body)

    def rhs_rows(q, pieces):
        for r, rows in pieces:
            c = wgt[q + 1, pl.ds(PAD + r, rows), :]
            f = uw[q + 1, pl.ds(PAD + r, rows), :]
            lane = lane_iota(c.shape)
            cr = jnp.where(lane == cols - 1, 0.0, next_lane(c))
            fr = jnp.where(lane == cols - 1, 0.0, next_lane(f))
            flow = (c + cr) * (f - fr)
            total = flow + jnp.where(lane == 0, c * f, -prev_lane(flow))
            for dq, dr in ((0, 1), (0, -1), (1, 0), (-1, 0)):
                cj = wgt[q + 1 + dq, pl.ds(PAD + r + dr, rows), :]
                fj = uw[q + 1 + dq, pl.ds(PAD + r + dr, rows), :]
                total = total + (c + cj) * (f - fj)
            v0[q + 1, pl.ds(PAD + r, rows), :] = -0.5 * total

    def copy_v(k, side, n, to):
        plane = depth if side == 0 else 1
        halo = 0 if side == 0 else depth + 1
        rows = pl.ds(PAD + n * half, half)
        ref = fields[k]
        return remote(
            ref.at[plane, rows], ref.at[halo, rows], s_v.at[k, side, n], r_v.at[k, side, n], (src, to)
        )

    def send_edge(k, side, n):
        out = 1 - side

        @pl.when(sends(out))
        def _():
            copy_v(k, out, n, below(out)).start()

    for n in (0, 1):
        for side in (0, 1):
            plane = 0 if side == 0 else depth + 1

            @pl.when(arrives(side))
            def _():
                if n == 0:
                    pl.when(core == 0)(lambda: forward(pth, side).wait_recv())
                    pl.when(core == 1)(lambda: forward(lch, side).wait_recv())
                for r, rows in chunks(half, n * half):
                    value = jnp.exp(lch[side, pl.ds(r, rows), :])
                    sig[plane, pl.ds(PAD + r, rows), :] = value
                    wgt[plane, pl.ds(PAD + r, rows), :] = value * pth[side, pl.ds(r, rows), :]
                    uw[plane, pl.ds(PAD + r, rows), :] = uh[side, pl.ds(r, rows), :]

            @pl.when(jnp.logical_not(arrives(side)))
            def _():
                for ref in (sig, wgt, uw):
                    ref[plane, pl.ds(PAD + n * half, half), :] = jnp.zeros((half, cols), F32)
                lch[side, part(n), :] = jnp.zeros((half, cols), F32)

            rhs_rows(0 if side == 0 else depth - 1, chunks(half, n * half))
            send_edge(0, side, n)

    frame_rows = half + PAD
    mine = half * side_x - PAD * side_x
    theirs = (half - PAD) - mine
    takes = []
    for n, (ref, dst, first, at) in enumerate((
        (lc, lc_half, 0, mine),
        (lch, lc_near, 0, mine),
        (uw, u_mine, 0, PAD + mine),
        (uw, u_first, 0, PAD + theirs),
        (uw, u_rest, EARLY, PAD + theirs),
    )):
        rows = pl.ds(pl.multiple_of(at, PAD), frame_rows)
        takes.append(pltpu.make_async_copy(ref.at[pl.ds(first, dst.shape[0]), rows], dst, s_take.at[n]))
    for take in takes:
        take.start()

    def inner(body, carry):
        return lax.fori_loop(1, depth - 1, body, carry)

    def rhs_plane(q, carry):
        rhs_rows(q, chunks(nx))
        return carry

    inner(rhs_plane, 0)
    first, last = -me * depth, (slabs - me) * depth - 1
    make_coefs(sig, dg, hx, hy, hz, 0, depth, first, last, chunks(nx))

    mean = splat(mean_sum.end(mean_part), 0) * (1.0 / (slabs * depth * nx * cols))
    mean_out[...] = jnp.broadcast_to(mean, (8, 128))
    scale = 6.0 * mean
    inv = 1.0 / scale

    zero = jnp.zeros((8, cols), F32)
    dots = []
    for k in range(3):
        shift = THETA[k] * mean * inv

        def step(q, accs, pieces=None, k=k, shift=shift):
            accs = list(accs)
            for r, rows in pieces or chunks(nx):
                here, image = operator(fields[k], q + 1, dg, hx, hy, hz, q, r, rows)
                new = inv * image - shift * here
                fields[k + 1][q + 1, pl.ds(PAD + r, rows), :] = new
                if k == 0:
                    accs[0] = accs[0] + fold(here * here)
                for i in range(k + 1):
                    other = here if i == k else fields[i][q + 1, pl.ds(PAD + r, rows), :]
                    accs[i + (k == 0)] = accs[i + (k == 0)] + fold(new * other)
                accs[-1] = accs[-1] + fold(new * new)
            return tuple(accs)

        accs = inner(step, (zero,) * (3 if k == 0 else k + 2))
        for n in (0, 1):
            for side in (0, 1):
                pl.when(arrives(side))(lambda side=side, n=n, k=k: copy_v(k, side, n, me).wait_recv())
                accs = step(0 if side == 0 else depth - 1, accs, chunks(half, n * half))
                if k < 2:
                    send_edge(k + 1, side, n)
        dots.extend(accs)

    def copy_edge(side, to):
        plane = depth if side == 0 else 1
        return remote(
            v3.at[plane, pl.ds(PAD + side * half, half)], edge.at[side], s_e.at[side], r_e.at[side], (src, to)
        )

    for side in (0, 1):
        pl.when(sends(side))(lambda side=side: copy_edge(side, below(side)).start())
    def energy(q, acc):
        for r, rows in chunks(nx):
            here, image = operator(v3, q + 1, dg, hx, hy, hz, q, r, rows)
            acc = acc + fold(here * image)
        return acc

    acc = lax.fori_loop(0, depth, energy, zero)
    for side in (0, 1):
        got = arrives(side)
        pl.when(got)(lambda side=side: copy_edge(side, me).wait_recv())

        @pl.when(jnp.logical_not(got))
        def _():
            edge[side] = jnp.zeros((half, cols), F32)

        for r, rows in chunks(half):
            at = side * half + r
            face = hz[side * depth, pl.ds(at, rows), :] * v3[1 + side * (depth - 1), pl.ds(PAD + at, rows), :]
            acc = acc - 2.0 * fold(face * edge[side, pl.ds(r, rows), :])
    dots.append(acc)
    mom_sum.start(pack_row(dots))
    value = mom_sum.middle()

    row = mom_sum.end(value)
    c = solve_small(row, scale, [t * mean for t in THETA])

    def combine(q, carry):
        for r, rows in chunks(nx):
            value = c[0] * v0[q + 1, pl.ds(PAD + r, rows), :]
            for i in (1, 2, 3):
                value = value + c[i] * fields[i][q + 1, pl.ds(PAD + r, rows), :]
            tan[q, pl.ds(r, rows), :] = value
        return carry

    lax.fori_loop(0, depth, combine, 0)

    for take in takes:
        take.wait()
    for side in (0, 1):
        @pl.when(sends(side))
        def _():
            copy_c(lc, lch, side, me).wait_send()
            copy_edge(side, me).wait_send()
            for n in (0, 1):
                for k in range(3):
                    copy_v(k, side, n, me).wait_send()

        @pl.when(arrives(side))
        def _():
            swap(lch, side, my_rows).wait_send()
            forward(lch, side).wait_send()
    mean_sum.close()
    mom_sum.close()


def first_solve(slabs, lc, pt, u, u_low, u_high):
    depth, nx, cols = lc.shape
    plane = (nx + 2 * PAD, cols)
    half = nx // 2
    full = pl.BlockSpec(memory_space=VMEM)
    pair = (DMA((2,)), DMA((2,)))
    return pl.pallas_call(
        functools.partial(first_kernel, slabs),
        name="first_solve",
        out_shape=[
            jax.ShapeDtypeStruct((depth, nx, cols), F32),
            jax.ShapeDtypeStruct((8, 128), F32),
            *(
                jax.ShapeDtypeStruct((planes, half + PAD, cols), F32)
                for planes in (depth, 2, depth + 2, EARLY, depth + 2 - EARLY)
            ),
        ],
        in_specs=[pl.BlockSpec(memory_space=pltpu.HBM)] * 3 + [full] * 2,
        out_specs=[full] * 7,
        scratch_shapes=[VMEM((depth, nx, cols), F32)] * 2
        + [VMEM((2, nx, cols), F32)] * 2
        + [VMEM((depth + 2, *plane), F32)] * 3
        + [
            VMEM((depth, nx, cols), F32),
            VMEM((depth, nx, cols), F32),
            VMEM((depth, *plane), F32),
            VMEM((depth + 1, nx, cols), F32),
        ]
        + [VMEM((depth + 2, *plane), F32)] * 4
        + [VMEM((2, nx, cols), F32), VMEM((2, half, cols), F32), VMEM((cols, cols), jnp.bfloat16)]
        + [DMA((3,)), DMA((5,)), *pair, *pair, *pair]
        + [DMA((3, 2, 2)), DMA((3, 2, 2)), *pair]
        + sum_scratch(slabs, (1, 128)) * 2,
        compiler_params=pltpu.CompilerParams(
            collective_id=0, has_side_effects=True, vmem_limit_bytes=43 << 20
        ),
    )(lc, pt, u, u_low, u_high)


def over_window(group, ordered, first_key, last_key, keys, cells, keys_s, cells_s, sems, body):
    start, stop = (
        jnp.sum(jnp.where(ordered[...] < bound, 1.0, 0.0)).astype(jnp.int32) for bound in (first_key, last_key)
    )
    size = keys_s.shape[0]

    def piece(w, carry):
        base = pl.multiple_of(w * size, size)
        copies = [
            pltpu.make_async_copy(ref.at[pl.ds(base, size)], dst, sems.at[n])
            for n, (ref, dst) in enumerate(((keys, keys_s), (cells, cells_s)))
        ]
        for copy in copies:
            copy.start()
        for copy in copies:
            copy.wait()
        low = jnp.maximum(start - base, 0)
        high = jnp.minimum(stop - base, size)

        def step(g, carry):
            body(low + g * group, high)
            return carry

        return lax.fori_loop(0, (high - low + group - 1) // group, step, carry)

    lax.fori_loop(start // size, (stop + size - 1) // size, piece, 0)


def window_scratch(entries):
    size = min(1024, entries)
    return [SMEM((size,), jnp.int32), SMEM((size,), jnp.int32), DMA((2,))]


def bits(count):
    assert count & (count - 1) == 0
    return count.bit_length() - 1


def gather_kernel(group, depth, dipoles, ordered, keys, cells, field, out, keys_s, cells_s, sems):
    me = lax.axis_index("slab")
    out[...] = jnp.zeros_like(out)
    lines, cols = field.shape
    nx = lines // depth
    entries = 2 * dipoles
    lane = lane_iota((1, cols))
    short = lane_iota((1, 128))
    base = me * lines

    def body(least, stop):
        parts = []
        j = jnp.minimum(least, keys_s.shape[0] - group)
        for e in range(group):
            key, cell = keys_s[j + e], cells_s[j + e]
            o = key & (entries - 1)
            k = o & (dipoles - 1)
            line = ((key >> bits(entries)) << bits(nx)) + (cell >> bits(cols)) - base
            inside = jnp.logical_and(j + e >= least, j + e < stop)
            lane_at = jnp.where(inside, lane_of(cell & (cols - 1), cols), -1)
            picked = jnp.where(lane == lane_at, field[pl.ds(jnp.where(inside, line, 0), 1), :], 0.0)
            value = jnp.sum(picked, axis=1, keepdims=True)
            value = jnp.where(o < dipoles, value, -value)
            parts.append((k >> 7, jnp.where(short == (k & 127), value, 0.0)))
        for line, value in parts:
            out[pl.ds(line, 1), :] = out[pl.ds(line, 1), :] + value

    first = me * depth * entries
    over_window(group, ordered, first, first + depth * entries, keys, cells, keys_s, cells_s, sems, body)


def gather(keys, cells, field, depth):
    anywhere = pl.BlockSpec(memory_space=pl.ANY)
    full = pl.BlockSpec(memory_space=VMEM)
    entries = keys.shape[0]
    return pl.pallas_call(
        functools.partial(gather_kernel, 16, depth, entries // 2),
        name="gather",
        out_shape=jax.ShapeDtypeStruct((entries // 256, 128), F32),
        in_specs=[full, anywhere, anywhere, full],
        out_specs=full,
        scratch_shapes=window_scratch(entries),
        compiler_params=pltpu.CompilerParams(vmem_limit_bytes=8 << 20),
    )(keys.reshape(-1, 128), keys, cells, field)


def share_kernel(slabs, part, out, s_x, r_x, *sums):
    src = lax.axis_index("src")
    me = lax.axis_index("slab")
    side_x = src // 2
    across = flip(src, 2)
    barrier, count = signal_all(src, me, slabs, [(across, me)])
    pl.semaphore_wait(barrier, count)
    total = Sum(src, me, slabs, sum_levels(sums))
    out[side_x] = total.whole(part[...])
    copy = remote(out.at[side_x], out.at[side_x], s_x, r_x, (across, me))
    copy.start()
    copy.wait()
    total.close()


def share(slabs, part):
    full = pl.BlockSpec(memory_space=VMEM)
    return pl.pallas_call(
        functools.partial(share_kernel, slabs),
        name="share_data",
        out_shape=jax.ShapeDtypeStruct((2, *part.shape), F32),
        in_specs=[full],
        out_specs=full,
        scratch_shapes=[DMA(()), DMA(())] + sum_scratch(slabs, part.shape),
        compiler_params=pltpu.CompilerParams(
            collective_id=1, has_side_effects=True, vmem_limit_bytes=8 << 20
        ),
    )(part)


def scatter_kernel(group, depth, nx, lines, ordered, keys, cells, data, out0, out1, keys_s, cells_s, sems):
    me = lax.axis_index("slab")
    side_x = lax.axis_index("src") // 2
    outs = (out0, out1)
    total, cols = out0.shape
    planes = total // lines
    entries = keys.shape[0]
    dipoles = entries // 2
    lane = lane_iota((1, cols))
    low = me * depth - WIDE
    row_base = (nx // 2) * side_x - 2 * PAD
    plane_base = low * lines + row_base

    def clear(q, carry):
        for out in outs:
            out[pl.ds(pl.multiple_of(q * lines, 8), lines), :] = jnp.zeros((lines, cols), F32)
        return carry

    lax.fori_loop(0, planes, clear, 0)

    def body(least, stop):
        parts = []
        j = jnp.minimum(least, keys_s.shape[0] - group)
        for e in range(group):
            key, cell = keys_s[j + e], cells_s[j + e]
            o = key & (entries - 1)
            k = o & (dipoles - 1)
            row = cell >> bits(cols)
            inside = jnp.logical_and(j + e >= least, j + e < stop)
            inside = jnp.logical_and(inside, jnp.logical_and(row >= row_base + PAD, row < row_base + lines - PAD))
            hit = lane == jnp.where(inside, lane_of(cell & (cols - 1), cols), -1)
            at = jnp.where(inside, (key >> bits(entries)) * lines + row - plane_base, 0)
            sign = jnp.where(o < dipoles, 1.0, -1.0)
            parts.append((at, [jnp.where(hit, data[k + n * dipoles] * sign, 0.0) for n in (0, 1)]))
        for at, values in parts:
            for out, value in zip(outs, values):
                out[pl.ds(at, 1), :] = out[pl.ds(at, 1), :] + value

    over_window(
        group, ordered, low * entries, (low + planes) * entries, keys, cells, keys_s, cells_s, sems, body
    )


def scatter(keys, cells, data, depth, nx, cols):
    smem = pl.BlockSpec(memory_space=SMEM)
    anywhere = pl.BlockSpec(memory_space=pl.ANY)
    full = pl.BlockSpec(memory_space=VMEM)
    lines = nx // 2 + 4 * PAD
    planes = depth + 2 * WIDE
    back = pl.pallas_call(
        functools.partial(scatter_kernel, 8, depth, nx, lines),
        name="scatter",
        out_shape=[jax.ShapeDtypeStruct((planes * lines, cols), F32)] * 2,
        in_specs=[full, anywhere, anywhere, smem],
        out_specs=[full, full],
        scratch_shapes=window_scratch(keys.shape[0]),
        compiler_params=pltpu.CompilerParams(vmem_limit_bytes=8 << 20),
    )(keys.reshape(-1, 128), keys, cells, data.reshape(-1))
    return [ref.reshape(planes, lines, cols) for ref in back]


def second_kernel(
    slabs, nx, lc_half, lc_near, u_mine, u_first, u_rest, mean_in, v00, v01, out,
    sig, dg, hx, hy, hz, v1, v2, v3, u2, adj, give, take, pair, far, order,
    s_load, s_u, r_u, s_far, r_far, s_c2, r_c2, s_give, r_give, s_x, r_x, s_own, r_own, s_fwd, r_fwd,
    *sums,
):
    src = lax.axis_index("src")
    me = lax.axis_index("slab")
    depth, _, cols = out.shape
    half = nx // 2
    frame = half + 2 * PAD
    frame_rows = half + PAD
    quarter = depth // 2
    core, side_x = lax.rem(src, 2), src // 2
    mate, across = flip(src, 1), flip(src, 2)
    wide = depth + 2 * WIDE
    ring = [(src, lax.rem(me + 1, slabs)), (src, lax.rem(me + slabs - 1, slabs))]
    barrier, count = signal_all(src, me, slabs, ring + [(mate, me)] + [(across, t) for t in pair_group(me)])
    total = Sum(src, me, slabs, sum_levels(sums), across)
    order[...] = order_matrix(cols, True)
    owned = chunks(half, PAD)
    rims = [(0, PAD), (PAD + half, PAD)]
    every = rims[:1] + owned + rims[1:]

    zero_pads(sig, frame)
    zero_pads(hy, frame)
    for ref in (v1, v2, v3):
        for j in (0, 1):
            zero_pads(ref.at[j], frame)

    outside = pl.ds(pl.multiple_of(PAD + (half + PAD) * side_x, PAD), PAD)
    u2[:, :, pl.ds(pl.multiple_of((half + PAD) * side_x, PAD), PAD), :] = jnp.zeros((2, depth + 2, PAD, cols), F32)
    frame_mine = pl.ds(pl.multiple_of(PAD * (1 - side_x), PAD), frame_rows)
    frame_theirs = pl.ds(pl.multiple_of(PAD * side_x, PAD), frame_rows)
    early = pl.ds(0, EARLY)
    late = pl.ds(EARLY, depth + 2 - EARLY)
    loads = [
        pltpu.make_async_copy(u_mine, u2.at[side_x, :, frame_mine], s_load.at[0]),
        pltpu.make_async_copy(u_first, u2.at[1 - side_x, early, frame_mine], s_load.at[1]),
    ]
    for load in loads:
        load.start()
    low_in, high_in = (me > 0).astype(F32), (me < slabs - 1).astype(F32)

    def conductivity(ref, count, first, factor=None):
        def body(n, carry):
            for r, rows in chunks(frame_rows):
                to = pl.multiple_of(PAD + PAD * (1 - side_x) + r, PAD)
                value = jnp.exp(ref[n, pl.ds(r, rows), :])
                sig[first + 1 + n, pl.ds(to, rows), :] = value if factor is None else factor * value
            sig[first + 1 + n, outside, :] = jnp.zeros((PAD, cols), F32)
            return carry

        lax.fori_loop(0, count, body, 0)

    conductivity(lc_half, depth, WIDE)
    conductivity(lc_near, 1, WIDE - 1, low_in)
    conductivity(lc_near.at[pl.ds(1, 1)], 1, WIDE + depth, high_in)

    arrives = (me > 0, me < slabs - 1)
    sends = (me < slabs - 1, me > 0)
    to_slab = (me + 1, me - 1)
    part = -(-frame_rows // (2 * PAD)) * PAD
    fetched = pl.ds(pl.multiple_of((frame_rows - part) * core, PAD), part)
    given = pl.ds(pl.multiple_of(part * core, PAD), frame_rows - part)
    taken = pl.ds(pl.multiple_of(part * (1 - core), PAD), frame_rows - part)

    def copy_far(side, to):
        planes = pl.ds(depth - WIDE if side == 0 else 1, WIDE - 1)
        return remote(lc_half.at[planes, fetched], far.at[side, :, fetched], s_far.at[side], r_far.at[side], (src, to))

    def share_far(side, rows):
        ref = far.at[side, :, rows]
        return remote(ref, ref, s_c2.at[side], r_c2.at[side], (mate, me))

    copy_rest = remote(u_rest, u2.at[side_x, late, frame_theirs], s_u, r_u, (across, me))
    pl.semaphore_wait(barrier, count)
    for side in (0, 1):
        pl.when(sends[side])(lambda side=side: copy_far(side, to_slab[side]).start())
    copy_rest.start()

    first, last = WIDE - me * depth, WIDE + (slabs - me) * depth - 1
    low_open, high_open = side_x.astype(F32), 1.0 - side_x.astype(F32)

    def coefs(start, stop, top=True):
        make_coefs(sig, dg, hx, hy, hz, start, stop, first, last, every, top)

        def close(q, carry):
            for line, factor in ((2 * PAD - 1, low_open), (2 * PAD + half - 1, high_open)):
                hy[q, pl.ds(line, 1), :] = hy[q, pl.ds(line, 1), :] * factor
            return carry

        lax.fori_loop(start, stop, close, 0)

    mean = mean_in[0:1, 0:1]
    scale = 6.0 * mean
    inv = 1.0 / scale
    zero = jnp.zeros((8, cols), F32)
    fields = [(v0, v1.at[j], v2.at[j], v3.at[j]) for j, v0 in enumerate((v00, v01))]
    sums_of = {}

    def run(k, start, stop, dotted):
        shift = THETA[k] * mean * inv
        for j in (0, 1):
            def step(q, accs, j=j):
                accs = list(accs)
                for r, rows in every:
                    here, image = operator(fields[j][k], q - k, dg, hx, hy, hz, q, r, rows)
                    new = inv * image - shift * here
                    fields[j][k + 1][q - k - 1, pl.ds(PAD + r, rows), :] = new
                    if not dotted or (r, rows) not in owned:
                        continue
                    if k == 0:
                        accs[0] = accs[0] + fold(here * here)
                    for i in range(k + 1):
                        other = here if i == k else fields[j][i][q - i, pl.ds(PAD + r, rows), :]
                        accs[i + (k == 0)] = accs[i + (k == 0)] + fold(new * other)
                    accs[-1] = accs[-1] + fold(new * new)
                return tuple(accs)

            accs = sums_of.get((j, k), (zero,) * (3 if k == 0 else k + 2)) if dotted else ()
            accs = lax.fori_loop(start, stop, step, accs)
            if dotted:
                sums_of[j, k] = accs

    top = WIDE + depth
    coefs(WIDE, top)
    run(0, WIDE, top, True)
    run(1, WIDE + 1, top - 1, True)
    for side in (0, 1):
        @pl.when(arrives[side])
        def _():
            copy_far(side, me).wait_recv()
            share_far(side, given).start()

        @pl.when(jnp.logical_not(arrives[side]))
        def _():
            far[side] = jnp.zeros(far.shape[1:], F32)

    run(2, WIDE + 2, top - 2, True)
    for side in (0, 1):
        pl.when(arrives[side])(lambda side=side: share_far(side, taken).wait_recv())
    conductivity(far.at[0], WIDE - 1, 0, low_in)
    conductivity(far.at[1], WIDE - 1, top + 1, high_in)
    coefs(1, WIDE, False)
    coefs(top, wide - 1)
    for k in range(3):
        run(k, k + 1, WIDE, False)
        if k:
            run(k, WIDE, WIDE + k, True)
            run(k, top - k, top, True)
        run(k, top, wide - k - 1, False)
    dots = [[acc for k in range(3) for acc in sums_of[j, k]] for j in (0, 1)]

    for j in (0, 1):
        def energy(q, acc, j=j):
            for r, rows in owned:
                here, image = operator(v3.at[j], q + 1, dg, hx, hy, hz, q + WIDE, r, rows)
                acc = acc + fold(here * image)
            return acc

        dots[j].append(lax.fori_loop(0, depth, energy, zero))

    row = total.whole(pack_row(dots[0] + dots[1]))
    thetas = [t * mean for t in THETA]
    coef = [solve_small(row, scale, thetas, n) for n in (0, len(dots[0]))]

    def combine(q, carry):
        for j in (0, 1):
            c = coef[j]
            for r, rows in every:
                value = c[3] * v3[j, q, pl.ds(PAD + r, rows), :]
                for i, ref in enumerate(fields[j][:3]):
                    value = value + c[i] * ref[q + 3 - i, pl.ds(PAD + r, rows), :]
                adj[j, q, pl.ds(r, rows), :] = value
        return carry

    lax.fori_loop(0, depth + 2, combine, 0)
    for load in loads:
        load.wait()
    copy_rest.wait()
    for side in (0, 1):
        pl.when(sends[side])(lambda side=side: copy_far(side, me).wait_send())
        pl.when(arrives[side])(lambda side=side: share_far(side, given).wait_send())

    def partial(q, dst, slot):
        for r, rows in owned:
            total = jnp.zeros((rows, cols), F32)
            for j in (0, 1):
                f = u2[j, q + 1, pl.ds(r, rows), :]
                a = adj[j, q + 1, pl.ds(r, rows), :]
                lane = lane_iota(f.shape)
                fr = jnp.where(lane == cols - 1, 0.0, next_lane(f))
                ar = jnp.where(lane == cols - 1, 0.0, next_lane(a))
                flow = (f - fr) * (a - ar)
                total = total + (flow + jnp.where(lane == 0, f * a, prev_lane(flow)))
                for dq, dr in ((0, 1), (0, -1), (1, 0), (-1, 0)):
                    fj = u2[j, q + 1 + dq, pl.ds(r + dr, rows), :]
                    aj = adj[j, q + 1 + dq, pl.ds(r + dr, rows), :]
                    total = total + (f - fj) * (a - aj)
            scaled = -0.5 * sig[q + WIDE + 1, pl.ds(PAD + r, rows), :] * total
            dst[slot, pl.ds(r - PAD, rows), :] = scaled

    def copy_give(n):
        return remote(give.at[n], take.at[n], s_give.at[n], r_give.at[n], (mate, me))

    rows_mine = pl.ds(pl.multiple_of(half * side_x, PAD), half)
    rows_theirs = pl.ds(pl.multiple_of(half * (1 - side_x), PAD), half)

    def copy_x(n):
        ref = out.at[core * quarter + n, rows_mine]
        return remote(ref, ref, s_x.at[n], r_x.at[n], (across, me))

    def copy_own(n):
        ref = out.at[core * quarter + n, rows_mine]
        return remote(ref, ref, s_own.at[n], r_own.at[n], (mate, me))

    def copy_fwd(n):
        ref = out.at[core * quarter + n, rows_theirs]
        return remote(ref, ref, s_fwd.at[n], r_fwd.at[n], (mate, me))

    def giving(n, carry):
        partial((1 - core) * quarter + n, give, n)
        copy_give(n).start()
        return carry

    def keeping(n, carry):
        partial(core * quarter + n, pair, n)
        copy_give(n).wait_recv()
        for r, rows in ((0, half),):
            at = pl.multiple_of(half * side_x + r, PAD)
            value = pair[n, pl.ds(r, rows), :] + take[n, pl.ds(r, rows), :]
            out[core * quarter + n, pl.ds(at, rows), :] = reorder(value, order[...])
        copy_x(n).start()
        copy_own(n).start()
        return carry

    def passing(n, carry):
        copy_x(n).wait_recv()
        copy_fwd(n).start()
        return carry

    def ending(n, carry):
        copy_own(n).wait_recv()
        copy_fwd(n).wait_recv()
        for copy in (copy_give, copy_x, copy_own, copy_fwd):
            copy(n).wait_send()
        return carry

    def in_turn(n, carry):
        giving(n + 1, carry)
        return keeping(n, carry)

    giving(0, 0)
    lax.fori_loop(0, quarter - 1, in_turn, 0)
    keeping(quarter - 1, 0)
    for body in (passing, ending):
        lax.fori_loop(0, quarter, body, 0)
    total.close()


def second_solve(slabs, nx, lc_half, lc_near, u_mine, u_first, u_rest, mean, back):
    depth, _, cols = lc_half.shape
    half = nx // 2
    frame = half + 2 * PAD
    plane = (frame + 2 * PAD, cols)
    wide = depth + 2 * WIDE
    quarter = depth // 2
    full = pl.BlockSpec(memory_space=VMEM)
    anywhere = pl.BlockSpec(memory_space=pl.ANY)
    pair = [DMA((2,)), DMA((2,))]
    return pl.pallas_call(
        functools.partial(second_kernel, slabs, nx),
        name="second_solve",
        out_shape=jax.ShapeDtypeStruct((depth, nx, cols), F32),
        in_specs=[full, full, anywhere, anywhere, anywhere, full, full, full],
        out_specs=full,
        scratch_shapes=[
            VMEM((wide + 2, *plane), F32),
            VMEM((wide, frame, cols), F32),
            VMEM((wide, frame, cols), F32),
            VMEM((wide, *plane), F32),
            VMEM((wide + 1, frame, cols), F32),
            VMEM((2, wide - 2, *plane), F32),
            VMEM((2, wide - 4, *plane), F32),
            VMEM((2, wide - 6, *plane), F32),
            VMEM((2, depth + 2, frame, cols), F32),
            VMEM((2, depth + 2, frame, cols), F32),
        ]
        + [VMEM((quarter, half, cols), F32)] * 3
        + [VMEM((2, WIDE - 1, half + PAD, cols), F32), VMEM((cols, cols), jnp.bfloat16)]
        + [DMA((2,)), DMA(()), DMA(())]
        + pair * 2
        + [DMA((quarter,))] * 8
        + sum_scratch(slabs, (1, 128), 8),
        compiler_params=pltpu.CompilerParams(
            collective_id=2, has_side_effects=True, vmem_limit_bytes=42 << 20
        ),
    )(lc_half, lc_near, u_mine, u_first, u_rest, mean, *back)


def shards(slabs, log_cond, perturb, potentials, rec_depth, rec_plan):
    depth, nx, cols = log_cond.shape
    dipoles = rec_depth.shape[1]
    order = lax.broadcasted_iota(jnp.int32, rec_depth.shape, 0) * dipoles
    order = order + lax.broadcasted_iota(jnp.int32, rec_depth.shape, 1)
    keys = (rec_depth * (2 * dipoles) + order).reshape(-1)
    keys, cells = lax.sort((keys, rec_plan.reshape(-1)), num_keys=1, is_stable=False)
    up = [(i, i + 1) for i in range(slabs - 1)]
    u_low = lax.ppermute(potentials[0, depth - 1 :], "slab", up)
    u_high = lax.ppermute(potentials[0, :1], "slab", [(j, i) for i, j in up])
    arguments = (pltpu.with_memory_space_constraint(a, pltpu.HBM) for a in (log_cond, perturb, potentials[0]))
    tangent, mean, lc_half, lc_near, u_mine, u_first, u_rest = first_solve(
        slabs, *arguments, u_low, u_high
    )
    part = gather(keys, cells, tangent.reshape(depth * nx, cols), depth)
    data = share(slabs, part)
    u_first, data = lax.optimization_barrier((u_first, data))
    u_first = lax.ppermute(u_first, "src", [(i, (i + 2) % 4) for i in range(4)])
    back = scatter(keys, cells, data, depth, nx, cols)
    return second_solve(slabs, nx, lc_half, lc_near, u_mine, u_first, u_rest, mean, back)


def solution(mesh):
    in_specs = (
        P("slab", None, None),
        P("slab", None, None),
        P("src", "slab", None, None),
        P(),
        P(),
    )
    return jax.shard_map(
        functools.partial(shards, mesh.shape["slab"]),
        mesh=mesh,
        in_specs=in_specs,
        out_specs=P("slab", None, None),
        check_vma=False,
    )
```

```python
import functools

import jax
import jax.numpy as jnp
from jax import lax
from jax.experimental import pallas as pl
from jax.experimental.pallas import tpu as pltpu
from jax.sharding import PartitionSpec as P

MESH = pl.DeviceIdType.MESH
F32 = jnp.float32
VMEM = pltpu.VMEM
SMEM = pltpu.SMEM
DMA = pltpu.SemaphoreType.DMA
PAD = 8
WIDE = 4
EARLY = 4
ROWS = 64
THETA = (6.0, 2.0, 10.0)


def lane_iota(shape):
    return lax.broadcasted_iota(jnp.int32, shape, len(shape) - 1)


def fold(value):
    rows, cols = value.shape
    return jnp.sum(value.reshape(rows // 8, 8, cols), axis=0)


def next_lane(value):
    half = value.shape[1] // 2
    even, odd = value[:, :half], value[:, half:]
    return jnp.concatenate([odd, pltpu.roll(even, half - 1, 1)], axis=1)


def prev_lane(value):
    half = value.shape[1] // 2
    even, odd = value[:, :half], value[:, half:]
    return jnp.concatenate([pltpu.roll(odd, 1, 1), even], axis=1)


def lane_of(column, cols):
    return (column >> 1) + (column & 1) * (cols // 2)


def order_matrix(cols, back):
    row = lax.broadcasted_iota(jnp.int32, (cols, cols), 0)
    col = lax.broadcasted_iota(jnp.int32, (cols, cols), 1)
    hit = row == lane_of(col, cols) if back else col == lane_of(row, cols)
    return jnp.where(hit, 1.0, 0.0).astype(jnp.bfloat16)


def reorder(value, matrix):
    total = None
    for _ in range(3):
        piece = value.astype(jnp.bfloat16)
        value = value - piece.astype(F32)
        moved = jnp.dot(piece, matrix, preferred_element_type=F32)
        total = moved if total is None else total + moved
    return total


def chunks(count, start=0):
    out = []
    done = 0
    while done < count:
        rows = min(ROWS, count - done)
        out.append((start + done, rows))
        done += rows
    return out


def make_coefs(sig, dg, hx, hy, hz, start, stop, first, last, pieces, top=True):
    cols = sig.shape[-1]

    def body(q, carry):
        low_in = jnp.logical_and(q - 1 >= first, q <= last).astype(F32)
        for r, rows in pieces:
            here = sig[q + 1, pl.ds(PAD + r, rows), :]
            up = sig[q + 1, pl.ds(PAD + r + 1, rows), :]
            down = sig[q + 1, pl.ds(PAD + r - 1, rows), :]
            low = sig[q, pl.ds(PAD + r, rows), :]
            high = sig[q + 2, pl.ds(PAD + r, rows), :]
            lane = lane_iota(here.shape)
            right = jnp.where(lane == cols - 1, 0.0, next_lane(here))
            left = jnp.where(lane == 0, 0.0, prev_lane(here))
            hx[q, pl.ds(r, rows), :] = jnp.where(lane == cols - 1, 0.0, 0.5 * (here + right))
            hy[q, pl.ds(PAD + r, rows), :] = 0.5 * (here + up)
            hz[q, pl.ds(r, rows), :] = (0.5 * low_in) * (here + low)
            total = ((up + down) + (left + right)) + (low + high)
            dg[q, pl.ds(r, rows), :] = 3.0 * here + 0.5 * total
        return carry

    lax.fori_loop(start, stop, body, 0)
    if not top:
        return
    inside = jnp.logical_and(stop - 1 >= first, stop <= last).astype(F32)
    for r, rows in pieces:
        here = sig[stop + 1, pl.ds(PAD + r, rows), :]
        low = sig[stop, pl.ds(PAD + r, rows), :]
        hz[stop, pl.ds(r, rows), :] = (0.5 * inside) * (here + low)


def operator(v, p, dg, hx, hy, hz, q, r, rows):
    here = v[p, pl.ds(PAD + r, rows), :]
    wx = hx[q, pl.ds(r, rows), :]
    acc = dg[q, pl.ds(r, rows), :] * here
    acc = acc - wx * next_lane(here)
    acc = acc - prev_lane(wx * here)
    acc = acc - hy[q, pl.ds(PAD + r, rows), :] * v[p, pl.ds(PAD + r + 1, rows), :]
    acc = acc - hy[q, pl.ds(PAD + r - 1, rows), :] * v[p, pl.ds(PAD + r - 1, rows), :]
    acc = acc - hz[q, pl.ds(r, rows), :] * v[p - 1, pl.ds(PAD + r, rows), :]
    acc = acc - hz[q + 1, pl.ds(r, rows), :] * v[p + 1, pl.ds(PAD + r, rows), :]
    return here, acc


def zero_pads(ref, nx):
    zero = jnp.zeros((ref.shape[0], PAD, ref.shape[2]), F32)
    ref[:, pl.ds(0, PAD), :] = zero
    ref[:, pl.ds(PAD + nx, PAD), :] = zero


def splat(row, index):
    return jnp.sum(jnp.where(lane_iota(row.shape) == index, row, 0.0), axis=1, keepdims=True)


def solve_small(row, scale, thetas, n=0):
    gram = {}
    for i in range(4):
        for j in range(i + 1):
            gram[i, j] = gram[j, i] = splat(row, n)
            n += 1
    last = splat(row, n)
    mat = {}
    for i in range(4):
        for j in range(i + 1):
            if j == 3:
                mat[i, j] = last
            else:
                mat[i, j] = scale * gram[i, j + 1] + thetas[j] * gram[i, j]
    low, inv = {}, {}
    for j in range(4):
        pivot = mat[j, j]
        for k in range(j):
            pivot = pivot - low[j, k] * low[j, k] * mat["d", k]
        mat["d", j] = pivot
        good = pivot > 1e-7 * mat[j, j]
        inv[j] = jnp.where(good, 1.0 / jnp.where(good, pivot, 1.0), 0.0)
        for i in range(j + 1, 4):
            value = mat[i, j]
            for k in range(j):
                value = value - low[i, k] * low[j, k] * mat["d", k]
            low[i, j] = value * inv[j]
    y = []
    for i in range(4):
        value = gram[i, 0]
        for k in range(i):
            value = value - low[i, k] * y[k]
        y.append(value)
    c = [None] * 4
    for i in reversed(range(4)):
        value = y[i] * inv[i]
        for k in range(i + 1, 4):
            value = value - low[k, i] * c[k]
        c[i] = value
    return c


def pack_row(accs):
    lane = lane_iota((1, 128))
    row = jnp.zeros((1, 128), F32)
    for n, acc in enumerate(accs):
        total = jnp.sum(jnp.sum(acc, axis=0, keepdims=True), axis=1, keepdims=True)
        row = row + jnp.where(lane == n, total, 0.0)
    return row


def remote(src_ref, dst_ref, send_sem, recv_sem, target):
    return pltpu.make_async_remote_copy(
        src_ref=src_ref,
        dst_ref=dst_ref,
        send_sem=send_sem,
        recv_sem=recv_sem,
        device_id=target,
        device_id_type=MESH,
    )


def flip(src, bit):
    return src + bit - 2 * bit * (lax.rem(src // bit, 2))


def partners(me, slabs):
    near = 4
    fours = slabs // near
    place, four = lax.rem(me, near), me // near
    return (
        [four * near + lax.rem(place + d, near) for d in range(1, near)],
        [lax.rem(four + d, fours) * near + place for d in range(1, fours)],
    )


def pair_group(me):
    place = lax.rem(me, 4)
    return [me - place + lax.rem(place + d, 4) for d in range(4)]


def signal_all(src, me, slabs, others):
    barrier = pltpu.get_barrier_semaphore()
    targets = [(src, t) for group in partners(me, slabs) for t in group] + others
    for target in targets:
        pl.semaphore_signal(barrier, inc=1, device_id=target, device_id_type=MESH)
    return barrier, len(targets)


class Sum:
    def __init__(self, src, me, slabs, levels, across=None):
        groups = [[(src, t) for t in group] for group in partners(me, slabs)]
        if across is not None:
            groups[0] += [(across, t) for t in pair_group(me)]
        self.levels = [(level, group) for level, group in zip(levels, groups) if group]

    def send(self, n, value):
        (buf, send_sem, recv_sem), group = self.levels[n]
        buf[0] = value
        for d, target in enumerate(group):
            remote(buf.at[0], buf.at[d + 1], send_sem, recv_sem, target).start()

    def _wait(self, n, which):
        level, group = self.levels[n]
        rest = level[0].at[pl.ds(1, len(group))]
        pltpu.make_async_copy(rest, rest, level[which]).wait()

    def receive(self, n):
        self._wait(n, 2)
        return jnp.sum(self.levels[n][0][0][...], axis=0)

    def start(self, value):
        self.send(0, value)

    def middle(self):
        value = self.receive(0)
        if len(self.levels) > 1:
            self.send(1, value)
        return value

    def end(self, value):
        return self.receive(1) if len(self.levels) > 1 else value

    def whole(self, value):
        self.start(value)
        return self.end(self.middle())

    def close(self):
        for n in range(len(self.levels)):
            self._wait(n, 1)


def sum_scratch(slabs, shape, first=4):
    return [
        VMEM((first, *shape), F32), DMA(()), DMA(()),
        VMEM((max(slabs // 4, 2), *shape), F32), DMA(()), DMA(()),
    ]


def sum_levels(refs):
    return (refs[0:3], refs[3:6])


def first_kernel(
    slabs, lc_in, pt_in, u, tan, mean_out, lc_half, lc_near, u_mine, u_first, u_rest,
    lc, pt, lch, uh, sig, wgt, uw, dg, hx, hy, hz, v0, v1, v2, v3, pth, edge, order,
    s_load, s_take, s_first, r_first, s_c, r_c, s_x, r_x, s_core, r_core, s_v, r_v, s_e, r_e, *sums,
):
    src = lax.axis_index("src")
    me = lax.axis_index("slab")
    depth, nx, cols = lc.shape
    half = nx // 2
    has_low = me > 0
    has_high = me < slabs - 1
    core, side_x = lax.rem(src, 2), src // 2
    mate, across = flip(src, 1), flip(src, 2)
    inner_rows = pl.ds(PAD, nx)
    loads = [
        pltpu.make_async_copy(u, uw.at[pl.ds(1, depth), inner_rows], s_load.at[0]),
        pltpu.make_async_copy(lc_in, lc, s_load.at[1]),
        pltpu.make_async_copy(pt_in, pt, s_load.at[2]),
    ]
    for load in loads:
        load.start()
    ring = [(src, lax.rem(me + 1, slabs)), (src, lax.rem(me + slabs - 1, slabs))]
    barrier, count = signal_all(src, me, slabs, ring + [(mate, me), (across, me)])
    order[...] = order_matrix(cols, False)

    def shuffle(q, carry):
        for n in (0, 1):
            for ref, plane, first in ((lc, q, 0), (pt, q, 0), (uw, q + 1, PAD)):
                rows = pl.ds(first + n * half, half)
                ref[plane, rows, :] = reorder(ref[plane, rows, :], order[...])
        return carry

    for load in loads:
        load.wait()
    lax.fori_loop(0, 2, lambda i, c: shuffle(i * (depth - 1), c), 0)
    pl.semaphore_wait(barrier, count)
    mean_sum = Sum(src, me, slabs, sum_levels(sums[0:6]))
    mom_sum = Sum(src, me, slabs, sum_levels(sums[6:12]))

    def arrives(side):
        return has_low if side == 0 else has_high

    def below(side):
        return me + 1 if side == 0 else me - 1

    def sends(side):
        return has_high if side == 0 else has_low

    def near(side):
        return depth - 1 if side == 0 else 0

    def part(n):
        return pl.ds(n * half, half)

    def copy_u(side, n, to):
        return remote(
            uw.at[1 + near(side), pl.ds(PAD + n * half, half)], uh.at[side, part(n)],
            s_first.at[side, n], r_first.at[side, n], (src, to),
        )

    my_rows = pl.ds(pl.multiple_of(half * side_x, PAD), half)
    their_rows = pl.ds(pl.multiple_of(half * (1 - side_x), PAD), half)

    def copy_c(ref, dst, side, to):
        return remote(
            ref.at[near(side), my_rows], dst.at[side, my_rows], s_c.at[side], r_c.at[side], (src, to)
        )

    def swap(ref, side, rows):
        return remote(ref.at[side, rows], ref.at[side, rows], s_x.at[side], r_x.at[side], (across, me))

    def forward(ref, side):
        return remote(ref.at[side], ref.at[side], s_core.at[side], r_core.at[side], (mate, me))

    def by_core(body):
        pl.when(core == 0)(lambda: body(lc, lch))
        pl.when(core == 1)(lambda: body(pt, pth))

    for side in (0, 1):
        @pl.when(sends(side))
        def _():
            by_core(lambda ref, dst: copy_c(ref, dst, side, below(side)).start())
    for n in (0, 1):
        for side in (0, 1):
            pl.when(sends(side))(lambda side=side, n=n: copy_u(side, n, below(side)).start())

    for ref in (sig, wgt, uw, hy, v0, v1, v2, v3):
        zero_pads(ref, nx)
    def own(q, acc):
        for r, rows in chunks(nx):
            value = jnp.exp(lc[q, pl.ds(r, rows), :])
            sig[q + 1, pl.ds(PAD + r, rows), :] = value
            wgt[q + 1, pl.ds(PAD + r, rows), :] = value * pt[q, pl.ds(r, rows), :]
            acc = acc + fold(value)
        return acc

    lax.fori_loop(1, depth - 1, shuffle, 0)
    acc = lax.fori_loop(0, depth, own, jnp.zeros((8, cols), F32))
    mean_sum.start(pack_row([acc]))

    fields = (v0, v1, v2, v3)
    for ref in fields:
        for side in (0, 1):
            def clear(ref=ref, side=side):
                ref[side * (depth + 1), pl.ds(PAD, nx), :] = jnp.zeros((nx, cols), F32)

            if ref is v3:
                clear()
            else:
                pl.when(jnp.logical_not(arrives(side)))(clear)
    mean_part = mean_sum.middle()

    for side in (0, 1):
        @pl.when(arrives(side))
        def _():
            def body(ref, dst):
                copy_c(ref, dst, side, me).wait_recv()
                swap(dst, side, my_rows).start()

            by_core(body)
    for side in (0, 1):
        @pl.when(arrives(side))
        def _():
            def body(ref, dst):
                swap(dst, side, their_rows).wait_recv()
                forward(dst, side).start()

            by_core(body)

    def rhs_rows(q, pieces):
        for r, rows in pieces:
            c = wgt[q + 1, pl.ds(PAD + r, rows), :]
            f = uw[q + 1, pl.ds(PAD + r, rows), :]
            lane = lane_iota(c.shape)
            cr = jnp.where(lane == cols - 1, 0.0, next_lane(c))
            fr = jnp.where(lane == cols - 1, 0.0, next_lane(f))
            flow = (c + cr) * (f - fr)
            total = flow + jnp.where(lane == 0, c * f, -prev_lane(flow))
            for dq, dr in ((0, 1), (0, -1), (1, 0), (-1, 0)):
                cj = wgt[q + 1 + dq, pl.ds(PAD + r + dr, rows), :]
                fj = uw[q + 1 + dq, pl.ds(PAD + r + dr, rows), :]
                total = total + (c + cj) * (f - fj)
            v0[q + 1, pl.ds(PAD + r, rows), :] = -0.5 * total

    def copy_v(k, side, n, to):
        plane = depth if side == 0 else 1
        halo = 0 if side == 0 else depth + 1
        rows = pl.ds(PAD + n * half, half)
        ref = fields[k]
        return remote(
            ref.at[plane, rows], ref.at[halo, rows], s_v.at[k, side, n], r_v.at[k, side, n], (src, to)
        )

    def send_edge(k, side, n):
        out = 1 - side

        @pl.when(sends(out))
        def _():
            copy_v(k, out, n, below(out)).start()

    for n in (0, 1):
        for side in (0, 1):
            plane = 0 if side == 0 else depth + 1

            @pl.when(arrives(side))
            def _():
                if n == 0:
                    pl.when(core == 0)(lambda: forward(pth, side).wait_recv())
                    pl.when(core == 1)(lambda: forward(lch, side).wait_recv())
                copy_u(side, n, me).wait_recv()
                for r, rows in chunks(half, n * half):
                    value = jnp.exp(lch[side, pl.ds(r, rows), :])
                    sig[plane, pl.ds(PAD + r, rows), :] = value
                    wgt[plane, pl.ds(PAD + r, rows), :] = value * pth[side, pl.ds(r, rows), :]
                    uw[plane, pl.ds(PAD + r, rows), :] = uh[side, pl.ds(r, rows), :]

            @pl.when(jnp.logical_not(arrives(side)))
            def _():
                for ref in (sig, wgt, uw):
                    ref[plane, pl.ds(PAD + n * half, half), :] = jnp.zeros((half, cols), F32)
                lch[side, part(n), :] = jnp.zeros((half, cols), F32)

            rhs_rows(0 if side == 0 else depth - 1, chunks(half, n * half))
            send_edge(0, side, n)

    frame_rows = half + PAD
    mine = half * side_x - PAD * side_x
    theirs = (half - PAD) - mine
    takes = []
    for n, (ref, dst, first, at) in enumerate((
        (lc, lc_half, 0, mine),
        (lch, lc_near, 0, mine),
        (uw, u_mine, 0, PAD + mine),
        (uw, u_first, 0, PAD + theirs),
        (uw, u_rest, EARLY, PAD + theirs),
    )):
        rows = pl.ds(pl.multiple_of(at, PAD), frame_rows)
        takes.append(pltpu.make_async_copy(ref.at[pl.ds(first, dst.shape[0]), rows], dst, s_take.at[n]))
    for take in takes:
        take.start()

    def inner(body, carry):
        return lax.fori_loop(1, depth - 1, body, carry)

    def rhs_plane(q, carry):
        rhs_rows(q, chunks(nx))
        return carry

    inner(rhs_plane, 0)
    first, last = -me * depth, (slabs - me) * depth - 1
    make_coefs(sig, dg, hx, hy, hz, 0, depth, first, last, chunks(nx))

    mean = splat(mean_sum.end(mean_part), 0) * (1.0 / (slabs * depth * nx * cols))
    mean_out[...] = jnp.broadcast_to(mean, (8, 128))
    scale = 6.0 * mean
    inv = 1.0 / scale

    zero = jnp.zeros((8, cols), F32)
    dots = []
    for k in range(3):
        shift = THETA[k] * mean * inv

        def step(q, accs, pieces=None, k=k, shift=shift):
            accs = list(accs)
            for r, rows in pieces or chunks(nx):
                here, image = operator(fields[k], q + 1, dg, hx, hy, hz, q, r, rows)
                new = inv * image - shift * here
                fields[k + 1][q + 1, pl.ds(PAD + r, rows), :] = new
                if k == 0:
                    accs[0] = accs[0] + fold(here * here)
                for i in range(k + 1):
                    other = here if i == k else fields[i][q + 1, pl.ds(PAD + r, rows), :]
                    accs[i + (k == 0)] = accs[i + (k == 0)] + fold(new * other)
                accs[-1] = accs[-1] + fold(new * new)
            return tuple(accs)

        accs = inner(step, (zero,) * (3 if k == 0 else k + 2))
        for n in (0, 1):
            for side in (0, 1):
                pl.when(arrives(side))(lambda side=side, n=n, k=k: copy_v(k, side, n, me).wait_recv())
                accs = step(0 if side == 0 else depth - 1, accs, chunks(half, n * half))
                if k < 2:
                    send_edge(k + 1, side, n)
        dots.extend(accs)

    def copy_edge(side, to):
        plane = depth if side == 0 else 1
        return remote(
            v3.at[plane, pl.ds(PAD + side * half, half)], edge.at[side], s_e.at[side], r_e.at[side], (src, to)
        )

    for side in (0, 1):
        pl.when(sends(side))(lambda side=side: copy_edge(side, below(side)).start())
    def energy(q, acc):
        for r, rows in chunks(nx):
            here, image = operator(v3, q + 1, dg, hx, hy, hz, q, r, rows)
            acc = acc + fold(here * image)
        return acc

    acc = lax.fori_loop(0, depth, energy, zero)
    for side in (0, 1):
        got = arrives(side)
        pl.when(got)(lambda side=side: copy_edge(side, me).wait_recv())

        @pl.when(jnp.logical_not(got))
        def _():
            edge[side] = jnp.zeros((half, cols), F32)

        for r, rows in chunks(half):
            at = side * half + r
            face = hz[side * depth, pl.ds(at, rows), :] * v3[1 + side * (depth - 1), pl.ds(PAD + at, rows), :]
            acc = acc - 2.0 * fold(face * edge[side, pl.ds(r, rows), :])
    dots.append(acc)
    mom_sum.start(pack_row(dots))
    value = mom_sum.middle()

    row = mom_sum.end(value)
    c = solve_small(row, scale, [t * mean for t in THETA])

    def combine(q, carry):
        for r, rows in chunks(nx):
            value = c[0] * v0[q + 1, pl.ds(PAD + r, rows), :]
            for i in (1, 2, 3):
                value = value + c[i] * fields[i][q + 1, pl.ds(PAD + r, rows), :]
            tan[q, pl.ds(r, rows), :] = value
        return carry

    lax.fori_loop(0, depth, combine, 0)

    for take in takes:
        take.wait()
    for side in (0, 1):
        @pl.when(sends(side))
        def _():
            copy_c(lc, lch, side, me).wait_send()
            copy_edge(side, me).wait_send()
            for n in (0, 1):
                copy_u(side, n, me).wait_send()
                for k in range(3):
                    copy_v(k, side, n, me).wait_send()

        @pl.when(arrives(side))
        def _():
            swap(lch, side, my_rows).wait_send()
            forward(lch, side).wait_send()
    mean_sum.close()
    mom_sum.close()


def first_solve(slabs, lc, pt, u):
    depth, nx, cols = lc.shape
    plane = (nx + 2 * PAD, cols)
    half = nx // 2
    full = pl.BlockSpec(memory_space=VMEM)
    pair = (DMA((2,)), DMA((2,)))
    return pl.pallas_call(
        functools.partial(first_kernel, slabs),
        name="first_solve",
        out_shape=[
            jax.ShapeDtypeStruct((depth, nx, cols), F32),
            jax.ShapeDtypeStruct((8, 128), F32),
            *(
                jax.ShapeDtypeStruct((planes, half + PAD, cols), F32)
                for planes in (depth, 2, depth + 2, EARLY, depth + 2 - EARLY)
            ),
        ],
        in_specs=[pl.BlockSpec(memory_space=pltpu.HBM)] * 3,
        out_specs=[full] * 7,
        scratch_shapes=[VMEM((depth, nx, cols), F32)] * 2
        + [VMEM((2, nx, cols), F32)] * 2
        + [VMEM((depth + 2, *plane), F32)] * 3
        + [
            VMEM((depth, nx, cols), F32),
            VMEM((depth, nx, cols), F32),
            VMEM((depth, *plane), F32),
            VMEM((depth + 1, nx, cols), F32),
        ]
        + [VMEM((depth + 2, *plane), F32)] * 4
        + [VMEM((2, nx, cols), F32), VMEM((2, half, cols), F32), VMEM((cols, cols), jnp.bfloat16)]
        + [DMA((3,)), DMA((5,)), DMA((2, 2)), DMA((2, 2)), *pair, *pair, *pair]
        + [DMA((3, 2, 2)), DMA((3, 2, 2)), *pair]
        + sum_scratch(slabs, (1, 128)) * 2,
        compiler_params=pltpu.CompilerParams(
            collective_id=0, has_side_effects=True, vmem_limit_bytes=43 << 20
        ),
    )(lc, pt, u)


def over_window(group, ordered, first_key, last_key, keys, cells, keys_s, cells_s, sems, body):
    start, stop = (
        jnp.sum(jnp.where(ordered[...] < bound, 1.0, 0.0)).astype(jnp.int32) for bound in (first_key, last_key)
    )
    size = keys_s.shape[0]

    def piece(w, carry):
        base = pl.multiple_of(w * size, size)
        copies = [
            pltpu.make_async_copy(ref.at[pl.ds(base, size)], dst, sems.at[n])
            for n, (ref, dst) in enumerate(((keys, keys_s), (cells, cells_s)))
        ]
        for copy in copies:
            copy.start()
        for copy in copies:
            copy.wait()
        low = jnp.maximum(start - base, 0)
        high = jnp.minimum(stop - base, size)

        def step(g, carry):
            body(low + g * group, high)
            return carry

        return lax.fori_loop(0, (high - low + group - 1) // group, step, carry)

    lax.fori_loop(start // size, (stop + size - 1) // size, piece, 0)


def window_scratch(entries):
    size = min(1024, entries)
    return [SMEM((size,), jnp.int32), SMEM((size,), jnp.int32), DMA((2,))]


def bits(count):
    assert count & (count - 1) == 0
    return count.bit_length() - 1


def gather_kernel(group, depth, dipoles, ordered, keys, cells, field, out, keys_s, cells_s, sems):
    me = lax.axis_index("slab")
    out[...] = jnp.zeros_like(out)
    lines, cols = field.shape
    nx = lines // depth
    entries = 2 * dipoles
    lane = lane_iota((1, cols))
    short = lane_iota((1, 128))
    base = me * lines

    def body(least, stop):
        parts = []
        j = jnp.minimum(least, keys_s.shape[0] - group)
        for e in range(group):
            key, cell = keys_s[j + e], cells_s[j + e]
            o = key & (entries - 1)
            k = o & (dipoles - 1)
            line = ((key >> bits(entries)) << bits(nx)) + (cell >> bits(cols)) - base
            inside = jnp.logical_and(j + e >= least, j + e < stop)
            lane_at = jnp.where(inside, lane_of(cell & (cols - 1), cols), -1)
            picked = jnp.where(lane == lane_at, field[pl.ds(jnp.where(inside, line, 0), 1), :], 0.0)
            value = jnp.sum(picked, axis=1, keepdims=True)
            value = jnp.where(o < dipoles, value, -value)
            parts.append((k >> 7, jnp.where(short == (k & 127), value, 0.0)))
        for line, value in parts:
            out[pl.ds(line, 1), :] = out[pl.ds(line, 1), :] + value

    first = me * depth * entries
    over_window(group, ordered, first, first + depth * entries, keys, cells, keys_s, cells_s, sems, body)


def gather(keys, cells, field, depth):
    anywhere = pl.BlockSpec(memory_space=pl.ANY)
    full = pl.BlockSpec(memory_space=VMEM)
    entries = keys.shape[0]
    return pl.pallas_call(
        functools.partial(gather_kernel, 16, depth, entries // 2),
        name="gather",
        out_shape=jax.ShapeDtypeStruct((entries // 256, 128), F32),
        in_specs=[full, anywhere, anywhere, full],
        out_specs=full,
        scratch_shapes=window_scratch(entries),
        compiler_params=pltpu.CompilerParams(vmem_limit_bytes=8 << 20),
    )(keys.reshape(-1, 128), keys, cells, field)


def share_kernel(slabs, part, out, s_x, r_x, *sums):
    src = lax.axis_index("src")
    me = lax.axis_index("slab")
    side_x = src // 2
    across = flip(src, 2)
    barrier, count = signal_all(src, me, slabs, [(across, me)])
    pl.semaphore_wait(barrier, count)
    total = Sum(src, me, slabs, sum_levels(sums))
    out[side_x] = total.whole(part[...])
    copy = remote(out.at[side_x], out.at[side_x], s_x, r_x, (across, me))
    copy.start()
    copy.wait()
    total.close()


def share(slabs, part):
    full = pl.BlockSpec(memory_space=VMEM)
    return pl.pallas_call(
        functools.partial(share_kernel, slabs),
        name="share_data",
        out_shape=jax.ShapeDtypeStruct((2, *part.shape), F32),
        in_specs=[full],
        out_specs=full,
        scratch_shapes=[DMA(()), DMA(())] + sum_scratch(slabs, part.shape),
        compiler_params=pltpu.CompilerParams(
            collective_id=1, has_side_effects=True, vmem_limit_bytes=8 << 20
        ),
    )(part)


def scatter_kernel(group, depth, nx, lines, ordered, keys, cells, data, out0, out1, keys_s, cells_s, sems):
    me = lax.axis_index("slab")
    side_x = lax.axis_index("src") // 2
    outs = (out0, out1)
    total, cols = out0.shape
    planes = total // lines
    entries = keys.shape[0]
    dipoles = entries // 2
    lane = lane_iota((1, cols))
    low = me * depth - WIDE
    row_base = (nx // 2) * side_x - 2 * PAD
    plane_base = low * lines + row_base

    def clear(q, carry):
        for out in outs:
            out[pl.ds(pl.multiple_of(q * lines, 8), lines), :] = jnp.zeros((lines, cols), F32)
        return carry

    lax.fori_loop(0, planes, clear, 0)

    def body(least, stop):
        parts = []
        j = jnp.minimum(least, keys_s.shape[0] - group)
        for e in range(group):
            key, cell = keys_s[j + e], cells_s[j + e]
            o = key & (entries - 1)
            k = o & (dipoles - 1)
            row = cell >> bits(cols)
            inside = jnp.logical_and(j + e >= least, j + e < stop)
            inside = jnp.logical_and(inside, jnp.logical_and(row >= row_base + PAD, row < row_base + lines - PAD))
            hit = lane == jnp.where(inside, lane_of(cell & (cols - 1), cols), -1)
            at = jnp.where(inside, (key >> bits(entries)) * lines + row - plane_base, 0)
            sign = jnp.where(o < dipoles, 1.0, -1.0)
            parts.append((at, [jnp.where(hit, data[k + n * dipoles] * sign, 0.0) for n in (0, 1)]))
        for at, values in parts:
            for out, value in zip(outs, values):
                out[pl.ds(at, 1), :] = out[pl.ds(at, 1), :] + value

    over_window(
        group, ordered, low * entries, (low + planes) * entries, keys, cells, keys_s, cells_s, sems, body
    )


def scatter(keys, cells, data, depth, nx, cols):
    smem = pl.BlockSpec(memory_space=SMEM)
    anywhere = pl.BlockSpec(memory_space=pl.ANY)
    full = pl.BlockSpec(memory_space=VMEM)
    lines = nx // 2 + 4 * PAD
    planes = depth + 2 * WIDE
    back = pl.pallas_call(
        functools.partial(scatter_kernel, 8, depth, nx, lines),
        name="scatter",
        out_shape=[jax.ShapeDtypeStruct((planes * lines, cols), F32)] * 2,
        in_specs=[full, anywhere, anywhere, smem],
        out_specs=[full, full],
        scratch_shapes=window_scratch(keys.shape[0]),
        compiler_params=pltpu.CompilerParams(vmem_limit_bytes=8 << 20),
    )(keys.reshape(-1, 128), keys, cells, data.reshape(-1))
    return [ref.reshape(planes, lines, cols) for ref in back]


def second_kernel(
    slabs, nx, lc_half, lc_near, u_mine, u_first, u_rest, mean_in, v00, v01, out,
    sig, dg, hx, hy, hz, v1, v2, v3, u2, adj, give, take, pair, far, order,
    s_load, s_u, r_u, s_far, r_far, s_c2, r_c2, s_give, r_give, s_x, r_x, s_own, r_own, s_fwd, r_fwd,
    *sums,
):
    src = lax.axis_index("src")
    me = lax.axis_index("slab")
    depth, _, cols = out.shape
    half = nx // 2
    frame = half + 2 * PAD
    frame_rows = half + PAD
    quarter = depth // 2
    core, side_x = lax.rem(src, 2), src // 2
    mate, across = flip(src, 1), flip(src, 2)
    wide = depth + 2 * WIDE
    ring = [(src, lax.rem(me + 1, slabs)), (src, lax.rem(me + slabs - 1, slabs))]
    barrier, count = signal_all(src, me, slabs, ring + [(mate, me)] + [(across, t) for t in pair_group(me)])
    total = Sum(src, me, slabs, sum_levels(sums), across)
    order[...] = order_matrix(cols, True)
    owned = chunks(half, PAD)
    rims = [(0, PAD), (PAD + half, PAD)]
    every = rims[:1] + owned + rims[1:]

    zero_pads(sig, frame)
    zero_pads(hy, frame)
    for ref in (v1, v2, v3):
        for j in (0, 1):
            zero_pads(ref.at[j], frame)

    outside = pl.ds(pl.multiple_of(PAD + (half + PAD) * side_x, PAD), PAD)
    u2[:, :, pl.ds(pl.multiple_of((half + PAD) * side_x, PAD), PAD), :] = jnp.zeros((2, depth + 2, PAD, cols), F32)
    frame_mine = pl.ds(pl.multiple_of(PAD * (1 - side_x), PAD), frame_rows)
    frame_theirs = pl.ds(pl.multiple_of(PAD * side_x, PAD), frame_rows)
    early = pl.ds(0, EARLY)
    late = pl.ds(EARLY, depth + 2 - EARLY)
    loads = [
        pltpu.make_async_copy(u_mine, u2.at[side_x, :, frame_mine], s_load.at[0]),
        pltpu.make_async_copy(u_first, u2.at[1 - side_x, early, frame_mine], s_load.at[1]),
    ]
    for load in loads:
        load.start()
    low_in, high_in = (me > 0).astype(F32), (me < slabs - 1).astype(F32)

    def conductivity(ref, count, first, factor=None):
        def body(n, carry):
            for r, rows in chunks(frame_rows):
                to = pl.multiple_of(PAD + PAD * (1 - side_x) + r, PAD)
                value = jnp.exp(ref[n, pl.ds(r, rows), :])
                sig[first + 1 + n, pl.ds(to, rows), :] = value if factor is None else factor * value
            sig[first + 1 + n, outside, :] = jnp.zeros((PAD, cols), F32)
            return carry

        lax.fori_loop(0, count, body, 0)

    conductivity(lc_half, depth, WIDE)
    conductivity(lc_near, 1, WIDE - 1, low_in)
    conductivity(lc_near.at[pl.ds(1, 1)], 1, WIDE + depth, high_in)

    arrives = (me > 0, me < slabs - 1)
    sends = (me < slabs - 1, me > 0)
    to_slab = (me + 1, me - 1)
    part = -(-frame_rows // (2 * PAD)) * PAD
    fetched = pl.ds(pl.multiple_of((frame_rows - part) * core, PAD), part)
    given = pl.ds(pl.multiple_of(part * core, PAD), frame_rows - part)
    taken = pl.ds(pl.multiple_of(part * (1 - core), PAD), frame_rows - part)

    def copy_far(side, to):
        planes = pl.ds(depth - WIDE if side == 0 else 1, WIDE - 1)
        return remote(lc_half.at[planes, fetched], far.at[side, :, fetched], s_far.at[side], r_far.at[side], (src, to))

    def share_far(side, rows):
        ref = far.at[side, :, rows]
        return remote(ref, ref, s_c2.at[side], r_c2.at[side], (mate, me))

    copy_rest = remote(u_rest, u2.at[side_x, late, frame_theirs], s_u, r_u, (across, me))
    pl.semaphore_wait(barrier, count)
    for side in (0, 1):
        pl.when(sends[side])(lambda side=side: copy_far(side, to_slab[side]).start())
    copy_rest.start()

    first, last = WIDE - me * depth, WIDE + (slabs - me) * depth - 1
    low_open, high_open = side_x.astype(F32), 1.0 - side_x.astype(F32)

    def coefs(start, stop, top=True):
        make_coefs(sig, dg, hx, hy, hz, start, stop, first, last, every, top)

        def close(q, carry):
            for line, factor in ((2 * PAD - 1, low_open), (2 * PAD + half - 1, high_open)):
                hy[q, pl.ds(line, 1), :] = hy[q, pl.ds(line, 1), :] * factor
            return carry

        lax.fori_loop(start, stop, close, 0)

    mean = mean_in[0:1, 0:1]
    scale = 6.0 * mean
    inv = 1.0 / scale
    zero = jnp.zeros((8, cols), F32)
    fields = [(v0, v1.at[j], v2.at[j], v3.at[j]) for j, v0 in enumerate((v00, v01))]
    sums_of = {}

    def run(k, start, stop, dotted):
        shift = THETA[k] * mean * inv
        for j in (0, 1):
            def step(q, accs, j=j):
                accs = list(accs)
                for r, rows in every:
                    here, image = operator(fields[j][k], q - k, dg, hx, hy, hz, q, r, rows)
                    new = inv * image - shift * here
                    fields[j][k + 1][q - k - 1, pl.ds(PAD + r, rows), :] = new
                    if not dotted or (r, rows) not in owned:
                        continue
                    if k == 0:
                        accs[0] = accs[0] + fold(here * here)
                    for i in range(k + 1):
                        other = here if i == k else fields[j][i][q - i, pl.ds(PAD + r, rows), :]
                        accs[i + (k == 0)] = accs[i + (k == 0)] + fold(new * other)
                    accs[-1] = accs[-1] + fold(new * new)
                return tuple(accs)

            accs = sums_of.get((j, k), (zero,) * (3 if k == 0 else k + 2)) if dotted else ()
            accs = lax.fori_loop(start, stop, step, accs)
            if dotted:
                sums_of[j, k] = accs

    top = WIDE + depth
    coefs(WIDE, top)
    run(0, WIDE, top, True)
    run(1, WIDE + 1, top - 1, True)
    for side in (0, 1):
        @pl.when(arrives[side])
        def _():
            copy_far(side, me).wait_recv()
            share_far(side, given).start()

        @pl.when(jnp.logical_not(arrives[side]))
        def _():
            far[side] = jnp.zeros(far.shape[1:], F32)

    run(2, WIDE + 2, top - 2, True)
    for side in (0, 1):
        pl.when(arrives[side])(lambda side=side: share_far(side, taken).wait_recv())
    conductivity(far.at[0], WIDE - 1, 0, low_in)
    conductivity(far.at[1], WIDE - 1, top + 1, high_in)
    coefs(1, WIDE, False)
    coefs(top, wide - 1)
    for k in range(3):
        run(k, k + 1, WIDE, False)
        if k:
            run(k, WIDE, WIDE + k, True)
            run(k, top - k, top, True)
        run(k, top, wide - k - 1, False)
    dots = [[acc for k in range(3) for acc in sums_of[j, k]] for j in (0, 1)]

    for j in (0, 1):
        def energy(q, acc, j=j):
            for r, rows in owned:
                here, image = operator(v3.at[j], q + 1, dg, hx, hy, hz, q + WIDE, r, rows)
                acc = acc + fold(here * image)
            return acc

        dots[j].append(lax.fori_loop(0, depth, energy, zero))

    row = total.whole(pack_row(dots[0] + dots[1]))
    thetas = [t * mean for t in THETA]
    coef = [solve_small(row, scale, thetas, n) for n in (0, len(dots[0]))]

    def combine(q, carry):
        for j in (0, 1):
            c = coef[j]
            for r, rows in every:
                value = c[3] * v3[j, q, pl.ds(PAD + r, rows), :]
                for i, ref in enumerate(fields[j][:3]):
                    value = value + c[i] * ref[q + 3 - i, pl.ds(PAD + r, rows), :]
                adj[j, q, pl.ds(r, rows), :] = value
        return carry

    lax.fori_loop(0, depth + 2, combine, 0)
    for load in loads:
        load.wait()
    copy_rest.wait()
    for side in (0, 1):
        pl.when(sends[side])(lambda side=side: copy_far(side, me).wait_send())
        pl.when(arrives[side])(lambda side=side: share_far(side, given).wait_send())

    def partial(q, dst, slot):
        for r, rows in owned:
            total = jnp.zeros((rows, cols), F32)
            for j in (0, 1):
                f = u2[j, q + 1, pl.ds(r, rows), :]
                a = adj[j, q + 1, pl.ds(r, rows), :]
                lane = lane_iota(f.shape)
                fr = jnp.where(lane == cols - 1, 0.0, next_lane(f))
                ar = jnp.where(lane == cols - 1, 0.0, next_lane(a))
                flow = (f - fr) * (a - ar)
                total = total + (flow + jnp.where(lane == 0, f * a, prev_lane(flow)))
                for dq, dr in ((0, 1), (0, -1), (1, 0), (-1, 0)):
                    fj = u2[j, q + 1 + dq, pl.ds(r + dr, rows), :]
                    aj = adj[j, q + 1 + dq, pl.ds(r + dr, rows), :]
                    total = total + (f - fj) * (a - aj)
            scaled = -0.5 * sig[q + WIDE + 1, pl.ds(PAD + r, rows), :] * total
            dst[slot, pl.ds(r - PAD, rows), :] = scaled

    def copy_give(n):
        return remote(give.at[n], take.at[n], s_give.at[n], r_give.at[n], (mate, me))

    rows_mine = pl.ds(pl.multiple_of(half * side_x, PAD), half)
    rows_theirs = pl.ds(pl.multiple_of(half * (1 - side_x), PAD), half)

    def copy_x(n):
        ref = out.at[core * quarter + n, rows_mine]
        return remote(ref, ref, s_x.at[n], r_x.at[n], (across, me))

    def copy_own(n):
        ref = out.at[core * quarter + n, rows_mine]
        return remote(ref, ref, s_own.at[n], r_own.at[n], (mate, me))

    def copy_fwd(n):
        ref = out.at[core * quarter + n, rows_theirs]
        return remote(ref, ref, s_fwd.at[n], r_fwd.at[n], (mate, me))

    def giving(n, carry):
        partial((1 - core) * quarter + n, give, n)
        copy_give(n).start()
        return carry

    def keeping(n, carry):
        partial(core * quarter + n, pair, n)
        copy_give(n).wait_recv()
        for r, rows in ((0, half),):
            at = pl.multiple_of(half * side_x + r, PAD)
            value = pair[n, pl.ds(r, rows), :] + take[n, pl.ds(r, rows), :]
            out[core * quarter + n, pl.ds(at, rows), :] = reorder(value, order[...])
        copy_x(n).start()
        copy_own(n).start()
        return carry

    def passing(n, carry):
        copy_x(n).wait_recv()
        copy_fwd(n).start()
        return carry

    def ending(n, carry):
        copy_own(n).wait_recv()
        copy_fwd(n).wait_recv()
        for copy in (copy_give, copy_x, copy_own, copy_fwd):
            copy(n).wait_send()
        return carry

    def in_turn(n, carry):
        giving(n + 1, carry)
        return keeping(n, carry)

    giving(0, 0)
    lax.fori_loop(0, quarter - 1, in_turn, 0)
    keeping(quarter - 1, 0)
    for body in (passing, ending):
        lax.fori_loop(0, quarter, body, 0)
    total.close()


def second_solve(slabs, nx, lc_half, lc_near, u_mine, u_first, u_rest, mean, back):
    depth, _, cols = lc_half.shape
    half = nx // 2
    frame = half + 2 * PAD
    plane = (frame + 2 * PAD, cols)
    wide = depth + 2 * WIDE
    quarter = depth // 2
    full = pl.BlockSpec(memory_space=VMEM)
    anywhere = pl.BlockSpec(memory_space=pl.ANY)
    pair = [DMA((2,)), DMA((2,))]
    return pl.pallas_call(
        functools.partial(second_kernel, slabs, nx),
        name="second_solve",
        out_shape=jax.ShapeDtypeStruct((depth, nx, cols), F32),
        in_specs=[full, full, anywhere, anywhere, anywhere, full, full, full],
        out_specs=full,
        scratch_shapes=[
            VMEM((wide + 2, *plane), F32),
            VMEM((wide, frame, cols), F32),
            VMEM((wide, frame, cols), F32),
            VMEM((wide, *plane), F32),
            VMEM((wide + 1, frame, cols), F32),
            VMEM((2, wide - 2, *plane), F32),
            VMEM((2, wide - 4, *plane), F32),
            VMEM((2, wide - 6, *plane), F32),
            VMEM((2, depth + 2, frame, cols), F32),
            VMEM((2, depth + 2, frame, cols), F32),
        ]
        + [VMEM((quarter, half, cols), F32)] * 3
        + [VMEM((2, WIDE - 1, half + PAD, cols), F32), VMEM((cols, cols), jnp.bfloat16)]
        + [DMA((2,)), DMA(()), DMA(())]
        + pair * 2
        + [DMA((quarter,))] * 8
        + sum_scratch(slabs, (1, 128), 8),
        compiler_params=pltpu.CompilerParams(
            collective_id=2, has_side_effects=True, vmem_limit_bytes=42 << 20
        ),
    )(lc_half, lc_near, u_mine, u_first, u_rest, mean, *back)


def shards(slabs, log_cond, perturb, potentials, rec_depth, rec_plan):
    depth, nx, cols = log_cond.shape
    dipoles = rec_depth.shape[1]
    order = lax.broadcasted_iota(jnp.int32, rec_depth.shape, 0) * dipoles
    order = order + lax.broadcasted_iota(jnp.int32, rec_depth.shape, 1)
    keys = (rec_depth * (2 * dipoles) + order).reshape(-1)
    keys, cells = lax.sort((keys, rec_plan.reshape(-1)), num_keys=1, is_stable=False)
    arguments = (pltpu.with_memory_space_constraint(a, pltpu.HBM) for a in (log_cond, perturb, potentials[0]))
    tangent, mean, lc_half, lc_near, u_mine, u_first, u_rest = first_solve(slabs, *arguments)
    part = gather(keys, cells, tangent.reshape(depth * nx, cols), depth)
    data = share(slabs, part)
    u_first, data = lax.optimization_barrier((u_first, data))
    u_first = lax.ppermute(u_first, "src", [(i, (i + 2) % 4) for i in range(4)])
    back = scatter(keys, cells, data, depth, nx, cols)
    return second_solve(slabs, nx, lc_half, lc_near, u_mine, u_first, u_rest, mean, back)


def solution(mesh):
    in_specs = (
        P("slab", None, None),
        P("slab", None, None),
        P("src", "slab", None, None),
        P(),
        P(),
    )
    return jax.shard_map(
        functools.partial(shards, mesh.shape["slab"]),
        mesh=mesh,
        in_specs=in_specs,
        out_specs=P("slab", None, None),
        check_vma=False,
    )
```

```python
import functools

import jax
import jax.numpy as jnp
from jax import lax
from jax.experimental import pallas as pl
from jax.experimental.pallas import tpu as pltpu
from jax.sharding import PartitionSpec as P

MESH = pl.DeviceIdType.MESH
F32 = jnp.float32
VMEM = pltpu.VMEM
SMEM = pltpu.SMEM
DMA = pltpu.SemaphoreType.DMA
PAD = 8
WIDE = 4
EARLY = 4
ROWS = 64
THETA = (6.0, 2.0, 10.0)


def lane_iota(shape):
    return lax.broadcasted_iota(jnp.int32, shape, len(shape) - 1)


def fold(value):
    rows, cols = value.shape
    return jnp.sum(value.reshape(rows // 8, 8, cols), axis=0)


def next_lane(value):
    half = value.shape[1] // 2
    even, odd = value[:, :half], value[:, half:]
    return jnp.concatenate([odd, pltpu.roll(even, half - 1, 1)], axis=1)


def prev_lane(value):
    half = value.shape[1] // 2
    even, odd = value[:, :half], value[:, half:]
    return jnp.concatenate([pltpu.roll(odd, 1, 1), even], axis=1)


def lane_of(column, cols):
    return (column >> 1) + (column & 1) * (cols // 2)


def order_matrix(cols, back):
    row = lax.broadcasted_iota(jnp.int32, (cols, cols), 0)
    col = lax.broadcasted_iota(jnp.int32, (cols, cols), 1)
    hit = row == lane_of(col, cols) if back else col == lane_of(row, cols)
    return jnp.where(hit, 1.0, 0.0).astype(jnp.bfloat16)


def reorder(value, matrix):
    total = None
    for _ in range(3):
        piece = value.astype(jnp.bfloat16)
        value = value - piece.astype(F32)
        moved = jnp.dot(piece, matrix, preferred_element_type=F32)
        total = moved if total is None else total + moved
    return total


def chunks(count, start=0):
    out = []
    done = 0
    while done < count:
        rows = min(ROWS, count - done)
        out.append((start + done, rows))
        done += rows
    return out


def make_coefs(sig, dg, hx, hy, hz, start, stop, first, last, pieces, top=True):
    cols = sig.shape[-1]

    def body(q, carry):
        low_in = jnp.logical_and(q - 1 >= first, q <= last).astype(F32)
        for r, rows in pieces:
            here = sig[q + 1, pl.ds(PAD + r, rows), :]
            up = sig[q + 1, pl.ds(PAD + r + 1, rows), :]
            down = sig[q + 1, pl.ds(PAD + r - 1, rows), :]
            low = sig[q, pl.ds(PAD + r, rows), :]
            high = sig[q + 2, pl.ds(PAD + r, rows), :]
            lane = lane_iota(here.shape)
            right = jnp.where(lane == cols - 1, 0.0, next_lane(here))
            left = jnp.where(lane == 0, 0.0, prev_lane(here))
            hx[q, pl.ds(r, rows), :] = jnp.where(lane == cols - 1, 0.0, 0.5 * (here + right))
            hy[q, pl.ds(PAD + r, rows), :] = 0.5 * (here + up)
            hz[q, pl.ds(r, rows), :] = (0.5 * low_in) * (here + low)
            total = ((up + down) + (left + right)) + (low + high)
            dg[q, pl.ds(r, rows), :] = 3.0 * here + 0.5 * total
        return carry

    lax.fori_loop(start, stop, body, 0)
    if not top:
        return
    inside = jnp.logical_and(stop - 1 >= first, stop <= last).astype(F32)
    for r, rows in pieces:
        here = sig[stop + 1, pl.ds(PAD + r, rows), :]
        low = sig[stop, pl.ds(PAD + r, rows), :]
        hz[stop, pl.ds(r, rows), :] = (0.5 * inside) * (here + low)


def operator(v, p, dg, hx, hy, hz, q, r, rows):
    here = v[p, pl.ds(PAD + r, rows), :]
    wx = hx[q, pl.ds(r, rows), :]
    acc = dg[q, pl.ds(r, rows), :] * here
    acc = acc - wx * next_lane(here)
    acc = acc - prev_lane(wx * here)
    acc = acc - hy[q, pl.ds(PAD + r, rows), :] * v[p, pl.ds(PAD + r + 1, rows), :]
    acc = acc - hy[q, pl.ds(PAD + r - 1, rows), :] * v[p, pl.ds(PAD + r - 1, rows), :]
    acc = acc - hz[q, pl.ds(r, rows), :] * v[p - 1, pl.ds(PAD + r, rows), :]
    acc = acc - hz[q + 1, pl.ds(r, rows), :] * v[p + 1, pl.ds(PAD + r, rows), :]
    return here, acc


def zero_pads(ref, nx):
    zero = jnp.zeros((ref.shape[0], PAD, ref.shape[2]), F32)
    ref[:, pl.ds(0, PAD), :] = zero
    ref[:, pl.ds(PAD + nx, PAD), :] = zero


def splat(row, index):
    return jnp.sum(jnp.where(lane_iota(row.shape) == index, row, 0.0), axis=1, keepdims=True)


def solve_small(row, scale, thetas, n=0):
    gram = {}
    for i in range(4):
        for j in range(i + 1):
            gram[i, j] = gram[j, i] = splat(row, n)
            n += 1
    last = splat(row, n)
    mat = {}
    for i in range(4):
        for j in range(i + 1):
            if j == 3:
                mat[i, j] = last
            else:
                mat[i, j] = scale * gram[i, j + 1] + thetas[j] * gram[i, j]
    low, inv = {}, {}
    for j in range(4):
        pivot = mat[j, j]
        for k in range(j):
            pivot = pivot - low[j, k] * low[j, k] * mat["d", k]
        mat["d", j] = pivot
        good = pivot > 1e-7 * mat[j, j]
        inv[j] = jnp.where(good, 1.0 / jnp.where(good, pivot, 1.0), 0.0)
        for i in range(j + 1, 4):
            value = mat[i, j]
            for k in range(j):
                value = value - low[i, k] * low[j, k] * mat["d", k]
            low[i, j] = value * inv[j]
    y = []
    for i in range(4):
        value = gram[i, 0]
        for k in range(i):
            value = value - low[i, k] * y[k]
        y.append(value)
    c = [None] * 4
    for i in reversed(range(4)):
        value = y[i] * inv[i]
        for k in range(i + 1, 4):
            value = value - low[k, i] * c[k]
        c[i] = value
    return c


def pack_row(accs):
    lane = lane_iota((1, 128))
    row = jnp.zeros((1, 128), F32)
    for n, acc in enumerate(accs):
        total = jnp.sum(jnp.sum(acc, axis=0, keepdims=True), axis=1, keepdims=True)
        row = row + jnp.where(lane == n, total, 0.0)
    return row


def remote(src_ref, dst_ref, send_sem, recv_sem, target):
    return pltpu.make_async_remote_copy(
        src_ref=src_ref,
        dst_ref=dst_ref,
        send_sem=send_sem,
        recv_sem=recv_sem,
        device_id=target,
        device_id_type=MESH,
    )


def flip(src, bit):
    return src + bit - 2 * bit * (lax.rem(src // bit, 2))


def partners(me, slabs):
    near = 4
    fours = slabs // near
    place, four = lax.rem(me, near), me // near
    return (
        [four * near + lax.rem(place + d, near) for d in range(1, near)],
        [lax.rem(four + d, fours) * near + place for d in range(1, fours)],
    )


def pair_group(me):
    place = lax.rem(me, 4)
    return [me - place + lax.rem(place + d, 4) for d in range(4)]


def signal_all(src, me, slabs, others):
    barrier = pltpu.get_barrier_semaphore()
    targets = [(src, t) for group in partners(me, slabs) for t in group] + others
    for target in targets:
        pl.semaphore_signal(barrier, inc=1, device_id=target, device_id_type=MESH)
    return barrier, len(targets)


class Sum:
    def __init__(self, src, me, slabs, levels, across=None):
        groups = [[(src, t) for t in group] for group in partners(me, slabs)]
        if across is not None:
            groups[0] += [(across, t) for t in pair_group(me)]
        self.levels = [(level, group) for level, group in zip(levels, groups) if group]

    def send(self, n, value):
        (buf, send_sem, recv_sem), group = self.levels[n]
        buf[0] = value
        for d, target in enumerate(group):
            remote(buf.at[0], buf.at[d + 1], send_sem, recv_sem, target).start()

    def _wait(self, n, which):
        level, group = self.levels[n]
        rest = level[0].at[pl.ds(1, len(group))]
        pltpu.make_async_copy(rest, rest, level[which]).wait()

    def receive(self, n):
        self._wait(n, 2)
        return jnp.sum(self.levels[n][0][0][...], axis=0)

    def start(self, value):
        self.send(0, value)

    def middle(self):
        value = self.receive(0)
        if len(self.levels) > 1:
            self.send(1, value)
        return value

    def end(self, value):
        return self.receive(1) if len(self.levels) > 1 else value

    def whole(self, value):
        self.start(value)
        return self.end(self.middle())

    def close(self):
        for n in range(len(self.levels)):
            self._wait(n, 1)


def sum_scratch(slabs, shape, first=4):
    return [
        VMEM((first, *shape), F32), DMA(()), DMA(()),
        VMEM((max(slabs // 4, 2), *shape), F32), DMA(()), DMA(()),
    ]


def sum_levels(refs):
    return (refs[0:3], refs[3:6])


def first_kernel(
    slabs, lc_in, pt_in, u, tan, mean_out, lc_half, lc_near, u_mine, u_first, u_rest,
    lc, pt, lch, uh, sig, wgt, uw, dg, hx, hy, hz, v0, v1, v2, v3, pth, edge, order,
    s_load, s_take, s_first, r_first, s_c, r_c, s_x, r_x, s_core, r_core, s_v, r_v, s_e, r_e, *sums,
):
    src = lax.axis_index("src")
    me = lax.axis_index("slab")
    depth, nx, cols = lc.shape
    half = nx // 2
    has_low = me > 0
    has_high = me < slabs - 1
    core, side_x = lax.rem(src, 2), src // 2
    mate, across = flip(src, 1), flip(src, 2)
    inner_rows = pl.ds(PAD, nx)
    loads = [
        pltpu.make_async_copy(u, uw.at[pl.ds(1, depth), inner_rows], s_load.at[0]),
        pltpu.make_async_copy(lc_in, lc, s_load.at[1]),
        pltpu.make_async_copy(pt_in, pt, s_load.at[2]),
    ]
    for load in loads:
        load.start()
    ring = [(src, lax.rem(me + 1, slabs)), (src, lax.rem(me + slabs - 1, slabs))]
    barrier, count = signal_all(src, me, slabs, ring + [(mate, me), (across, me)])
    order[...] = order_matrix(cols, False)

    def shuffle(q, carry):
        for n in (0, 1):
            for ref, plane, first in ((lc, q, 0), (pt, q, 0), (uw, q + 1, PAD)):
                rows = pl.ds(first + n * half, half)
                ref[plane, rows, :] = reorder(ref[plane, rows, :], order[...])
        return carry

    for load in loads:
        load.wait()
    lax.fori_loop(0, 2, lambda i, c: shuffle(i * (depth - 1), c), 0)
    pl.semaphore_wait(barrier, count)
    mean_sum = Sum(src, me, slabs, sum_levels(sums[0:6]))
    mom_sum = Sum(src, me, slabs, sum_levels(sums[6:12]))

    def arrives(side):
        return has_low if side == 0 else has_high

    def below(side):
        return me + 1 if side == 0 else me - 1

    def sends(side):
        return has_high if side == 0 else has_low

    def near(side):
        return depth - 1 if side == 0 else 0

    def part(n):
        return pl.ds(n * half, half)

    def copy_u(side, n, to):
        return remote(
            uw.at[1 + near(side), pl.ds(PAD + n * half, half)], uh.at[side, part(n)],
            s_first.at[side, n], r_first.at[side, n], (src, to),
        )

    my_rows = pl.ds(pl.multiple_of(half * side_x, PAD), half)
    their_rows = pl.ds(pl.multiple_of(half * (1 - side_x), PAD), half)

    def copy_c(ref, dst, side, to):
        return remote(
            ref.at[near(side), my_rows], dst.at[side, my_rows], s_c.at[side], r_c.at[side], (src, to)
        )

    def swap(ref, side, rows):
        return remote(ref.at[side, rows], ref.at[side, rows], s_x.at[side], r_x.at[side], (across, me))

    def forward(ref, side):
        return remote(ref.at[side], ref.at[side], s_core.at[side], r_core.at[side], (mate, me))

    def by_core(body):
        pl.when(core == 0)(lambda: body(lc, lch))
        pl.when(core == 1)(lambda: body(pt, pth))

    for side in (0, 1):
        @pl.when(sends(side))
        def _():
            by_core(lambda ref, dst: copy_c(ref, dst, side, below(side)).start())

    for ref in (sig, wgt, uw, hy, v0, v1, v2, v3):
        zero_pads(ref, nx)
    for side in (0, 1):
        @pl.when(sends(side))
        def _():
            copy_c(lc, lch, side, me).wait_send()

    for n in (0, 1):
        for side in (0, 1):
            pl.when(sends(side))(lambda side=side, n=n: copy_u(side, n, below(side)).start())

    def own(q, acc):
        for r, rows in chunks(nx):
            value = jnp.exp(lc[q, pl.ds(r, rows), :])
            sig[q + 1, pl.ds(PAD + r, rows), :] = value
            wgt[q + 1, pl.ds(PAD + r, rows), :] = value * pt[q, pl.ds(r, rows), :]
            acc = acc + fold(value)
        return acc

    lax.fori_loop(1, depth - 1, shuffle, 0)
    acc = lax.fori_loop(0, depth, own, jnp.zeros((8, cols), F32))
    mean_sum.start(pack_row([acc]))

    fields = (v0, v1, v2, v3)
    for ref in fields:
        for side in (0, 1):
            def clear(ref=ref, side=side):
                ref[side * (depth + 1), pl.ds(PAD, nx), :] = jnp.zeros((nx, cols), F32)

            if ref is v3:
                clear()
            else:
                pl.when(jnp.logical_not(arrives(side)))(clear)
    mean_part = mean_sum.middle()

    for side in (0, 1):
        @pl.when(arrives(side))
        def _():
            def body(ref, dst):
                copy_c(ref, dst, side, me).wait_recv()
                swap(dst, side, my_rows).start()

            by_core(body)
    for side in (0, 1):
        @pl.when(arrives(side))
        def _():
            def body(ref, dst):
                swap(dst, side, their_rows).wait_recv()
                forward(dst, side).start()

            by_core(body)

    def rhs_rows(q, pieces):
        for r, rows in pieces:
            c = wgt[q + 1, pl.ds(PAD + r, rows), :]
            f = uw[q + 1, pl.ds(PAD + r, rows), :]
            lane = lane_iota(c.shape)
            cr = jnp.where(lane == cols - 1, 0.0, next_lane(c))
            fr = jnp.where(lane == cols - 1, 0.0, next_lane(f))
            flow = (c + cr) * (f - fr)
            total = flow + jnp.where(lane == 0, c * f, -prev_lane(flow))
            for dq, dr in ((0, 1), (0, -1), (1, 0), (-1, 0)):
                cj = wgt[q + 1 + dq, pl.ds(PAD + r + dr, rows), :]
                fj = uw[q + 1 + dq, pl.ds(PAD + r + dr, rows), :]
                total = total + (c + cj) * (f - fj)
            v0[q + 1, pl.ds(PAD + r, rows), :] = -0.5 * total

    def copy_v(k, side, n, to):
        plane = depth if side == 0 else 1
        halo = 0 if side == 0 else depth + 1
        rows = pl.ds(PAD + n * half, half)
        ref = fields[k]
        return remote(
            ref.at[plane, rows], ref.at[halo, rows], s_v.at[k, side, n], r_v.at[k, side, n], (src, to)
        )

    def send_edge(k, side, n):
        out = 1 - side

        @pl.when(sends(out))
        def _():
            copy_v(k, out, n, below(out)).start()

    for n in (0, 1):
        for side in (0, 1):
            plane = 0 if side == 0 else depth + 1

            @pl.when(arrives(side))
            def _():
                if n == 0:
                    pl.when(core == 0)(lambda: forward(pth, side).wait_recv())
                    pl.when(core == 1)(lambda: forward(lch, side).wait_recv())
                copy_u(side, n, me).wait_recv()
                for r, rows in chunks(half, n * half):
                    value = jnp.exp(lch[side, pl.ds(r, rows), :])
                    sig[plane, pl.ds(PAD + r, rows), :] = value
                    wgt[plane, pl.ds(PAD + r, rows), :] = value * pth[side, pl.ds(r, rows), :]
                    uw[plane, pl.ds(PAD + r, rows), :] = uh[side, pl.ds(r, rows), :]

            @pl.when(jnp.logical_not(arrives(side)))
            def _():
                for ref in (sig, wgt, uw):
                    ref[plane, pl.ds(PAD + n * half, half), :] = jnp.zeros((half, cols), F32)
                lch[side, part(n), :] = jnp.zeros((half, cols), F32)

            rhs_rows(0 if side == 0 else depth - 1, chunks(half, n * half))
            send_edge(0, side, n)

    frame_rows = half + PAD
    mine = half * side_x - PAD * side_x
    theirs = (half - PAD) - mine
    takes = []
    for n, (ref, dst, first, at) in enumerate((
        (lc, lc_half, 0, mine),
        (lch, lc_near, 0, mine),
        (uw, u_mine, 0, PAD + mine),
        (uw, u_first, 0, PAD + theirs),
        (uw, u_rest, EARLY, PAD + theirs),
    )):
        rows = pl.ds(pl.multiple_of(at, PAD), frame_rows)
        takes.append(pltpu.make_async_copy(ref.at[pl.ds(first, dst.shape[0]), rows], dst, s_take.at[n]))
    for take in takes:
        take.start()

    def inner(body, carry):
        return lax.fori_loop(1, depth - 1, body, carry)

    def rhs_plane(q, carry):
        rhs_rows(q, chunks(nx))
        return carry

    inner(rhs_plane, 0)
    first, last = -me * depth, (slabs - me) * depth - 1
    make_coefs(sig, dg, hx, hy, hz, 0, depth, first, last, chunks(nx))

    mean = splat(mean_sum.end(mean_part), 0) * (1.0 / (slabs * depth * nx * cols))
    mean_out[...] = jnp.broadcast_to(mean, (8, 128))
    scale = 6.0 * mean
    inv = 1.0 / scale

    zero = jnp.zeros((8, cols), F32)
    dots = []
    for k in range(3):
        shift = THETA[k] * mean * inv

        def step(q, accs, pieces=None, k=k, shift=shift):
            accs = list(accs)
            for r, rows in pieces or chunks(nx):
                here, image = operator(fields[k], q + 1, dg, hx, hy, hz, q, r, rows)
                new = inv * image - shift * here
                fields[k + 1][q + 1, pl.ds(PAD + r, rows), :] = new
                if k == 0:
                    accs[0] = accs[0] + fold(here * here)
                for i in range(k + 1):
                    other = here if i == k else fields[i][q + 1, pl.ds(PAD + r, rows), :]
                    accs[i + (k == 0)] = accs[i + (k == 0)] + fold(new * other)
                accs[-1] = accs[-1] + fold(new * new)
            return tuple(accs)

        accs = inner(step, (zero,) * (3 if k == 0 else k + 2))
        for n in (0, 1):
            for side in (0, 1):
                pl.when(arrives(side))(lambda side=side, n=n, k=k: copy_v(k, side, n, me).wait_recv())
                accs = step(0 if side == 0 else depth - 1, accs, chunks(half, n * half))
                if k < 2:
                    send_edge(k + 1, side, n)
        dots.extend(accs)

    def copy_edge(side, to):
        plane = depth if side == 0 else 1
        return remote(
            v3.at[plane, pl.ds(PAD + side * half, half)], edge.at[side], s_e.at[side], r_e.at[side], (src, to)
        )

    for side in (0, 1):
        pl.when(sends(side))(lambda side=side: copy_edge(side, below(side)).start())
    def energy(q, acc):
        for r, rows in chunks(nx):
            here, image = operator(v3, q + 1, dg, hx, hy, hz, q, r, rows)
            acc = acc + fold(here * image)
        return acc

    acc = lax.fori_loop(0, depth, energy, zero)
    for side in (0, 1):
        got = arrives(side)
        pl.when(got)(lambda side=side: copy_edge(side, me).wait_recv())

        @pl.when(jnp.logical_not(got))
        def _():
            edge[side] = jnp.zeros((half, cols), F32)

        for r, rows in chunks(half):
            at = side * half + r
            face = hz[side * depth, pl.ds(at, rows), :] * v3[1 + side * (depth - 1), pl.ds(PAD + at, rows), :]
            acc = acc - 2.0 * fold(face * edge[side, pl.ds(r, rows), :])
    dots.append(acc)
    mom_sum.start(pack_row(dots))
    value = mom_sum.middle()

    row = mom_sum.end(value)
    c = solve_small(row, scale, [t * mean for t in THETA])

    def combine(q, carry):
        for r, rows in chunks(nx):
            value = c[0] * v0[q + 1, pl.ds(PAD + r, rows), :]
            for i in (1, 2, 3):
                value = value + c[i] * fields[i][q + 1, pl.ds(PAD + r, rows), :]
            tan[q, pl.ds(r, rows), :] = value
        return carry

    lax.fori_loop(0, depth, combine, 0)

    for take in takes:
        take.wait()
    for side in (0, 1):
        @pl.when(sends(side))
        def _():
            copy_edge(side, me).wait_send()
            for n in (0, 1):
                copy_u(side, n, me).wait_send()
                for k in range(3):
                    copy_v(k, side, n, me).wait_send()

        @pl.when(arrives(side))
        def _():
            swap(lch, side, my_rows).wait_send()
            forward(lch, side).wait_send()
    mean_sum.close()
    mom_sum.close()


def first_solve(slabs, lc, pt, u):
    depth, nx, cols = lc.shape
    plane = (nx + 2 * PAD, cols)
    half = nx // 2
    full = pl.BlockSpec(memory_space=VMEM)
    pair = (DMA((2,)), DMA((2,)))
    return pl.pallas_call(
        functools.partial(first_kernel, slabs),
        name="first_solve",
        out_shape=[
            jax.ShapeDtypeStruct((depth, nx, cols), F32),
            jax.ShapeDtypeStruct((8, 128), F32),
            *(
                jax.ShapeDtypeStruct((planes, half + PAD, cols), F32)
                for planes in (depth, 2, depth + 2, EARLY, depth + 2 - EARLY)
            ),
        ],
        in_specs=[pl.BlockSpec(memory_space=pltpu.HBM)] * 3,
        out_specs=[full] * 7,
        scratch_shapes=[VMEM((depth, nx, cols), F32)] * 2
        + [VMEM((2, nx, cols), F32)] * 2
        + [VMEM((depth + 2, *plane), F32)] * 3
        + [
            VMEM((depth, nx, cols), F32),
            VMEM((depth, nx, cols), F32),
            VMEM((depth, *plane), F32),
            VMEM((depth + 1, nx, cols), F32),
        ]
        + [VMEM((depth + 2, *plane), F32)] * 4
        + [VMEM((2, nx, cols), F32), VMEM((2, half, cols), F32), VMEM((cols, cols), jnp.bfloat16)]
        + [DMA((3,)), DMA((5,)), DMA((2, 2)), DMA((2, 2)), *pair, *pair, *pair]
        + [DMA((3, 2, 2)), DMA((3, 2, 2)), *pair]
        + sum_scratch(slabs, (1, 128)) * 2,
        compiler_params=pltpu.CompilerParams(
            collective_id=0, has_side_effects=True, vmem_limit_bytes=43 << 20
        ),
    )(lc, pt, u)


def over_window(group, ordered, first_key, last_key, keys, cells, keys_s, cells_s, sems, body):
    start, stop = (
        jnp.sum(jnp.where(ordered[...] < bound, 1.0, 0.0)).astype(jnp.int32) for bound in (first_key, last_key)
    )
    size = keys_s.shape[0]

    def piece(w, carry):
        base = pl.multiple_of(w * size, size)
        copies = [
            pltpu.make_async_copy(ref.at[pl.ds(base, size)], dst, sems.at[n])
            for n, (ref, dst) in enumerate(((keys, keys_s), (cells, cells_s)))
        ]
        for copy in copies:
            copy.start()
        for copy in copies:
            copy.wait()
        low = jnp.maximum(start - base, 0)
        high = jnp.minimum(stop - base, size)

        def step(g, carry):
            body(low + g * group, high)
            return carry

        return lax.fori_loop(0, (high - low + group - 1) // group, step, carry)

    lax.fori_loop(start // size, (stop + size - 1) // size, piece, 0)


def window_scratch(entries):
    size = min(1024, entries)
    return [SMEM((size,), jnp.int32), SMEM((size,), jnp.int32), DMA((2,))]


def bits(count):
    assert count & (count - 1) == 0
    return count.bit_length() - 1


def gather_kernel(group, depth, dipoles, ordered, keys, cells, field, out, keys_s, cells_s, sems):
    me = lax.axis_index("slab")
    out[...] = jnp.zeros_like(out)
    lines, cols = field.shape
    nx = lines // depth
    entries = 2 * dipoles
    lane = lane_iota((1, cols))
    short = lane_iota((1, 128))
    base = me * lines

    def body(least, stop):
        parts = []
        j = jnp.minimum(least, keys_s.shape[0] - group)
        for e in range(group):
            key, cell = keys_s[j + e], cells_s[j + e]
            o = key & (entries - 1)
            k = o & (dipoles - 1)
            line = ((key >> bits(entries)) << bits(nx)) + (cell >> bits(cols)) - base
            inside = jnp.logical_and(j + e >= least, j + e < stop)
            lane_at = jnp.where(inside, lane_of(cell & (cols - 1), cols), -1)
            picked = jnp.where(lane == lane_at, field[pl.ds(jnp.where(inside, line, 0), 1), :], 0.0)
            value = jnp.sum(picked, axis=1, keepdims=True)
            value = jnp.where(o < dipoles, value, -value)
            parts.append((k >> 7, jnp.where(short == (k & 127), value, 0.0)))
        for line, value in parts:
            out[pl.ds(line, 1), :] = out[pl.ds(line, 1), :] + value

    first = me * depth * entries
    over_window(group, ordered, first, first + depth * entries, keys, cells, keys_s, cells_s, sems, body)


def gather(keys, cells, field, depth):
    anywhere = pl.BlockSpec(memory_space=pl.ANY)
    full = pl.BlockSpec(memory_space=VMEM)
    entries = keys.shape[0]
    return pl.pallas_call(
        functools.partial(gather_kernel, 16, depth, entries // 2),
        name="gather",
        out_shape=jax.ShapeDtypeStruct((entries // 256, 128), F32),
        in_specs=[full, anywhere, anywhere, full],
        out_specs=full,
        scratch_shapes=window_scratch(entries),
        compiler_params=pltpu.CompilerParams(vmem_limit_bytes=8 << 20),
    )(keys.reshape(-1, 128), keys, cells, field)


def share_kernel(slabs, part, out, s_x, r_x, *sums):
    src = lax.axis_index("src")
    me = lax.axis_index("slab")
    side_x = src // 2
    across = flip(src, 2)
    barrier, count = signal_all(src, me, slabs, [(across, me)])
    pl.semaphore_wait(barrier, count)
    total = Sum(src, me, slabs, sum_levels(sums))
    out[side_x] = total.whole(part[...])
    copy = remote(out.at[side_x], out.at[side_x], s_x, r_x, (across, me))
    copy.start()
    copy.wait()
    total.close()


def share(slabs, part):
    full = pl.BlockSpec(memory_space=VMEM)
    return pl.pallas_call(
        functools.partial(share_kernel, slabs),
        name="share_data",
        out_shape=jax.ShapeDtypeStruct((2, *part.shape), F32),
        in_specs=[full],
        out_specs=full,
        scratch_shapes=[DMA(()), DMA(())] + sum_scratch(slabs, part.shape),
        compiler_params=pltpu.CompilerParams(
            collective_id=1, has_side_effects=True, vmem_limit_bytes=8 << 20
        ),
    )(part)


def scatter_kernel(group, depth, nx, lines, ordered, keys, cells, data, out, keys_s, cells_s, sems):
    me = lax.axis_index("slab")
    side_x = lax.axis_index("src") // 2
    total, cols = out.shape[0], out.shape[1] // 2
    planes = total // lines
    entries = keys.shape[0]
    dipoles = entries // 2
    lane = lane_iota((1, cols))
    low = me * depth - WIDE
    row_base = (nx // 2) * side_x - 2 * PAD
    plane_base = low * lines + row_base

    def clear(q, carry):
        out[pl.ds(pl.multiple_of(q * lines, 8), lines), :] = jnp.zeros((lines, 2 * cols), F32)
        return carry

    lax.fori_loop(0, planes, clear, 0)

    def body(least, stop):
        parts = []
        j = jnp.minimum(least, keys_s.shape[0] - group)
        for e in range(group):
            key, cell = keys_s[j + e], cells_s[j + e]
            o = key & (entries - 1)
            k = o & (dipoles - 1)
            row = cell >> bits(cols)
            inside = jnp.logical_and(j + e >= least, j + e < stop)
            inside = jnp.logical_and(inside, jnp.logical_and(row >= row_base + PAD, row < row_base + lines - PAD))
            hit = lane == jnp.where(inside, lane_of(cell & (cols - 1), cols), -1)
            at = jnp.where(inside, (key >> bits(entries)) * lines + row - plane_base, 0)
            signed = jnp.where(hit, jnp.where(o < dipoles, 1.0, -1.0), 0.0)
            values = [signed * data[k + n * dipoles] for n in (0, 1)]
            parts.append((at, jnp.concatenate(values, axis=1)))
        for at, value in parts:
            out[pl.ds(at, 1), :] = out[pl.ds(at, 1), :] + value

    over_window(
        group, ordered, low * entries, (low + planes) * entries, keys, cells, keys_s, cells_s, sems, body
    )


def scatter(keys, cells, data, depth, nx, cols):
    smem = pl.BlockSpec(memory_space=SMEM)
    anywhere = pl.BlockSpec(memory_space=pl.ANY)
    full = pl.BlockSpec(memory_space=VMEM)
    lines = nx // 2 + 4 * PAD
    planes = depth + 2 * WIDE
    back = pl.pallas_call(
        functools.partial(scatter_kernel, 8, depth, nx, lines),
        name="scatter",
        out_shape=jax.ShapeDtypeStruct((planes * lines, 2 * cols), F32),
        in_specs=[full, anywhere, anywhere, smem],
        out_specs=full,
        scratch_shapes=window_scratch(keys.shape[0]),
        compiler_params=pltpu.CompilerParams(vmem_limit_bytes=8 << 20),
    )(keys.reshape(-1, 128), keys, cells, data.reshape(-1))
    return back.reshape(planes, lines, 2 * cols)


def second_kernel(
    slabs, nx, lc_half, lc_near, u_mine, u_first, u_rest, mean_in, v0, out,
    sig, dg, hx, hy, hz, v1, v2, v3, u2, adj, give, take, pair, far, order,
    s_load, s_u, r_u, s_far, r_far, s_c2, r_c2, s_give, r_give, s_x, r_x, s_own, r_own, s_fwd, r_fwd,
    *sums,
):
    src = lax.axis_index("src")
    me = lax.axis_index("slab")
    depth, _, cols = out.shape
    half = nx // 2
    frame = half + 2 * PAD
    frame_rows = half + PAD
    quarter = depth // 2
    core, side_x = lax.rem(src, 2), src // 2
    mate, across = flip(src, 1), flip(src, 2)
    wide = depth + 2 * WIDE
    ring = [(src, lax.rem(me + 1, slabs)), (src, lax.rem(me + slabs - 1, slabs))]
    barrier, count = signal_all(src, me, slabs, ring + [(mate, me)] + [(across, t) for t in pair_group(me)])
    total = Sum(src, me, slabs, sum_levels(sums), across)
    order[...] = order_matrix(cols, True)
    owned = chunks(half, PAD)
    rims = [(0, PAD), (PAD + half, PAD)]
    every = rims[:1] + owned + rims[1:]

    zero_pads(sig, frame)
    zero_pads(hy, frame)
    for ref in (v1, v2, v3):
        for j in (0, 1):
            zero_pads(ref.at[j], frame)

    outside = pl.ds(pl.multiple_of(PAD + (half + PAD) * side_x, PAD), PAD)
    u2[:, :, pl.ds(pl.multiple_of((half + PAD) * side_x, PAD), PAD), :] = jnp.zeros((2, depth + 2, PAD, cols), F32)
    frame_mine = pl.ds(pl.multiple_of(PAD * (1 - side_x), PAD), frame_rows)
    frame_theirs = pl.ds(pl.multiple_of(PAD * side_x, PAD), frame_rows)
    early = pl.ds(0, EARLY)
    late = pl.ds(EARLY, depth + 2 - EARLY)
    loads = [
        pltpu.make_async_copy(u_mine, u2.at[side_x, :, frame_mine], s_load.at[0]),
        pltpu.make_async_copy(u_first, u2.at[1 - side_x, early, frame_mine], s_load.at[1]),
    ]
    for load in loads:
        load.start()
    low_in, high_in = (me > 0).astype(F32), (me < slabs - 1).astype(F32)

    def conductivity(ref, count, first, factor=None):
        def body(n, carry):
            for r, rows in chunks(frame_rows):
                to = pl.multiple_of(PAD + PAD * (1 - side_x) + r, PAD)
                value = jnp.exp(ref[n, pl.ds(r, rows), :])
                sig[first + 1 + n, pl.ds(to, rows), :] = value if factor is None else factor * value
            sig[first + 1 + n, outside, :] = jnp.zeros((PAD, cols), F32)
            return carry

        lax.fori_loop(0, count, body, 0)

    conductivity(lc_half, depth, WIDE)
    conductivity(lc_near, 1, WIDE - 1, low_in)
    conductivity(lc_near.at[pl.ds(1, 1)], 1, WIDE + depth, high_in)

    arrives = (me > 0, me < slabs - 1)
    sends = (me < slabs - 1, me > 0)
    to_slab = (me + 1, me - 1)
    part = -(-frame_rows // (2 * PAD)) * PAD
    fetched = pl.ds(pl.multiple_of((frame_rows - part) * core, PAD), part)
    given = pl.ds(pl.multiple_of(part * core, PAD), frame_rows - part)
    taken = pl.ds(pl.multiple_of(part * (1 - core), PAD), frame_rows - part)

    def copy_far(side, to):
        planes = pl.ds(depth - WIDE if side == 0 else 1, WIDE - 1)
        return remote(lc_half.at[planes, fetched], far.at[side, :, fetched], s_far.at[side], r_far.at[side], (src, to))

    def share_far(side, rows):
        ref = far.at[side, :, rows]
        return remote(ref, ref, s_c2.at[side], r_c2.at[side], (mate, me))

    copy_rest = remote(u_rest, u2.at[side_x, late, frame_theirs], s_u, r_u, (across, me))
    pl.semaphore_wait(barrier, count)
    for side in (0, 1):
        pl.when(sends[side])(lambda side=side: copy_far(side, to_slab[side]).start())
    copy_rest.start()

    first, last = WIDE - me * depth, WIDE + (slabs - me) * depth - 1
    low_open, high_open = side_x.astype(F32), 1.0 - side_x.astype(F32)

    def coefs(start, stop, top=True):
        make_coefs(sig, dg, hx, hy, hz, start, stop, first, last, every, top)

        def close(q, carry):
            for line, factor in ((2 * PAD - 1, low_open), (2 * PAD + half - 1, high_open)):
                hy[q, pl.ds(line, 1), :] = hy[q, pl.ds(line, 1), :] * factor
            return carry

        lax.fori_loop(start, stop, close, 0)

    mean = mean_in[0:1, 0:1]
    scale = 6.0 * mean
    inv = 1.0 / scale
    zero = jnp.zeros((8, cols), F32)
    fields = [(v0.at[:, :, pl.ds(j * cols, cols)], v1.at[j], v2.at[j], v3.at[j]) for j in (0, 1)]
    sums_of = {}

    def run(k, start, stop, dotted):
        shift = THETA[k] * mean * inv
        for j in (0, 1):
            def step(q, accs, j=j):
                accs = list(accs)
                for r, rows in every:
                    here, image = operator(fields[j][k], q - k, dg, hx, hy, hz, q, r, rows)
                    new = inv * image - shift * here
                    fields[j][k + 1][q - k - 1, pl.ds(PAD + r, rows), :] = new
                    if not dotted or (r, rows) not in owned:
                        continue
                    if k == 0:
                        accs[0] = accs[0] + fold(here * here)
                    for i in range(k + 1):
                        other = here if i == k else fields[j][i][q - i, pl.ds(PAD + r, rows), :]
                        accs[i + (k == 0)] = accs[i + (k == 0)] + fold(new * other)
                    accs[-1] = accs[-1] + fold(new * new)
                return tuple(accs)

            accs = sums_of.get((j, k), (zero,) * (3 if k == 0 else k + 2)) if dotted else ()
            accs = lax.fori_loop(start, stop, step, accs)
            if dotted:
                sums_of[j, k] = accs

    top = WIDE + depth
    coefs(WIDE, top)
    run(0, WIDE, top, True)
    run(1, WIDE + 1, top - 1, True)
    for side in (0, 1):
        @pl.when(arrives[side])
        def _():
            copy_far(side, me).wait_recv()
            share_far(side, given).start()

        @pl.when(jnp.logical_not(arrives[side]))
        def _():
            far[side] = jnp.zeros(far.shape[1:], F32)

    run(2, WIDE + 2, top - 2, True)
    for side in (0, 1):
        pl.when(arrives[side])(lambda side=side: share_far(side, taken).wait_recv())
    conductivity(far.at[0], WIDE - 1, 0, low_in)
    conductivity(far.at[1], WIDE - 1, top + 1, high_in)
    coefs(1, WIDE, False)
    coefs(top, wide - 1)
    for k in range(3):
        run(k, k + 1, WIDE, False)
        if k:
            run(k, WIDE, WIDE + k, True)
            run(k, top - k, top, True)
        run(k, top, wide - k - 1, False)
    dots = [[acc for k in range(3) for acc in sums_of[j, k]] for j in (0, 1)]

    for j in (0, 1):
        def energy(q, acc, j=j):
            for r, rows in owned:
                here, image = operator(v3.at[j], q + 1, dg, hx, hy, hz, q + WIDE, r, rows)
                acc = acc + fold(here * image)
            return acc

        dots[j].append(lax.fori_loop(0, depth, energy, zero))

    row = total.whole(pack_row(dots[0] + dots[1]))
    thetas = [t * mean for t in THETA]
    coef = [solve_small(row, scale, thetas, n) for n in (0, len(dots[0]))]

    def combine(q, carry):
        for j in (0, 1):
            c = coef[j]
            for r, rows in every:
                value = c[3] * v3[j, q, pl.ds(PAD + r, rows), :]
                for i, ref in enumerate(fields[j][:3]):
                    value = value + c[i] * ref[q + 3 - i, pl.ds(PAD + r, rows), :]
                adj[j, q, pl.ds(r, rows), :] = value
        return carry

    give_first, keep_first = (1 - core) * quarter, core * quarter
    lax.fori_loop(give_first, give_first + 3, combine, 0)
    for load in loads:
        load.wait()
    copy_rest.wait()
    for side in (0, 1):
        pl.when(sends[side])(lambda side=side: copy_far(side, me).wait_send())
        pl.when(arrives[side])(lambda side=side: share_far(side, given).wait_send())

    def partial(q, dst, slot):
        for r, rows in owned:
            total = jnp.zeros((rows, cols), F32)
            for j in (0, 1):
                f = u2[j, q + 1, pl.ds(r, rows), :]
                a = adj[j, q + 1, pl.ds(r, rows), :]
                lane = lane_iota(f.shape)
                fr = jnp.where(lane == cols - 1, 0.0, next_lane(f))
                ar = jnp.where(lane == cols - 1, 0.0, next_lane(a))
                flow = (f - fr) * (a - ar)
                total = total + (flow + jnp.where(lane == 0, f * a, prev_lane(flow)))
                for dq, dr in ((0, 1), (0, -1), (1, 0), (-1, 0)):
                    fj = u2[j, q + 1 + dq, pl.ds(r + dr, rows), :]
                    aj = adj[j, q + 1 + dq, pl.ds(r + dr, rows), :]
                    total = total + (f - fj) * (a - aj)
            scaled = -0.5 * sig[q + WIDE + 1, pl.ds(PAD + r, rows), :] * total
            dst[slot, pl.ds(r - PAD, rows), :] = scaled

    def copy_give(n):
        return remote(give.at[n], take.at[n], s_give.at[n], r_give.at[n], (mate, me))

    rows_mine = pl.ds(pl.multiple_of(half * side_x, PAD), half)
    rows_theirs = pl.ds(pl.multiple_of(half * (1 - side_x), PAD), half)

    def copy_x(n):
        ref = out.at[core * quarter + n, rows_mine]
        return remote(ref, ref, s_x.at[n], r_x.at[n], (across, me))

    def copy_own(n):
        ref = out.at[core * quarter + n, rows_mine]
        return remote(ref, ref, s_own.at[n], r_own.at[n], (mate, me))

    def copy_fwd(n):
        ref = out.at[core * quarter + n, rows_theirs]
        return remote(ref, ref, s_fwd.at[n], r_fwd.at[n], (mate, me))

    def giving(n, carry):
        partial((1 - core) * quarter + n, give, n)
        copy_give(n).start()
        return carry

    def keeping(n, carry):
        partial(core * quarter + n, pair, n)
        copy_give(n).wait_recv()
        for r, rows in ((0, half),):
            at = pl.multiple_of(half * side_x + r, PAD)
            value = pair[n, pl.ds(r, rows), :] + take[n, pl.ds(r, rows), :]
            out[core * quarter + n, pl.ds(at, rows), :] = reorder(value, order[...])
        copy_x(n).start()
        copy_own(n).start()
        return carry

    def passing(n, carry):
        copy_x(n).wait_recv()
        copy_fwd(n).start()
        return carry

    def ending(n, carry):
        copy_own(n).wait_recv()
        copy_fwd(n).wait_recv()
        for copy in (copy_give, copy_x, copy_own, copy_fwd):
            copy(n).wait_send()
        return carry

    def in_turn(n, carry):
        combine(give_first + n + 3, carry)
        giving(n + 1, carry)
        keeping(n, carry)
        return combine(keep_first + n + 3, carry)

    giving(0, 0)
    lax.fori_loop(keep_first, keep_first + 3, combine, 0)
    lax.fori_loop(0, quarter - 1, in_turn, 0)
    keeping(quarter - 1, 0)
    for body in (passing, ending):
        lax.fori_loop(0, quarter, body, 0)
    total.close()


def second_solve(slabs, nx, lc_half, lc_near, u_mine, u_first, u_rest, mean, back):
    depth, _, cols = lc_half.shape
    half = nx // 2
    frame = half + 2 * PAD
    plane = (frame + 2 * PAD, cols)
    wide = depth + 2 * WIDE
    quarter = depth // 2
    full = pl.BlockSpec(memory_space=VMEM)
    anywhere = pl.BlockSpec(memory_space=pl.ANY)
    pair = [DMA((2,)), DMA((2,))]
    return pl.pallas_call(
        functools.partial(second_kernel, slabs, nx),
        name="second_solve",
        out_shape=jax.ShapeDtypeStruct((depth, nx, cols), F32),
        in_specs=[full, full, anywhere, anywhere, anywhere, full, full],
        out_specs=full,
        scratch_shapes=[
            VMEM((wide + 2, *plane), F32),
            VMEM((wide, frame, cols), F32),
            VMEM((wide, frame, cols), F32),
            VMEM((wide, *plane), F32),
            VMEM((wide + 1, frame, cols), F32),
            VMEM((2, wide - 2, *plane), F32),
            VMEM((2, wide - 4, *plane), F32),
            VMEM((2, wide - 6, *plane), F32),
            VMEM((2, depth + 2, frame, cols), F32),
            VMEM((2, depth + 2, frame, cols), F32),
        ]
        + [VMEM((quarter, half, cols), F32)] * 3
        + [VMEM((2, WIDE - 1, half + PAD, cols), F32), VMEM((cols, cols), jnp.bfloat16)]
        + [DMA((2,)), DMA(()), DMA(())]
        + pair * 2
        + [DMA((quarter,))] * 8
        + sum_scratch(slabs, (1, 128), 8),
        compiler_params=pltpu.CompilerParams(
            collective_id=2, has_side_effects=True, vmem_limit_bytes=42 << 20
        ),
    )(lc_half, lc_near, u_mine, u_first, u_rest, mean, back)


def shards(slabs, log_cond, perturb, potentials, rec_depth, rec_plan):
    depth, nx, cols = log_cond.shape
    dipoles = rec_depth.shape[1]
    order = lax.broadcasted_iota(jnp.int32, rec_depth.shape, 0) * dipoles
    order = order + lax.broadcasted_iota(jnp.int32, rec_depth.shape, 1)
    keys = (rec_depth * (2 * dipoles) + order).reshape(-1)
    keys, cells = lax.sort((keys, rec_plan.reshape(-1)), num_keys=1, is_stable=False)
    arguments = (pltpu.with_memory_space_constraint(a, pltpu.HBM) for a in (log_cond, perturb, potentials[0]))
    tangent, mean, lc_half, lc_near, u_mine, u_first, u_rest = first_solve(slabs, *arguments)
    part = gather(keys, cells, tangent.reshape(depth * nx, cols), depth)
    data = share(slabs, part)
    u_first, data = lax.optimization_barrier((u_first, data))
    u_first = lax.ppermute(u_first, "src", [(i, (i + 2) % 4) for i in range(4)])
    back = scatter(keys, cells, data, depth, nx, cols)
    return second_solve(slabs, nx, lc_half, lc_near, u_mine, u_first, u_rest, mean, back)


def solution(mesh):
    in_specs = (
        P("slab", None, None),
        P("slab", None, None),
        P("src", "slab", None, None),
        P(),
        P(),
    )
    return jax.shard_map(
        functools.partial(shards, mesh.shape["slab"]),
        mesh=mesh,
        in_specs=in_specs,
        out_specs=P("slab", None, None),
        check_vma=False,
    )
```

```python
import functools

import jax
import jax.numpy as jnp
from jax import lax
from jax.experimental import pallas as pl
from jax.experimental.pallas import tpu as pltpu
from jax.sharding import PartitionSpec as P

MESH = pl.DeviceIdType.MESH
F32 = jnp.float32
VMEM = pltpu.VMEM
SMEM = pltpu.SMEM
DMA = pltpu.SemaphoreType.DMA
PAD = 8
WIDE = 4
EARLY = 3
ROWS = 64
THETA = (6.0, 2.0, 10.0)


def lane_iota(shape):
    return lax.broadcasted_iota(jnp.int32, shape, len(shape) - 1)


def fold(value):
    rows, cols = value.shape
    return jnp.sum(value.reshape(rows // 8, 8, cols), axis=0)


def next_lane(value):
    half = value.shape[1] // 2
    even, odd = value[:, :half], value[:, half:]
    return jnp.concatenate([odd, pltpu.roll(even, half - 1, 1)], axis=1)


def prev_lane(value):
    half = value.shape[1] // 2
    even, odd = value[:, :half], value[:, half:]
    return jnp.concatenate([pltpu.roll(odd, 1, 1), even], axis=1)


def lane_of(column, cols):
    return (column >> 1) + (column & 1) * (cols // 2)


def order_matrix(cols, back):
    row = lax.broadcasted_iota(jnp.int32, (cols, cols), 0)
    col = lax.broadcasted_iota(jnp.int32, (cols, cols), 1)
    hit = row == lane_of(col, cols) if back else col == lane_of(row, cols)
    return jnp.where(hit, 1.0, 0.0).astype(jnp.bfloat16)


def reorder(value, matrix):
    total = None
    for _ in range(3):
        piece = value.astype(jnp.bfloat16)
        value = value - piece.astype(F32)
        moved = jnp.dot(piece, matrix, preferred_element_type=F32)
        total = moved if total is None else total + moved
    return total


def chunks(count, start=0):
    out = []
    done = 0
    while done < count:
        rows = min(ROWS, count - done)
        out.append((start + done, rows))
        done += rows
    return out


def make_coefs(sig, dg, hx, hy, hz, start, stop, first, last, pieces, top=True):
    cols = sig.shape[-1]

    def body(q, carry):
        low_in = jnp.logical_and(q - 1 >= first, q <= last).astype(F32)
        for r, rows in pieces:
            here = sig[q + 1, pl.ds(PAD + r, rows), :]
            up = sig[q + 1, pl.ds(PAD + r + 1, rows), :]
            down = sig[q + 1, pl.ds(PAD + r - 1, rows), :]
            low = sig[q, pl.ds(PAD + r, rows), :]
            high = sig[q + 2, pl.ds(PAD + r, rows), :]
            lane = lane_iota(here.shape)
            right = jnp.where(lane == cols - 1, 0.0, next_lane(here))
            left = jnp.where(lane == 0, 0.0, prev_lane(here))
            hx[q, pl.ds(r, rows), :] = jnp.where(lane == cols - 1, 0.0, 0.5 * (here + right))
            hy[q, pl.ds(PAD + r, rows), :] = 0.5 * (here + up)
            hz[q, pl.ds(r, rows), :] = (0.5 * low_in) * (here + low)
            total = ((up + down) + (left + right)) + (low + high)
            dg[q, pl.ds(r, rows), :] = 3.0 * here + 0.5 * total
        return carry

    lax.fori_loop(start, stop, body, 0)
    if not top:
        return
    inside = jnp.logical_and(stop - 1 >= first, stop <= last).astype(F32)
    for r, rows in pieces:
        here = sig[stop + 1, pl.ds(PAD + r, rows), :]
        low = sig[stop, pl.ds(PAD + r, rows), :]
        hz[stop, pl.ds(r, rows), :] = (0.5 * inside) * (here + low)


def operator(v, p, dg, hx, hy, hz, q, r, rows):
    here = v[p, pl.ds(PAD + r, rows), :]
    wx = hx[q, pl.ds(r, rows), :]
    acc = dg[q, pl.ds(r, rows), :] * here
    acc = acc - wx * next_lane(here)
    acc = acc - prev_lane(wx * here)
    acc = acc - hy[q, pl.ds(PAD + r, rows), :] * v[p, pl.ds(PAD + r + 1, rows), :]
    acc = acc - hy[q, pl.ds(PAD + r - 1, rows), :] * v[p, pl.ds(PAD + r - 1, rows), :]
    acc = acc - hz[q, pl.ds(r, rows), :] * v[p - 1, pl.ds(PAD + r, rows), :]
    acc = acc - hz[q + 1, pl.ds(r, rows), :] * v[p + 1, pl.ds(PAD + r, rows), :]
    return here, acc


def zero_pads(ref, nx):
    zero = jnp.zeros((ref.shape[0], PAD, ref.shape[2]), F32)
    ref[:, pl.ds(0, PAD), :] = zero
    ref[:, pl.ds(PAD + nx, PAD), :] = zero


def splat(row, index):
    return jnp.sum(jnp.where(lane_iota(row.shape) == index, row, 0.0), axis=1, keepdims=True)


def solve_small(row, scale, thetas, n=0):
    gram = {}
    for i in range(4):
        for j in range(i + 1):
            gram[i, j] = gram[j, i] = splat(row, n)
            n += 1
    last = splat(row, n)
    mat = {}
    for i in range(4):
        for j in range(i + 1):
            if j == 3:
                mat[i, j] = last
            else:
                mat[i, j] = scale * gram[i, j + 1] + thetas[j] * gram[i, j]
    low, inv = {}, {}
    for j in range(4):
        pivot = mat[j, j]
        for k in range(j):
            pivot = pivot - low[j, k] * low[j, k] * mat["d", k]
        mat["d", j] = pivot
        good = pivot > 1e-7 * mat[j, j]
        inv[j] = jnp.where(good, 1.0 / jnp.where(good, pivot, 1.0), 0.0)
        for i in range(j + 1, 4):
            value = mat[i, j]
            for k in range(j):
                value = value - low[i, k] * low[j, k] * mat["d", k]
            low[i, j] = value * inv[j]
    y = []
    for i in range(4):
        value = gram[i, 0]
        for k in range(i):
            value = value - low[i, k] * y[k]
        y.append(value)
    c = [None] * 4
    for i in reversed(range(4)):
        value = y[i] * inv[i]
        for k in range(i + 1, 4):
            value = value - low[k, i] * c[k]
        c[i] = value
    return c


def pack_row(accs):
    lane = lane_iota((1, 128))
    row = jnp.zeros((1, 128), F32)
    for n, acc in enumerate(accs):
        total = jnp.sum(jnp.sum(acc, axis=0, keepdims=True), axis=1, keepdims=True)
        row = row + jnp.where(lane == n, total, 0.0)
    return row


def remote(src_ref, dst_ref, send_sem, recv_sem, target):
    return pltpu.make_async_remote_copy(
        src_ref=src_ref,
        dst_ref=dst_ref,
        send_sem=send_sem,
        recv_sem=recv_sem,
        device_id=target,
        device_id_type=MESH,
    )


def flip(src, bit):
    return src + bit - 2 * bit * (lax.rem(src // bit, 2))


def partners(me, slabs):
    near = 4
    fours = slabs // near
    place, four = lax.rem(me, near), me // near
    return (
        [four * near + lax.rem(place + d, near) for d in range(1, near)],
        [lax.rem(four + d, fours) * near + place for d in range(1, fours)],
    )


def pair_group(me):
    place = lax.rem(me, 4)
    return [me - place + lax.rem(place + d, 4) for d in range(4)]


def signal_all(src, me, slabs, others):
    barrier = pltpu.get_barrier_semaphore()
    targets = [(src, t) for group in partners(me, slabs) for t in group] + others
    for target in targets:
        pl.semaphore_signal(barrier, inc=1, device_id=target, device_id_type=MESH)
    return barrier, len(targets)


class Sum:
    def __init__(self, src, me, slabs, levels, across=None):
        groups = [[(src, t) for t in group] for group in partners(me, slabs)]
        if across is not None:
            groups[0] += [(across, t) for t in pair_group(me)]
        self.levels = [(level, group) for level, group in zip(levels, groups) if group]

    def send(self, n, value):
        (buf, send_sem, recv_sem), group = self.levels[n]
        buf[0] = value
        for d, target in enumerate(group):
            remote(buf.at[0], buf.at[d + 1], send_sem, recv_sem, target).start()

    def _wait(self, n, which):
        level, group = self.levels[n]
        rest = level[0].at[pl.ds(1, len(group))]
        pltpu.make_async_copy(rest, rest, level[which]).wait()

    def receive(self, n):
        self._wait(n, 2)
        return jnp.sum(self.levels[n][0][0][...], axis=0)

    def start(self, value):
        self.send(0, value)

    def middle(self):
        value = self.receive(0)
        if len(self.levels) > 1:
            self.send(1, value)
        return value

    def end(self, value):
        return self.receive(1) if len(self.levels) > 1 else value

    def whole(self, value):
        self.start(value)
        return self.end(self.middle())

    def close(self):
        for n in range(len(self.levels)):
            self._wait(n, 1)


def sum_scratch(slabs, shape, first=4):
    return [
        VMEM((first, *shape), F32), DMA(()), DMA(()),
        VMEM((max(slabs // 4, 2), *shape), F32), DMA(()), DMA(()),
    ]


def sum_levels(refs):
    return (refs[0:3], refs[3:6])


def first_kernel(
    slabs, lc_in, pt_in, u, tan, mean_out, lc_half, lc_near, u_mine, u_first, u_rest,
    lc, pt, lch, uh, sig, wgt, uw, dg, hx, hy, hz, v0, v1, v2, v3, pth, edge, order,
    s_load, s_take, s_first, r_first, s_c, r_c, s_x, r_x, s_core, r_core, s_v, r_v, s_e, r_e, *sums,
):
    src = lax.axis_index("src")
    me = lax.axis_index("slab")
    depth, nx, cols = lc.shape
    half = nx // 2
    has_low = me > 0
    has_high = me < slabs - 1
    core, side_x = lax.rem(src, 2), src // 2
    mate, across = flip(src, 1), flip(src, 2)
    inner_rows = pl.ds(PAD, nx)
    loads = [
        pltpu.make_async_copy(u, uw.at[pl.ds(1, depth), inner_rows], s_load.at[0]),
        pltpu.make_async_copy(lc_in, lc, s_load.at[1]),
        pltpu.make_async_copy(pt_in, pt, s_load.at[2]),
    ]
    for load in loads:
        load.start()
    ring = [(src, lax.rem(me + 1, slabs)), (src, lax.rem(me + slabs - 1, slabs))]
    barrier, count = signal_all(src, me, slabs, ring + [(mate, me), (across, me)])
    order[...] = order_matrix(cols, False)

    def shuffle(q, carry):
        for n in (0, 1):
            for ref, plane, first in ((lc, q, 0), (pt, q, 0), (uw, q + 1, PAD)):
                rows = pl.ds(first + n * half, half)
                ref[plane, rows, :] = reorder(ref[plane, rows, :], order[...])
        return carry

    for load in loads:
        load.wait()
    lax.fori_loop(0, 2, lambda i, c: shuffle(i * (depth - 1), c), 0)
    pl.semaphore_wait(barrier, count)
    mean_sum = Sum(src, me, slabs, sum_levels(sums[0:6]))
    mom_sum = Sum(src, me, slabs, sum_levels(sums[6:12]))

    def arrives(side):
        return has_low if side == 0 else has_high

    def below(side):
        return me + 1 if side == 0 else me - 1

    def sends(side):
        return has_high if side == 0 else has_low

    def near(side):
        return depth - 1 if side == 0 else 0

    def part(n):
        return pl.ds(n * half, half)

    def copy_u(side, n, to):
        return remote(
            uw.at[1 + near(side), pl.ds(PAD + n * half, half)], uh.at[side, part(n)],
            s_first.at[side, n], r_first.at[side, n], (src, to),
        )

    my_rows = pl.ds(pl.multiple_of(half * side_x, PAD), half)
    their_rows = pl.ds(pl.multiple_of(half * (1 - side_x), PAD), half)

    def copy_c(ref, dst, side, to):
        return remote(
            ref.at[near(side), my_rows], dst.at[side, my_rows], s_c.at[side], r_c.at[side], (src, to)
        )

    def swap(ref, side, rows):
        return remote(ref.at[side, rows], ref.at[side, rows], s_x.at[side], r_x.at[side], (across, me))

    def forward(ref, side):
        return remote(ref.at[side], ref.at[side], s_core.at[side], r_core.at[side], (mate, me))

    def by_core(body):
        pl.when(core == 0)(lambda: body(lc, lch))
        pl.when(core == 1)(lambda: body(pt, pth))

    for side in (0, 1):
        @pl.when(sends(side))
        def _():
            by_core(lambda ref, dst: copy_c(ref, dst, side, below(side)).start())

    for ref in (sig, wgt, uw, hy, v0, v1, v2, v3):
        zero_pads(ref, nx)
    for side in (0, 1):
        @pl.when(sends(side))
        def _():
            copy_c(lc, lch, side, me).wait_send()

    for n in (0, 1):
        for side in (0, 1):
            pl.when(sends(side))(lambda side=side, n=n: copy_u(side, n, below(side)).start())

    def own(q, acc):
        for r, rows in chunks(nx):
            value = jnp.exp(lc[q, pl.ds(r, rows), :])
            sig[q + 1, pl.ds(PAD + r, rows), :] = value
            wgt[q + 1, pl.ds(PAD + r, rows), :] = value * pt[q, pl.ds(r, rows), :]
            acc = acc + fold(value)
        return acc

    lax.fori_loop(1, depth - 1, shuffle, 0)
    acc = lax.fori_loop(0, depth, own, jnp.zeros((8, cols), F32))
    mean_sum.start(pack_row([acc]))

    fields = (v0, v1, v2, v3)
    for ref in fields:
        for side in (0, 1):
            def clear(ref=ref, side=side):
                ref[side * (depth + 1), pl.ds(PAD, nx), :] = jnp.zeros((nx, cols), F32)

            if ref is v3:
                clear()
            else:
                pl.when(jnp.logical_not(arrives(side)))(clear)
    mean_part = mean_sum.middle()

    for side in (0, 1):
        @pl.when(arrives(side))
        def _():
            def body(ref, dst):
                copy_c(ref, dst, side, me).wait_recv()
                swap(dst, side, my_rows).start()

            by_core(body)
    for side in (0, 1):
        @pl.when(arrives(side))
        def _():
            def body(ref, dst):
                swap(dst, side, their_rows).wait_recv()
                forward(dst, side).start()

            by_core(body)

    def rhs_rows(q, pieces):
        for r, rows in pieces:
            c = wgt[q + 1, pl.ds(PAD + r, rows), :]
            f = uw[q + 1, pl.ds(PAD + r, rows), :]
            lane = lane_iota(c.shape)
            cr = jnp.where(lane == cols - 1, 0.0, next_lane(c))
            fr = jnp.where(lane == cols - 1, 0.0, next_lane(f))
            flow = (c + cr) * (f - fr)
            total = flow + jnp.where(lane == 0, c * f, -prev_lane(flow))
            for dq, dr in ((0, 1), (0, -1), (1, 0), (-1, 0)):
                cj = wgt[q + 1 + dq, pl.ds(PAD + r + dr, rows), :]
                fj = uw[q + 1 + dq, pl.ds(PAD + r + dr, rows), :]
                total = total + (c + cj) * (f - fj)
            v0[q + 1, pl.ds(PAD + r, rows), :] = -0.5 * total

    def copy_v(k, side, n, to):
        plane = depth if side == 0 else 1
        halo = 0 if side == 0 else depth + 1
        rows = pl.ds(PAD + n * half, half)
        ref = fields[k]
        return remote(
            ref.at[plane, rows], ref.at[halo, rows], s_v.at[k, side, n], r_v.at[k, side, n], (src, to)
        )

    def send_edge(k, side, n):
        out = 1 - side

        @pl.when(sends(out))
        def _():
            copy_v(k, out, n, below(out)).start()

    for n in (0, 1):
        for side in (0, 1):
            plane = 0 if side == 0 else depth + 1

            @pl.when(arrives(side))
            def _():
                if n == 0:
                    pl.when(core == 0)(lambda: forward(pth, side).wait_recv())
                    pl.when(core == 1)(lambda: forward(lch, side).wait_recv())
                copy_u(side, n, me).wait_recv()
                for r, rows in chunks(half, n * half):
                    value = jnp.exp(lch[side, pl.ds(r, rows), :])
                    sig[plane, pl.ds(PAD + r, rows), :] = value
                    wgt[plane, pl.ds(PAD + r, rows), :] = value * pth[side, pl.ds(r, rows), :]
                    uw[plane, pl.ds(PAD + r, rows), :] = uh[side, pl.ds(r, rows), :]

            @pl.when(jnp.logical_not(arrives(side)))
            def _():
                for ref in (sig, wgt, uw):
                    ref[plane, pl.ds(PAD + n * half, half), :] = jnp.zeros((half, cols), F32)
                lch[side, part(n), :] = jnp.zeros((half, cols), F32)

            rhs_rows(0 if side == 0 else depth - 1, chunks(half, n * half))
            send_edge(0, side, n)

    frame_rows = half + PAD
    mine = half * side_x - PAD * side_x
    theirs = (half - PAD) - mine
    takes = []
    for n, (ref, dst, first, at) in enumerate((
        (lc, lc_half, 0, mine),
        (lch, lc_near, 0, mine),
        (uw, u_mine, 0, PAD + mine),
        (uw, u_first, 0, PAD + theirs),
        (uw, u_rest, EARLY, PAD + theirs),
    )):
        rows = pl.ds(pl.multiple_of(at, PAD), frame_rows)
        takes.append(pltpu.make_async_copy(ref.at[pl.ds(first, dst.shape[0]), rows], dst, s_take.at[n]))
    for take in takes:
        take.start()

    def inner(body, carry):
        return lax.fori_loop(1, depth - 1, body, carry)

    def rhs_plane(q, carry):
        rhs_rows(q, chunks(nx))
        return carry

    inner(rhs_plane, 0)
    first, last = -me * depth, (slabs - me) * depth - 1
    make_coefs(sig, dg, hx, hy, hz, 0, depth, first, last, chunks(nx))

    mean = splat(mean_sum.end(mean_part), 0) * (1.0 / (slabs * depth * nx * cols))
    mean_out[...] = jnp.broadcast_to(mean, (8, 128))
    scale = 6.0 * mean
    inv = 1.0 / scale

    zero = jnp.zeros((8, cols), F32)
    dots = []
    for k in range(3):
        shift = THETA[k] * mean * inv

        def step(q, accs, pieces=None, k=k, shift=shift):
            accs = list(accs)
            for r, rows in pieces or chunks(nx):
                here, image = operator(fields[k], q + 1, dg, hx, hy, hz, q, r, rows)
                new = inv * image - shift * here
                fields[k + 1][q + 1, pl.ds(PAD + r, rows), :] = new
                if k == 0:
                    accs[0] = accs[0] + fold(here * here)
                for i in range(k + 1):
                    other = here if i == k else fields[i][q + 1, pl.ds(PAD + r, rows), :]
                    accs[i + (k == 0)] = accs[i + (k == 0)] + fold(new * other)
                accs[-1] = accs[-1] + fold(new * new)
            return tuple(accs)

        accs = inner(step, (zero,) * (3 if k == 0 else k + 2))
        for n in (0, 1):
            for side in (0, 1):
                pl.when(arrives(side))(lambda side=side, n=n, k=k: copy_v(k, side, n, me).wait_recv())
                accs = step(0 if side == 0 else depth - 1, accs, chunks(half, n * half))
                if k < 2:
                    send_edge(k + 1, side, n)
        dots.extend(accs)

    def copy_edge(side, to):
        plane = depth if side == 0 else 1
        return remote(
            v3.at[plane, pl.ds(PAD + side * half, half)], edge.at[side], s_e.at[side], r_e.at[side], (src, to)
        )

    for side in (0, 1):
        pl.when(sends(side))(lambda side=side: copy_edge(side, below(side)).start())
    def energy(q, acc):
        for r, rows in chunks(nx):
            here, image = operator(v3, q + 1, dg, hx, hy, hz, q, r, rows)
            acc = acc + fold(here * image)
        return acc

    acc = lax.fori_loop(0, depth, energy, zero)
    for side in (0, 1):
        got = arrives(side)
        pl.when(got)(lambda side=side: copy_edge(side, me).wait_recv())

        @pl.when(jnp.logical_not(got))
        def _():
            edge[side] = jnp.zeros((half, cols), F32)

        for r, rows in chunks(half):
            at = side * half + r
            face = hz[side * depth, pl.ds(at, rows), :] * v3[1 + side * (depth - 1), pl.ds(PAD + at, rows), :]
            acc = acc - 2.0 * fold(face * edge[side, pl.ds(r, rows), :])
    dots.append(acc)
    mom_sum.start(pack_row(dots))
    value = mom_sum.middle()

    row = mom_sum.end(value)
    c = solve_small(row, scale, [t * mean for t in THETA])

    def combine(q, carry):
        for r, rows in chunks(nx):
            value = c[0] * v0[q + 1, pl.ds(PAD + r, rows), :]
            for i in (1, 2, 3):
                value = value + c[i] * fields[i][q + 1, pl.ds(PAD + r, rows), :]
            tan[q, pl.ds(r, rows), :] = value
        return carry

    lax.fori_loop(0, depth, combine, 0)

    for take in takes:
        take.wait()
    for side in (0, 1):
        @pl.when(sends(side))
        def _():
            copy_edge(side, me).wait_send()
            for n in (0, 1):
                copy_u(side, n, me).wait_send()
                for k in range(3):
                    copy_v(k, side, n, me).wait_send()

        @pl.when(arrives(side))
        def _():
            swap(lch, side, my_rows).wait_send()
            forward(lch, side).wait_send()
    mean_sum.close()
    mom_sum.close()


def first_solve(slabs, lc, pt, u):
    depth, nx, cols = lc.shape
    plane = (nx + 2 * PAD, cols)
    half = nx // 2
    full = pl.BlockSpec(memory_space=VMEM)
    pair = (DMA((2,)), DMA((2,)))
    return pl.pallas_call(
        functools.partial(first_kernel, slabs),
        name="first_solve",
        out_shape=[
            jax.ShapeDtypeStruct((depth, nx, cols), F32),
            jax.ShapeDtypeStruct((8, 128), F32),
            *(
                jax.ShapeDtypeStruct((planes, half + PAD, cols), F32)
                for planes in (depth, 2, depth + 2, EARLY, depth + 2 - EARLY)
            ),
        ],
        in_specs=[pl.BlockSpec(memory_space=pltpu.HBM)] * 3,
        out_specs=[full] * 7,
        scratch_shapes=[VMEM((depth, nx, cols), F32)] * 2
        + [VMEM((2, nx, cols), F32)] * 2
        + [VMEM((depth + 2, *plane), F32)] * 3
        + [
            VMEM((depth, nx, cols), F32),
            VMEM((depth, nx, cols), F32),
            VMEM((depth, *plane), F32),
            VMEM((depth + 1, nx, cols), F32),
        ]
        + [VMEM((depth + 2, *plane), F32)] * 4
        + [VMEM((2, nx, cols), F32), VMEM((2, half, cols), F32), VMEM((cols, cols), jnp.bfloat16)]
        + [DMA((3,)), DMA((5,)), DMA((2, 2)), DMA((2, 2)), *pair, *pair, *pair]
        + [DMA((3, 2, 2)), DMA((3, 2, 2)), *pair]
        + sum_scratch(slabs, (1, 128)) * 2,
        compiler_params=pltpu.CompilerParams(
            collective_id=0, has_side_effects=True, vmem_limit_bytes=43 << 20
        ),
    )(lc, pt, u)


def over_window(group, ordered, first_key, last_key, keys, cells, keys_s, cells_s, sems, body):
    start, stop = (
        jnp.sum(jnp.where(ordered[...] < bound, 1.0, 0.0)).astype(jnp.int32) for bound in (first_key, last_key)
    )
    size = keys_s.shape[0]

    def piece(w, carry):
        base = pl.multiple_of(w * size, size)
        copies = [
            pltpu.make_async_copy(ref.at[pl.ds(base, size)], dst, sems.at[n])
            for n, (ref, dst) in enumerate(((keys, keys_s), (cells, cells_s)))
        ]
        for copy in copies:
            copy.start()
        for copy in copies:
            copy.wait()
        low = jnp.maximum(start - base, 0)
        high = jnp.minimum(stop - base, size)

        def step(g, carry):
            body(low + g * group, high)
            return carry

        return lax.fori_loop(0, (high - low + group - 1) // group, step, carry)

    lax.fori_loop(start // size, (stop + size - 1) // size, piece, 0)


def window_scratch(entries):
    size = min(1024, entries)
    return [SMEM((size,), jnp.int32), SMEM((size,), jnp.int32), DMA((2,))]


def bits(count):
    assert count & (count - 1) == 0
    return count.bit_length() - 1


def gather_kernel(group, depth, dipoles, ordered, keys, cells, field, out, keys_s, cells_s, sems):
    me = lax.axis_index("slab")
    out[...] = jnp.zeros_like(out)
    lines, cols = field.shape
    nx = lines // depth
    entries = 2 * dipoles
    lane = lane_iota((1, cols))
    short = lane_iota((1, 128))
    base = me * lines

    def body(least, stop):
        parts = []
        j = jnp.minimum(least, keys_s.shape[0] - group)
        for e in range(group):
            key, cell = keys_s[j + e], cells_s[j + e]
            o = key & (entries - 1)
            k = o & (dipoles - 1)
            line = ((key >> bits(entries)) << bits(nx)) + (cell >> bits(cols)) - base
            inside = jnp.logical_and(j + e >= least, j + e < stop)
            lane_at = jnp.where(inside, lane_of(cell & (cols - 1), cols), -1)
            picked = jnp.where(lane == lane_at, field[pl.ds(jnp.where(inside, line, 0), 1), :], 0.0)
            value = jnp.sum(picked, axis=1, keepdims=True)
            value = jnp.where(o < dipoles, value, -value)
            parts.append((k >> 7, jnp.where(short == (k & 127), value, 0.0)))
        for line, value in parts:
            out[pl.ds(line, 1), :] = out[pl.ds(line, 1), :] + value

    first = me * depth * entries
    over_window(group, ordered, first, first + depth * entries, keys, cells, keys_s, cells_s, sems, body)


def gather(keys, cells, field, depth):
    anywhere = pl.BlockSpec(memory_space=pl.ANY)
    full = pl.BlockSpec(memory_space=VMEM)
    entries = keys.shape[0]
    return pl.pallas_call(
        functools.partial(gather_kernel, 16, depth, entries // 2),
        name="gather",
        out_shape=jax.ShapeDtypeStruct((entries // 256, 128), F32),
        in_specs=[full, anywhere, anywhere, full],
        out_specs=full,
        scratch_shapes=window_scratch(entries),
        compiler_params=pltpu.CompilerParams(vmem_limit_bytes=8 << 20),
    )(keys.reshape(-1, 128), keys, cells, field)


def share_kernel(slabs, part, out, s_x, r_x, *sums):
    src = lax.axis_index("src")
    me = lax.axis_index("slab")
    side_x = src // 2
    across = flip(src, 2)
    barrier, count = signal_all(src, me, slabs, [(across, me)])
    pl.semaphore_wait(barrier, count)
    total = Sum(src, me, slabs, sum_levels(sums))
    out[side_x] = total.whole(part[...])
    copy = remote(out.at[side_x], out.at[side_x], s_x, r_x, (across, me))
    copy.start()
    copy.wait()
    total.close()


def share(slabs, part):
    full = pl.BlockSpec(memory_space=VMEM)
    return pl.pallas_call(
        functools.partial(share_kernel, slabs),
        name="share_data",
        out_shape=jax.ShapeDtypeStruct((2, *part.shape), F32),
        in_specs=[full],
        out_specs=full,
        scratch_shapes=[DMA(()), DMA(())] + sum_scratch(slabs, part.shape),
        compiler_params=pltpu.CompilerParams(
            collective_id=1, has_side_effects=True, vmem_limit_bytes=8 << 20
        ),
    )(part)


def scatter_kernel(group, depth, nx, lines, ordered, keys, cells, data, out, keys_s, cells_s, sems):
    me = lax.axis_index("slab")
    side_x = lax.axis_index("src") // 2
    total, cols = out.shape[0], out.shape[1] // 2
    planes = total // lines
    entries = keys.shape[0]
    dipoles = entries // 2
    lane = lane_iota((1, cols))
    low = me * depth - WIDE
    row_base = (nx // 2) * side_x - 2 * PAD
    plane_base = low * lines + row_base

    def clear(q, carry):
        out[pl.ds(pl.multiple_of(q * lines, 8), lines), :] = jnp.zeros((lines, 2 * cols), F32)
        return carry

    lax.fori_loop(0, planes, clear, 0)

    def body(least, stop):
        parts = []
        j = jnp.minimum(least, keys_s.shape[0] - group)
        for e in range(group):
            key, cell = keys_s[j + e], cells_s[j + e]
            o = key & (entries - 1)
            k = o & (dipoles - 1)
            row = cell >> bits(cols)
            inside = jnp.logical_and(j + e >= least, j + e < stop)
            inside = jnp.logical_and(inside, jnp.logical_and(row >= row_base + PAD, row < row_base + lines - PAD))
            hit = lane == jnp.where(inside, lane_of(cell & (cols - 1), cols), -1)
            at = jnp.where(inside, (key >> bits(entries)) * lines + row - plane_base, 0)
            signed = jnp.where(hit, jnp.where(o < dipoles, 1.0, -1.0), 0.0)
            values = [signed * data[k + n * dipoles] for n in (0, 1)]
            parts.append((at, jnp.concatenate(values, axis=1)))
        for at, value in parts:
            out[pl.ds(at, 1), :] = out[pl.ds(at, 1), :] + value

    over_window(
        group, ordered, low * entries, (low + planes) * entries, keys, cells, keys_s, cells_s, sems, body
    )


def scatter(keys, cells, data, depth, nx, cols):
    smem = pl.BlockSpec(memory_space=SMEM)
    anywhere = pl.BlockSpec(memory_space=pl.ANY)
    full = pl.BlockSpec(memory_space=VMEM)
    lines = nx // 2 + 4 * PAD
    planes = depth + 2 * WIDE
    back = pl.pallas_call(
        functools.partial(scatter_kernel, 8, depth, nx, lines),
        name="scatter",
        out_shape=jax.ShapeDtypeStruct((planes * lines, 2 * cols), F32),
        in_specs=[full, anywhere, anywhere, smem],
        out_specs=full,
        scratch_shapes=window_scratch(keys.shape[0]),
        compiler_params=pltpu.CompilerParams(vmem_limit_bytes=8 << 20),
    )(keys.reshape(-1, 128), keys, cells, data.reshape(-1))
    return back.reshape(planes, lines, 2 * cols)


def second_kernel(
    slabs, nx, lc_half, lc_near, u_mine, u_first, u_rest, mean_in, v0, out,
    sig, dg, hx, hy, hz, v1, v2, v3, u2, adj, give, take, pair, far, order,
    s_load, s_u, r_u, s_far, r_far, s_c2, r_c2, s_give, r_give, s_x, r_x, s_own, r_own, s_fwd, r_fwd,
    *sums,
):
    src = lax.axis_index("src")
    me = lax.axis_index("slab")
    depth, _, cols = out.shape
    half = nx // 2
    frame = half + 2 * PAD
    frame_rows = half + PAD
    quarter = depth // 2
    core, side_x = lax.rem(src, 2), src // 2
    mate, across = flip(src, 1), flip(src, 2)
    wide = depth + 2 * WIDE
    ring = [(src, lax.rem(me + 1, slabs)), (src, lax.rem(me + slabs - 1, slabs))]
    barrier, count = signal_all(src, me, slabs, ring + [(mate, me)] + [(across, t) for t in pair_group(me)])
    total = Sum(src, me, slabs, sum_levels(sums), across)
    order[...] = order_matrix(cols, True)
    owned = chunks(half, PAD)
    rims = [(0, PAD), (PAD + half, PAD)]
    every = rims[:1] + owned + rims[1:]

    zero_pads(sig, frame)
    zero_pads(hy, frame)
    for ref in (v1, v2, v3):
        for j in (0, 1):
            zero_pads(ref.at[j], frame)

    outside = pl.ds(pl.multiple_of(PAD + (half + PAD) * side_x, PAD), PAD)
    u2[:, :, pl.ds(pl.multiple_of((half + PAD) * side_x, PAD), PAD), :] = jnp.zeros((2, depth + 2, PAD, cols), F32)
    frame_mine = pl.ds(pl.multiple_of(PAD * (1 - side_x), PAD), frame_rows)
    frame_theirs = pl.ds(pl.multiple_of(PAD * side_x, PAD), frame_rows)
    early = pl.ds(0, EARLY)
    late = pl.ds(EARLY, depth + 2 - EARLY)
    loads = [
        pltpu.make_async_copy(u_mine, u2.at[side_x, :, frame_mine], s_load.at[0]),
        pltpu.make_async_copy(u_first, u2.at[1 - side_x, early, frame_mine], s_load.at[1]),
    ]
    for load in loads:
        load.start()
    low_in, high_in = (me > 0).astype(F32), (me < slabs - 1).astype(F32)

    def conductivity(ref, count, first, factor=None):
        def body(n, carry):
            for r, rows in chunks(frame_rows):
                to = pl.multiple_of(PAD + PAD * (1 - side_x) + r, PAD)
                value = jnp.exp(ref[n, pl.ds(r, rows), :])
                sig[first + 1 + n, pl.ds(to, rows), :] = value if factor is None else factor * value
            sig[first + 1 + n, outside, :] = jnp.zeros((PAD, cols), F32)
            return carry

        lax.fori_loop(0, count, body, 0)

    conductivity(lc_half, depth, WIDE)
    conductivity(lc_near, 1, WIDE - 1, low_in)
    conductivity(lc_near.at[pl.ds(1, 1)], 1, WIDE + depth, high_in)

    arrives = (me > 0, me < slabs - 1)
    sends = (me < slabs - 1, me > 0)
    to_slab = (me + 1, me - 1)
    part = -(-frame_rows // (2 * PAD)) * PAD
    fetched = pl.ds(pl.multiple_of((frame_rows - part) * core, PAD), part)
    given = pl.ds(pl.multiple_of(part * core, PAD), frame_rows - part)
    taken = pl.ds(pl.multiple_of(part * (1 - core), PAD), frame_rows - part)

    def copy_far(side, to):
        planes = pl.ds(depth - WIDE if side == 0 else 1, WIDE - 1)
        return remote(lc_half.at[planes, fetched], far.at[side, :, fetched], s_far.at[side], r_far.at[side], (src, to))

    def share_far(side, rows):
        ref = far.at[side, :, rows]
        return remote(ref, ref, s_c2.at[side], r_c2.at[side], (mate, me))

    copy_rest = remote(u_rest, u2.at[side_x, late, frame_theirs], s_u, r_u, (across, me))
    pl.semaphore_wait(barrier, count)
    for side in (0, 1):
        pl.when(sends[side])(lambda side=side: copy_far(side, to_slab[side]).start())
    copy_rest.start()

    first, last = WIDE - me * depth, WIDE + (slabs - me) * depth - 1
    low_open, high_open = side_x.astype(F32), 1.0 - side_x.astype(F32)

    def coefs(start, stop, top=True):
        make_coefs(sig, dg, hx, hy, hz, start, stop, first, last, every, top)

        def close(q, carry):
            for line, factor in ((2 * PAD - 1, low_open), (2 * PAD + half - 1, high_open)):
                hy[q, pl.ds(line, 1), :] = hy[q, pl.ds(line, 1), :] * factor
            return carry

        lax.fori_loop(start, stop, close, 0)

    mean = mean_in[0:1, 0:1]
    scale = 6.0 * mean
    inv = 1.0 / scale
    zero = jnp.zeros((8, cols), F32)
    fields = [(v0.at[:, :, pl.ds(j * cols, cols)], v1.at[j], v2.at[j], v3.at[j]) for j in (0, 1)]
    sums_of = {}

    def run(k, start, stop, dotted):
        shift = THETA[k] * mean * inv
        for j in (0, 1):
            def step(q, accs, j=j):
                accs = list(accs)
                for r, rows in every:
                    here, image = operator(fields[j][k], q - k, dg, hx, hy, hz, q, r, rows)
                    new = inv * image - shift * here
                    fields[j][k + 1][q - k - 1, pl.ds(PAD + r, rows), :] = new
                    if not dotted or (r, rows) not in owned:
                        continue
                    if k == 0:
                        accs[0] = accs[0] + fold(here * here)
                    for i in range(k + 1):
                        other = here if i == k else fields[j][i][q - i, pl.ds(PAD + r, rows), :]
                        accs[i + (k == 0)] = accs[i + (k == 0)] + fold(new * other)
                    accs[-1] = accs[-1] + fold(new * new)
                return tuple(accs)

            accs = sums_of.get((j, k), (zero,) * (3 if k == 0 else k + 2)) if dotted else ()
            accs = lax.fori_loop(start, stop, step, accs)
            if dotted:
                sums_of[j, k] = accs

    top = WIDE + depth
    coefs(WIDE, top)
    run(0, WIDE, top, True)
    run(1, WIDE + 1, top - 1, True)
    for side in (0, 1):
        @pl.when(arrives[side])
        def _():
            copy_far(side, me).wait_recv()
            share_far(side, given).start()

        @pl.when(jnp.logical_not(arrives[side]))
        def _():
            far[side] = jnp.zeros(far.shape[1:], F32)

    run(2, WIDE + 2, top - 2, True)
    for side in (0, 1):
        pl.when(arrives[side])(lambda side=side: share_far(side, taken).wait_recv())
    conductivity(far.at[0], WIDE - 1, 0, low_in)
    conductivity(far.at[1], WIDE - 1, top + 1, high_in)
    coefs(1, WIDE, False)
    coefs(top, wide - 1)
    for k in range(3):
        run(k, k + 1, WIDE, False)
        if k:
            run(k, WIDE, WIDE + k, True)
            run(k, top - k, top, True)
        run(k, top, wide - k - 1, False)
    dots = [[acc for k in range(3) for acc in sums_of[j, k]] for j in (0, 1)]

    for j in (0, 1):
        def energy(q, acc, j=j):
            for r, rows in owned:
                here, image = operator(v3.at[j], q + 1, dg, hx, hy, hz, q + WIDE, r, rows)
                acc = acc + fold(here * image)
            return acc

        dots[j].append(lax.fori_loop(0, depth, energy, zero))

    row = total.whole(pack_row(dots[0] + dots[1]))
    thetas = [t * mean for t in THETA]
    coef = [solve_small(row, scale, thetas, n) for n in (0, len(dots[0]))]

    def combine(q, carry):
        for j in (0, 1):
            c = coef[j]
            for r, rows in every:
                value = c[3] * v3[j, q, pl.ds(PAD + r, rows), :]
                for i, ref in enumerate(fields[j][:3]):
                    value = value + c[i] * ref[q + 3 - i, pl.ds(PAD + r, rows), :]
                adj[j, q, pl.ds(r, rows), :] = value
        return carry

    give_first, keep_first = (1 - core) * quarter, core * quarter
    lax.fori_loop(give_first, give_first + 3, combine, 0)
    for load in loads:
        load.wait()
    copy_rest.wait()
    for side in (0, 1):
        pl.when(sends[side])(lambda side=side: copy_far(side, me).wait_send())
        pl.when(arrives[side])(lambda side=side: share_far(side, given).wait_send())

    def partial(q, dst, slot):
        for r, rows in owned:
            total = jnp.zeros((rows, cols), F32)
            for j in (0, 1):
                f = u2[j, q + 1, pl.ds(r, rows), :]
                a = adj[j, q + 1, pl.ds(r, rows), :]
                lane = lane_iota(f.shape)
                fr = jnp.where(lane == cols - 1, 0.0, next_lane(f))
                ar = jnp.where(lane == cols - 1, 0.0, next_lane(a))
                flow = (f - fr) * (a - ar)
                total = total + (flow + jnp.where(lane == 0, f * a, prev_lane(flow)))
                for dq, dr in ((0, 1), (0, -1), (1, 0), (-1, 0)):
                    fj = u2[j, q + 1 + dq, pl.ds(r + dr, rows), :]
                    aj = adj[j, q + 1 + dq, pl.ds(r + dr, rows), :]
                    total = total + (f - fj) * (a - aj)
            scaled = -0.5 * sig[q + WIDE + 1, pl.ds(PAD + r, rows), :] * total
            dst[slot, pl.ds(r - PAD, rows), :] = scaled

    def copy_give(n):
        return remote(give.at[n], take.at[n], s_give.at[n], r_give.at[n], (mate, me))

    rows_mine = pl.ds(pl.multiple_of(half * side_x, PAD), half)
    rows_theirs = pl.ds(pl.multiple_of(half * (1 - side_x), PAD), half)

    def copy_x(n):
        ref = out.at[core * quarter + n, rows_mine]
        return remote(ref, ref, s_x.at[n], r_x.at[n], (across, me))

    def copy_own(n):
        ref = out.at[core * quarter + n, rows_mine]
        return remote(ref, ref, s_own.at[n], r_own.at[n], (mate, me))

    def copy_fwd(n):
        ref = out.at[core * quarter + n, rows_theirs]
        return remote(ref, ref, s_fwd.at[n], r_fwd.at[n], (mate, me))

    def giving(n, carry):
        partial((1 - core) * quarter + n, give, n)
        copy_give(n).start()
        return carry

    def keeping(n, carry):
        partial(core * quarter + n, pair, n)
        copy_give(n).wait_recv()
        for r, rows in ((0, half),):
            at = pl.multiple_of(half * side_x + r, PAD)
            value = pair[n, pl.ds(r, rows), :] + take[n, pl.ds(r, rows), :]
            out[core * quarter + n, pl.ds(at, rows), :] = reorder(value, order[...])
        copy_x(n).start()
        copy_own(n).start()
        return carry

    def passing(n, carry):
        copy_x(n).wait_recv()
        copy_fwd(n).start()
        return carry

    def ending(n, carry):
        copy_own(n).wait_recv()
        copy_fwd(n).wait_recv()
        for copy in (copy_give, copy_x, copy_own, copy_fwd):
            copy(n).wait_send()
        return carry

    def in_turn(n, carry):
        combine(give_first + n + 3, carry)
        giving(n + 1, carry)
        keeping(n, carry)
        return combine(keep_first + n + 3, carry)

    giving(0, 0)
    lax.fori_loop(keep_first, keep_first + 3, combine, 0)
    lax.fori_loop(0, quarter - 1, in_turn, 0)
    keeping(quarter - 1, 0)
    for body in (passing, ending):
        lax.fori_loop(0, quarter, body, 0)
    total.close()


def second_solve(slabs, nx, lc_half, lc_near, u_mine, u_first, u_rest, mean, back):
    depth, _, cols = lc_half.shape
    half = nx // 2
    frame = half + 2 * PAD
    plane = (frame + 2 * PAD, cols)
    wide = depth + 2 * WIDE
    quarter = depth // 2
    full = pl.BlockSpec(memory_space=VMEM)
    anywhere = pl.BlockSpec(memory_space=pl.ANY)
    pair = [DMA((2,)), DMA((2,))]
    return pl.pallas_call(
        functools.partial(second_kernel, slabs, nx),
        name="second_solve",
        out_shape=jax.ShapeDtypeStruct((depth, nx, cols), F32),
        in_specs=[full, full, anywhere, anywhere, anywhere, full, full],
        out_specs=full,
        scratch_shapes=[
            VMEM((wide + 2, *plane), F32),
            VMEM((wide, frame, cols), F32),
            VMEM((wide, frame, cols), F32),
            VMEM((wide, *plane), F32),
            VMEM((wide + 1, frame, cols), F32),
            VMEM((2, wide - 2, *plane), F32),
            VMEM((2, wide - 4, *plane), F32),
            VMEM((2, wide - 6, *plane), F32),
            VMEM((2, depth + 2, frame, cols), F32),
            VMEM((2, depth + 2, frame, cols), F32),
        ]
        + [VMEM((quarter, half, cols), F32)] * 3
        + [VMEM((2, WIDE - 1, half + PAD, cols), F32), VMEM((cols, cols), jnp.bfloat16)]
        + [DMA((2,)), DMA(()), DMA(())]
        + pair * 2
        + [DMA((quarter,))] * 8
        + sum_scratch(slabs, (1, 128), 8),
        compiler_params=pltpu.CompilerParams(
            collective_id=2, has_side_effects=True, vmem_limit_bytes=42 << 20
        ),
    )(lc_half, lc_near, u_mine, u_first, u_rest, mean, back)


def shards(slabs, log_cond, perturb, potentials, rec_depth, rec_plan):
    depth, nx, cols = log_cond.shape
    dipoles = rec_depth.shape[1]
    order = lax.broadcasted_iota(jnp.int32, rec_depth.shape, 0) * dipoles
    order = order + lax.broadcasted_iota(jnp.int32, rec_depth.shape, 1)
    keys = (rec_depth * (2 * dipoles) + order).reshape(-1)
    keys, cells = lax.sort((keys, rec_plan.reshape(-1)), num_keys=1, is_stable=False)
    arguments = (pltpu.with_memory_space_constraint(a, pltpu.HBM) for a in (log_cond, perturb, potentials[0]))
    tangent, mean, lc_half, lc_near, u_mine, u_first, u_rest = first_solve(slabs, *arguments)
    part = gather(keys, cells, tangent.reshape(depth * nx, cols), depth)
    data = share(slabs, part)
    u_first, data = lax.optimization_barrier((u_first, data))
    u_first = lax.ppermute(u_first, "src", [(i, (i + 2) % 4) for i in range(4)])
    back = scatter(keys, cells, data, depth, nx, cols)
    return second_solve(slabs, nx, lc_half, lc_near, u_mine, u_first, u_rest, mean, back)


def solution(mesh):
    in_specs = (
        P("slab", None, None),
        P("slab", None, None),
        P("src", "slab", None, None),
        P(),
        P(),
    )
    return jax.shard_map(
        functools.partial(shards, mesh.shape["slab"]),
        mesh=mesh,
        in_specs=in_specs,
        out_specs=P("slab", None, None),
        check_vma=False,
    )
```
